32 devices in a mesh: wide: 8 (over z, x), narrow: 4 (over y, core).
Axes of the slice: x: 2, y: 2, z: 4, core: 2. Of those that a mesh axis runs over, the one named last changes fastest.
Arguments:
- tokens: bfloat16 [32, 448, 768], P('wide'), may hold values from -6 to 6
- lengths: int32 [32], P('wide'), may hold values from 1 to 448, 7168 in all
- memory: bfloat16 [32, 1536, 768], P(None, 'wide'), may hold values from -6 to 6
- gains: float32 [4, 768], replicated, may hold values from 0.5 to 1.5
- self_qkv: bfloat16 [3, 768, 768], P(None, None, 'narrow'), may hold values from -0.21875 to 0.21875
- self_out: bfloat16 [768, 768], P('narrow'), may hold values from -1.5 to 1.5
- cross_q: bfloat16 [768, 768], P(None, 'narrow'), may hold values from -0.21875 to 0.21875
- cross_kv: bfloat16 [2, 768, 768], P(None, None, 'narrow'), may hold values from -0.21875 to 0.21875
- cross_out: bfloat16 [768, 768], P('narrow'), may hold values from -4 to 4
- fc_in: bfloat16 [768, 3072], P(None, 'narrow'), may hold values from -0.21875 to 0.21875
- fc_out: bfloat16 [3072, 768], P('narrow'), may hold values from -0.109375 to 0.109375
- out_grad: bfloat16 [32, 448, 768], P('wide'), may hold values from -6 to 6
Outputs:
- block_out: bfloat16 [32, 448, 768], P('wide')
- tokens_grad: bfloat16 [32, 448, 768], P('wide')
- memory_grad: bfloat16 [32, 1536, 768], P(None, 'wide')
- gains_grad: float32 [4, 768], P(None, 'wide')
- self_qkv_grad: float32 [3, 768, 768], P(None, 'wide', 'narrow')
- self_out_grad: float32 [768, 768], P('narrow', 'wide')
- cross_q_grad: float32 [768, 768], P('wide', 'narrow')
- cross_kv_grad: float32 [2, 768, 768], P(None, 'wide', 'narrow')
- cross_out_grad: float32 [768, 768], P('narrow', 'wide')
- fc_in_grad: float32 [768, 3072], P('wide', 'narrow')
- fc_out_grad: float32 [3072, 768], P('narrow', 'wide')
The draws below stay inside these ranges and needn't reach their ends.
Inputs may be any that keep to these rules, and one draw needn't show every extreme that they name: `lengths`: some clip has exactly 448 tokens in every draw.
All inputs are finite; a program needn't handle non-finite values. No bound on the sum of `lengths` on one device may be relied on, other than what follows from the above.
Results may differ from the reference program's by a relative error of at most 0.019.
Values may be sent and summed in bfloat16 or wider, within the bound.
No kernel may reach another device: no remote copies, remote signals or barrier semaphores. Data moves between devices by JAX's collectives and lax.ppermute only.
A program may use at most 384 MiB of HBM per device.

```python
import math
import jax
import jax.numpy as jnp
import numpy as np
from jax import lax

D = 768
HEAD_DIM = 64
FF = 3072
SEQ = 448
FRAMES = 1536
AUDIO = 1500
CLIP_DEV = 4
CLIPS = 32


def with_spikes(entries, own_key, source, target, parts, factor):
    def block_of(position):
        return (jnp.arange(entries.shape[position]) // (entries.shape[position] // parts)).reshape((-1,) + (1,) * (entries.ndim - 1 - position))

    near = jax.random.permutation(own_key, parts)[block_of(target)]
    second = (block_of(target) + parts // 2) % parts
    return jnp.where((block_of(source) == near) | (block_of(source) == second), factor * entries, entries)


def block_levels(key, shape, pieces, smallest, high):
    gain = 1.0
    for position, shards_of in pieces:
        heights = jax.random.uniform(jax.random.fold_in(jax.random.fold_in(key, 6), position), (shards_of,), jnp.float32, smallest / len(pieces), high / len(pieces))
        gain = gain * jnp.repeat(jnp.exp(heights), shape[position] // shards_of).reshape((-1,) + (1,) * (len(shape) - 1 - position))
    return gain


def split_up(amount, total, reach, slope):
    weights = [(1 << 20) // math.isqrt(grade ** slope) + 1 for grade in range(2, amount + 1)]
    rest, holding = total - reach - (amount - 1), [1] * (amount - 1)
    while rest > 0:
        free = [i for i in range(amount - 1) if holding[i] < reach]
        whole, budget = sum([weights[i] for i in free]), rest
        for i in free:
            addition = min(reach - holding[i], max(1, budget * weights[i] // whole), rest)
            holding[i] = holding[i] + addition
            rest = rest - addition
    return np.array([reach] + holding)


def uneven_parts(stream_key, count, total, reach, slope):
    if count == 2:
        one = jax.random.randint(stream_key, (), max(1, total - reach), min(reach, total - 1) + 1)
        return jnp.stack([one, total - one])
    tallies = jnp.asarray(split_up(count, total, reach, slope), jnp.int32)
    pairs = (count - 1) // 2
    source_of, receiver = tallies[1:1 + 2 * pairs:2], tallies[2:2 + 2 * pairs:2]
    slack = jnp.minimum(source_of - 1, reach - receiver)
    passed = jax.random.randint(jax.random.fold_in(stream_key, 1), (pairs,), 0, 1 << 20) % (slack + 1)
    tallies = tallies.at[1:1 + 2 * pairs:2].set(source_of - passed).at[2:2 + 2 * pairs:2].set(receiver + passed)
    return tallies[jax.random.permutation(jax.random.fold_in(stream_key, 2), count)]


def normal_values(rng, dims, scale, reach, split=(), dtype=jnp.bfloat16):
    level = block_levels(rng, dims, split, -0.22, 0.18) if split else 1.0
    array = jax.random.normal(rng, dims, jnp.float32) * scale * level
    return jnp.minimum(jnp.maximum(array, -reach), reach).astype(dtype)


def heavy_noise(stream_key, dims, width, most, split, heavy, kind=jnp.bfloat16):
    drawn = width * jax.random.normal(stream_key, dims, jnp.float32)
    if split:
        drawn = drawn * block_levels(stream_key, dims, split, -0.22, 0.18)
    return jnp.clip(with_spikes(drawn, jax.random.fold_in(stream_key, 3), *heavy), -most, most).astype(kind)


def setup_inputs(seed: int = 0) -> dict:
    splits = jax.random.split(jax.random.key(seed), 13)
    return {
        "tokens": normal_values(splits[0], (CLIPS, SEQ, D), 1.0, 6.0, ((0, 8),)),
        "lengths": uneven_parts(splits[1], CLIPS, CLIPS * SEQ // 2, SEQ, 2).astype(jnp.int32),
        "memory": normal_values(splits[2], (CLIPS, FRAMES, D), 1.0, 6.0, ((1, 8),)),
        "gains": jnp.clip(1.0 + 0.1 * jax.random.normal(splits[3], (4, D), jnp.float32), 0.5, 1.5),
        "self_qkv": normal_values(splits[4], (3, D, D), D ** -0.5, 0.21875, ((2, 4),)),
        "self_out": normal_values(splits[5], (D, D), (D * 8 // SEQ + 1) ** -0.5, 1.5, ((0, 4),)),
        "cross_q": normal_values(splits[6], (D, D), D ** -0.5, 0.21875, ((1, 4),)),
        "cross_kv": normal_values(splits[7], (2, D, D), D ** -0.5, 0.21875, ((2, 4),)),
        "cross_out": normal_values(splits[8], (D, D), (D * 3 // AUDIO + 1) ** -0.5, 4.0, ((0, 4),)),
        "fc_in": normal_values(splits[9], (D, FF), D ** -0.5, 0.21875, ((1, 4),)),
        "fc_out": normal_values(splits[10], (FF, D), FF ** -0.5, 0.109375, ((0, 4),)),
        "out_grad": heavy_noise(splits[11], (CLIPS, SEQ, D), 1.0, 6.0, ((0, 8),), (0, 2, 8, 2.0)),
    }


EPSILON = 1e-05
NEG_FILL = -1e+30

@jax.custom_vjp
def low(v):
    return lax.optimization_barrier(v.astype(jnp.bfloat16)).astype(jnp.float32)

@jax.custom_vjp
def low_back(v):
    return v

def low_keep(v):
    return (low(v), None)

def low_pass(kept, grad):
    return (grad,)

def back_keep(v):
    return (v, None)

def back_low(kept, grad):
    return (low(grad),)
low.defvjp(low_keep, low_pass)
low_back.defvjp(back_keep, back_low)

def rounded_both(values):
    return low_back(low(values))

def norm_rows(values, gain_row):
    center = values - lax.optimization_barrier(jnp.mean(values, axis=-1, keepdims=True))
    spread = lax.optimization_barrier(jnp.mean(center * center, axis=-1, keepdims=True))
    return center * lax.rsqrt(spread + EPSILON) * gain_row

def split_heads(values):
    return values.reshape(values.shape[:-1] + (values.shape[-1] // HEAD_DIM, HEAD_DIM))

def attention(queries, key_rows, value_rows, allowed):
    in_shape = queries.shape
    scores = jnp.einsum('cshd,cthd->chst', split_heads(queries), split_heads(key_rows), precision=lax.Precision.HIGHEST) * HEAD_DIM ** (-0.5)
    scores = low_back(scores)
    masked = jnp.where(allowed, scores, NEG_FILL)
    attn_probs = low(jnp.exp(masked - jax.nn.logsumexp(masked, axis=-1, keepdims=True)))
    mixture = jnp.einsum('chst,cthd->cshd', attn_probs, split_heads(value_rows), precision=lax.Precision.HIGHEST)
    return rounded_both(mixture.reshape(in_shape))

def group_block(token_rows, memory_rows, clip_lengths, weight_set):
    gains, self_qkv, self_out, cross_q, cross_kv, cross_out, fc_in, fc_out = weight_set
    highest = lax.Precision.HIGHEST
    positions = jnp.arange(SEQ)
    live_rows = positions[None, :] < clip_lengths[:, None]
    self_allowed = (positions[None, :] <= positions[:, None])[None, None] & live_rows[:, None, None, :]
    cross_allowed = (jnp.arange(FRAMES) < AUDIO)[None, None, None, :]
    encoded = rounded_both(norm_rows(memory_rows, gains[0]))
    normed_one = low(norm_rows(token_rows, gains[1]))
    projected = rounded_both(jnp.einsum('csd,kde->kcse', normed_one, self_qkv, precision=highest))
    self_mixed = attention(projected[0], projected[1], projected[2], self_allowed)
    after_self = token_rows + low_back(jnp.einsum('cse,ed->csd', self_mixed, self_out, precision=highest))
    normed_two = low(norm_rows(after_self, gains[2]))
    cross_query = rounded_both(jnp.einsum('csd,de->cse', normed_two, cross_q, precision=highest))
    key_value = rounded_both(jnp.einsum('cfd,kde->kcfe', encoded, cross_kv, precision=highest))
    cross_mixed = attention(cross_query, key_value[0], key_value[1], cross_allowed)
    after_cross = after_self + low_back(jnp.einsum('cse,ed->csd', cross_mixed, cross_out, precision=highest))
    normed_three = low(norm_rows(after_cross, gains[3]))
    hidden_pre = low_back(jnp.einsum('csd,df->csf', normed_three, fc_in, precision=highest))
    activated = low(jax.nn.gelu(hidden_pre, approximate=False))
    return after_cross + low_back(jnp.einsum('csf,fd->csd', activated, fc_out, precision=highest))

def reference(tokens, lengths, memory, gains, self_qkv, self_out, cross_q, cross_kv, cross_out, fc_in, fc_out, out_grad):
    groups = tokens.shape[0] // CLIP_DEV
    weight_set = tuple((item.astype(jnp.float32) for item in (gains, self_qkv, self_out, cross_q, cross_kv, cross_out, fc_in, fc_out)))
    token_rows = tokens.astype(jnp.float32).reshape(groups, CLIP_DEV, SEQ, D)
    memory_rows = memory.astype(jnp.float32).reshape(groups, CLIP_DEV, FRAMES, D)
    clip_lengths = lengths.reshape(groups, CLIP_DEV)
    block_step = jax.checkpoint(group_block)

    def forward(token_part, memory_part, weights_now):

        def apply_block(item_set):
            return block_step(item_set[0], item_set[1], item_set[2], weights_now)
        return lax.map(apply_block, (token_part, memory_part, clip_lengths))
    block_out, pullback = jax.vjp(forward, token_rows, memory_rows, weight_set)
    live_rows = (jnp.arange(SEQ)[None, :] < lengths[:, None]).astype(jnp.float32)
    cotangent = (out_grad.astype(jnp.float32) * live_rows[:, :, None]).reshape(token_rows.shape)
    grad_tokens, grad_memory, grad_weights = pullback(cotangent)
    return (block_out.reshape(tokens.shape).astype(jnp.bfloat16), grad_tokens.reshape(tokens.shape).astype(jnp.bfloat16), grad_memory.reshape(memory.shape).astype(jnp.bfloat16), grad_weights[0], grad_weights[1], grad_weights[2], grad_weights[3], grad_weights[4], grad_weights[5], grad_weights[6], grad_weights[7])
```

```python
import jax
import jax.numpy as jnp
from jax import lax
from jax.sharding import PartitionSpec as P

HEAD_DIM = 64
AUDIO = 1500
EPSILON = 1e-05
NEG_FILL = -1e30
INV_ROOT = HEAD_DIM**-0.5
F32 = jnp.float32
BF16 = jnp.bfloat16


def dot(left, right, left_dim=1, right_dim=0):
    return lax.dot_general(
        left, right, (((left_dim,), (right_dim,)), ((), ())), preferred_element_type=F32
    )


def norm_stats(values):
    center = values - jnp.mean(values, axis=-1, keepdims=True)
    spread = jnp.mean(center * center, axis=-1, keepdims=True)
    inverse = lax.rsqrt(spread + EPSILON)
    return center * inverse, inverse


def norm_back(unit, inverse, gain_row, grad):
    scaled = grad * gain_row
    first = jnp.mean(scaled, axis=-1, keepdims=True)
    second = jnp.mean(scaled * unit, axis=-1, keepdims=True)
    back = (scaled - first - unit * second) * inverse
    axes = tuple(range(grad.ndim - 1))
    return back, jnp.sum(grad * unit, axis=axes)


def swap(values, axis, bit):
    size = lax.axis_size(axis)
    return lax.ppermute(values, axis, [(i, i ^ bit) for i in range(size)])


def gather_narrow(own):
    core = swap(own, "narrow", 1)
    other = swap(own, "narrow", 2)
    diagonal = swap(other, "narrow", 1)
    return [own, core, other, diagonal]


def scatter_narrow(zero, one, two, three):
    near = swap(jnp.stack((one, three)), "narrow", 1)
    far = swap((two.astype(F32) + near[1].astype(F32)).astype(BF16), "narrow", 2)
    return zero.astype(F32) + near[0].astype(F32) + far.astype(F32)


def scatter_wide(pack):
    size = lax.axis_size("wide")
    index = lax.axis_index("wide")
    bit = 1
    shape = pack.shape[1:]
    pack = pack.astype(F32)
    while bit < size:
        halves = pack.reshape((pack.shape[0] // 2, 2) + shape)
        mine = (index // bit) % 2
        keep = lax.dynamic_index_in_dim(halves, mine, 1, keepdims=False)
        give = lax.dynamic_index_in_dim(halves, 1 - mine, 1, keepdims=False)
        pack = keep + swap(give.astype(BF16), "wide", bit).astype(F32)
        bit *= 2
    return pack[0]


def split_heads(values):
    return values.reshape(values.shape[:-1] + (values.shape[-1] // HEAD_DIM, HEAD_DIM))


def attend(queries, key_rows, value_rows, allowed):
    scores = jnp.einsum(
        "cshd,cthd->chst",
        split_heads(queries),
        split_heads(key_rows),
        preferred_element_type=F32,
    ) * INV_ROOT
    masked = jnp.where(allowed, scores, NEG_FILL)
    log_total = jax.nn.logsumexp(masked, axis=-1, keepdims=True)
    probs = jnp.exp(masked - log_total).astype(BF16)
    mixture = jnp.einsum(
        "chst,cthd->cshd", probs, split_heads(value_rows), preferred_element_type=F32
    )
    return mixture.reshape(queries.shape).astype(BF16), log_total


def attend_back(queries, key_rows, value_rows, allowed, log_total, grad_mixture):
    query_heads = split_heads(queries)
    key_heads = split_heads(key_rows)
    value_heads = split_heads(value_rows)
    grad_heads = split_heads(grad_mixture)
    scores = jnp.einsum("cshd,cthd->chst", query_heads, key_heads, preferred_element_type=F32) * INV_ROOT
    masked = jnp.where(allowed, scores, NEG_FILL)
    probs = jnp.exp(masked - log_total)
    grad_probs = jnp.einsum("cshd,cthd->chst", grad_heads, value_heads, preferred_element_type=F32)
    inner = jnp.sum(probs * grad_probs, axis=-1, keepdims=True)
    grad_scores = (probs * (grad_probs - inner)).astype(BF16)
    grad_query = jnp.einsum("chst,cthd->cshd", grad_scores, key_heads, preferred_element_type=F32) * INV_ROOT
    grad_key = jnp.einsum("chst,cshd->cthd", grad_scores, query_heads, preferred_element_type=F32) * INV_ROOT
    grad_value = jnp.einsum("chst,cshd->cthd", probs.astype(BF16), grad_heads, preferred_element_type=F32)
    return (
        grad_query.reshape(queries.shape).astype(BF16),
        grad_key.reshape(key_rows.shape).astype(BF16),
        grad_value.reshape(value_rows.shape).astype(BF16),
    )


def on_device(
    tokens, lengths, memory, gains, self_qkv, self_out, cross_q, cross_kv, cross_out, fc_in, fc_out, out_grad
):
    clips, seq, width = tokens.shape
    wide = lax.axis_size("wide")
    narrow = lax.axis_size("narrow")
    me = lax.axis_index("narrow")
    share = memory.shape[1]
    frames = share * wide
    heads_width = self_qkv.shape[2]
    take = lambda array, r: lax.dynamic_index_in_dim(array, me ^ r, 0, keepdims=False)
    by_distance = lambda array: jnp.stack([take(array, r) for r in range(narrow)])

    memory_own = lax.dynamic_index_in_dim(
        memory.reshape(wide, narrow, share, width), me, 1, keepdims=False
    ).astype(F32)
    memory_unit, memory_inverse = norm_stats(memory_own)
    encoded_own = (memory_unit * gains[0]).astype(BF16)
    encoded = lax.all_to_all(encoded_own, "wide", 0, 0, tiled=True).reshape(frames, width)

    self_out_all = jnp.concatenate(gather_narrow(self_out), axis=0)
    cross_q_all = jnp.concatenate(gather_narrow(cross_q), axis=1)
    cross_kv_all = jnp.concatenate(gather_narrow(cross_kv), axis=2)
    cross_out_all = jnp.concatenate(gather_narrow(cross_out), axis=0)

    clip_lengths = by_distance(lengths)
    positions = jnp.arange(seq)
    live_rows = positions[None, :] < clip_lengths[:, None]
    self_allowed = (positions[None, :] <= positions[:, None])[None, None] & live_rows[:, None, None, :]
    tokens_by = by_distance(tokens).astype(F32)
    unit_one, inverse_one = norm_stats(tokens_by)
    normed_one = (unit_one * gains[1]).astype(BF16)
    rows_one = normed_one.reshape(clips * seq, width)
    projected = [
        dot(rows_one, self_qkv[i]).astype(BF16).reshape(clips, seq, heads_width) for i in range(3)
    ]
    mixed_heads, self_total = attend(projected[0], projected[1], projected[2], self_allowed)
    near = swap(jnp.stack((mixed_heads[1], mixed_heads[3])), "narrow", 1)
    own_half = jnp.concatenate((mixed_heads[0], near[0]), axis=1)
    far_half = swap(jnp.concatenate((mixed_heads[2], near[1]), axis=1), "narrow", 2)
    self_mixed = jnp.concatenate((own_half, far_half), axis=1)

    after_self = tokens_by[0] + dot(self_mixed, self_out_all)
    unit_two, inverse_two = norm_stats(after_self)
    normed_two = (unit_two * gains[2]).astype(BF16)
    cross_query = dot(normed_two, cross_q_all).astype(BF16)
    keys = dot(encoded, cross_kv_all[0]).astype(BF16)
    values = dot(encoded, cross_kv_all[1]).astype(BF16)
    cross_allowed = (jnp.arange(frames) < AUDIO)[None, None, None, :]
    cross_mixed, cross_total = attend(cross_query[None], keys[None], values[None], cross_allowed)
    cross_mixed = cross_mixed[0]
    after_cross = after_self + dot(cross_mixed, cross_out_all)
    unit_three, inverse_three = norm_stats(after_cross)
    normed_three = (unit_three * gains[3]).astype(BF16)

    rows_three = jnp.concatenate(gather_narrow(normed_three), axis=0)
    hidden_pre = dot(rows_three, fc_in)
    activated, gelu_back = jax.vjp(lambda v: jax.nn.gelu(v, approximate=False), hidden_pre)
    hidden = activated.astype(BF16)
    feed_part = dot(hidden, fc_out).astype(BF16).reshape(clips, seq, width)
    grad_by = by_distance(out_grad).astype(F32) * live_rows[:, :, None].astype(F32)
    grad_three = grad_by.astype(BF16).reshape(clips * seq, width)
    grad_fc_out = dot(grad_three, hidden, 0, 0)
    grad_pre = gelu_back(dot(grad_three, fc_out, 1, 1))[0].astype(BF16)
    grad_fc_in = dot(rows_three, grad_pre, 0, 0)
    part = dot(grad_pre, fc_in, 1, 1).astype(BF16).reshape(clips, seq, width)
    grad_normed = scatter_narrow(part[0], part[1], part[2], part[3])
    feed = scatter_narrow(feed_part[0], feed_part[1], feed_part[2], feed_part[3])
    block_own = (after_cross + feed).astype(BF16)
    block_out = by_distance(jnp.stack(gather_narrow(block_own)))

    back, gain_three = norm_back(unit_three, inverse_three, gains[3], grad_normed)
    grad_cross = grad_by[0] + back
    grad_two = grad_cross.astype(BF16)
    grad_cross_out = dot(cross_mixed, grad_two, 0, 0)
    grad_mixed = dot(grad_two, cross_out_all, 1, 1).astype(BF16)
    grad_query, grad_keys, grad_values = attend_back(
        cross_query[None], keys[None], values[None], cross_allowed, cross_total, grad_mixed[None]
    )
    grad_query, grad_keys, grad_values = grad_query[0], grad_keys[0], grad_values[0]

    grad_encoded = (
        dot(grad_keys, cross_kv_all[0], 1, 1) + dot(grad_values, cross_kv_all[1], 1, 1)
    ).astype(BF16)
    grad_encoded = lax.all_to_all(
        grad_encoded.reshape(wide, share, width), "wide", 0, 0, tiled=True
    ).astype(F32)
    memory_back, gain_zero = norm_back(memory_unit, memory_inverse, gains[0], grad_encoded)
    memory_back = jnp.stack(gather_narrow(memory_back.astype(BF16)))
    memory_grad = by_distance(memory_back).transpose(1, 0, 2, 3).reshape(memory.shape)

    grad_cross_q = dot(normed_two, grad_query, 0, 0)
    grad_cross_k = dot(encoded, grad_keys, 0, 0)
    grad_cross_v = dot(encoded, grad_values, 0, 0)
    back, gain_two = norm_back(unit_two, inverse_two, gains[2], dot(grad_query, cross_q_all, 1, 1))
    grad_self = grad_cross + back
    grad_one = grad_self.astype(BF16)
    grad_self_out = dot(self_mixed, grad_one, 0, 0)
    grad_mixed = dot(grad_one, self_out_all, 1, 1).astype(BF16)
    half = width // 2
    far_half = swap(grad_mixed[:, half:], "narrow", 2)
    near = swap(
        jnp.stack((grad_mixed[:, heads_width:half], far_half[:, heads_width:])), "narrow", 1
    )
    grad_heads = jnp.stack((grad_mixed[:, :heads_width], near[0], far_half[:, :heads_width], near[1]))
    grad_triple = attend_back(
        projected[0], projected[1], projected[2], self_allowed, self_total, grad_heads
    )
    grad_triple = [item.reshape(clips * seq, heads_width) for item in grad_triple]
    grad_qkv = [dot(rows_one, item, 0, 0) for item in grad_triple]
    part = sum(dot(grad_triple[i], self_qkv[i], 1, 1) for i in range(3))
    part = part.astype(BF16).reshape(clips, seq, width)
    grad_normed = scatter_narrow(part[0], part[1], part[2], part[3])
    back, gain_one = norm_back(unit_one[0], inverse_one[0], gains[1], grad_normed)
    tokens_own = (grad_self + back).astype(BF16)
    tokens_grad = by_distance(jnp.stack(gather_narrow(tokens_own)))

    blocks = []
    for r in range(narrow):
        columns = slice(r * heads_width, (r + 1) * heads_width)
        blocks.append(
            jnp.stack(
                (
                    grad_self_out[columns].T,
                    grad_cross_q[:, columns],
                    grad_cross_k[:, columns],
                    grad_cross_v[:, columns],
                    grad_cross_out[columns].T,
                )
            ).astype(BF16)
        )
    shared = scatter_narrow(*blocks)
    gain_terms = jnp.stack((gain_zero, gain_one, gain_two, gain_three))
    gain_terms = gain_terms + swap(gain_terms, "narrow", 1)
    gain_terms = gain_terms + swap(gain_terms, "narrow", 2)
    depth = width // wide

    def cut(matrix):
        return matrix.reshape(wide, -1)

    pieces = [cut(gain_terms.T)]
    pieces += [cut(shared[i]) for i in range(5)]
    pieces += [cut(item) for item in grad_qkv]
    pieces += [cut(grad_fc_in), cut(grad_fc_out)]
    sizes = [piece.shape[1] for piece in pieces]
    total = scatter_wide(jnp.concatenate([p.astype(BF16) for p in pieces], axis=1))
    outs = []
    start = 0
    for size in sizes:
        outs.append(total[start : start + size].reshape(depth, -1))
        start += size
    return (
        block_out,
        tokens_grad,
        memory_grad,
        outs[0].T,
        jnp.stack(outs[6:9]),
        outs[1].T,
        outs[2],
        jnp.stack(outs[3:5]),
        outs[5].T,
        outs[9],
        outs[10].T,
    )


def solution(mesh):
    placed = (
        P("wide", None, None),
        P("wide"),
        P(None, "wide", None),
        P(),
        P(None, None, "narrow"),
        P("narrow", None),
        P(None, "narrow"),
        P(None, None, "narrow"),
        P("narrow", None),
        P(None, "narrow"),
        P("narrow", None),
        P("wide", None, None),
    )
    return jax.shard_map(
        on_device,
        mesh=mesh,
        in_specs=placed,
        out_specs=(
            P("wide", None, None),
            P("wide", None, None),
            P(None, "wide", None),
            P(None, "wide"),
            P(None, "wide", "narrow"),
            P("narrow", "wide"),
            P("wide", "narrow"),
            P(None, "wide", "narrow"),
            P("narrow", "wide"),
            P("wide", "narrow"),
            P("narrow", "wide"),
        ),
        check_vma=False,
    )
```

```python
import functools

import jax
import jax.numpy as jnp
from jax import lax
from jax.experimental import pallas as pl
from jax.experimental.pallas import tpu as pltpu
from jax.sharding import PartitionSpec as P

HEAD_DIM = 64
AUDIO = 1500
EPSILON = 1e-05
NEG_FILL = -1e30
INV_ROOT = HEAD_DIM**-0.5
F32 = jnp.float32
BF16 = jnp.bfloat16
VMEM_LIMIT = 56 << 20
COST_SCALE = 1.0


def dot(left, right, left_dim=1, right_dim=0):
    return lax.dot_general(
        left, right, (((left_dim,), (right_dim,)), ((), ())), preferred_element_type=F32
    )


def call(body, grid, in_specs, out_specs, out_shape, name, estimate, prefetch=0, scratch=()):
    return pl.pallas_call(
        body,
        grid_spec=pltpu.PrefetchScalarGridSpec(
            num_scalar_prefetch=prefetch,
            grid=grid,
            in_specs=in_specs,
            out_specs=out_specs,
            scratch_shapes=list(scratch),
        ),
        out_shape=out_shape,
        compiler_params=pltpu.CompilerParams(vmem_limit_bytes=VMEM_LIMIT),
        cost_estimate=estimate,
        name=name,
    )


def shape(dims, dtype=BF16):
    return jax.ShapeDtypeStruct(dims, dtype)


def cost(flops, moved, exps=0):
    scale = COST_SCALE
    return pl.CostEstimate(
        flops=int(flops * scale), bytes_accessed=int(moved * scale), transcendentals=int(exps * scale)
    )


def whole(shape):
    return pl.BlockSpec(shape, lambda *_: (0,) * len(shape))


def norm_stats(values):
    center = values - jnp.mean(values, axis=-1, keepdims=True)
    spread = jnp.mean(center * center, axis=-1, keepdims=True)
    inverse = lax.rsqrt(spread + EPSILON)
    return center * inverse, inverse


def norm_back(unit, inverse, gain_row, grad):
    scaled = grad * gain_row
    first = jnp.mean(scaled, axis=-1, keepdims=True)
    second = jnp.mean(scaled * unit, axis=-1, keepdims=True)
    return (scaled - first - unit * second) * inverse


def swap(values, axis, bit):
    size = lax.axis_size(axis)
    return lax.ppermute(values, axis, [(i, i ^ bit) for i in range(size)])


def gather_narrow(own):
    other = swap(own, "narrow", 2)
    return [own, swap(own, "narrow", 1), other]


def finish(blocks, then):
    return blocks + [swap(then(blocks[2]), "narrow", 1)]


class Order:
    def __init__(self):
        self.last = None

    def __call__(self, item, *named):
        named = named if self.last is None else named + (self.last,)
        if named:
            item, _ = lax.optimization_barrier((item, named))
        return item


def encode_body(order, memory_ref, gain_ref, out_ref):
    unit, _ = norm_stats(memory_ref[:, 0].astype(F32))
    out_ref[...] = (unit * gain_ref[...]).astype(BF16)


def encode(order, memory, gain_row, start, size):
    wide, _, _, width = memory.shape
    group = min(4, wide)
    return call(
        encode_body,
        (wide // group,),
        [
            pl.BlockSpec((group, 1, size, width), lambda i, order: (i, order[0], start // size, 0)),
            whole((1, width)),
        ],
        pl.BlockSpec((group, size, width), lambda i, *_: (i, 0, 0)),
        shape((wide, size, width)),
        "encode",
        cost(0, 4 * wide * size * width),
        prefetch=1,
    )(order, memory, gain_row)


def memory_back_body(order, memory_ref, gain_ref, grad_ref, out_ref, gain_out):
    unit, inverse = norm_stats(memory_ref[:, 0].astype(F32))
    grad = grad_ref[...].astype(F32)
    out_ref[...] = norm_back(unit, inverse, gain_ref[...], grad).astype(BF16)

    @pl.when(pl.program_id(0) == 0)
    def _():
        gain_out[...] = jnp.zeros_like(gain_out)

    gain_out[...] += jnp.sum(jnp.sum(grad * unit, axis=0), axis=0, keepdims=True)


def memory_back(order, memory, gain_row, grad, start):
    wide, _, _, width = memory.shape
    size = grad.shape[1]
    group = min(4, wide)
    rows = pl.BlockSpec((group, size, width), lambda i, *_: (i, 0, 0))
    return call(
        memory_back_body,
        (wide // group,),
        [
            pl.BlockSpec((group, 1, size, width), lambda i, order: (i, order[0], start // size, 0)),
            whole((1, width)),
            rows,
        ],
        [rows, whole((1, width))],
        [shape((wide, size, width)), shape((1, width), F32)],
        "memory_back",
        cost(0, 6 * wide * size * width),
        prefetch=1,
    )(order, memory, gain_row, grad)


def self_fwd_body(order, lengths, token_ref, gain_ref, weight_ref, normed_ref, qkv_ref, first_ref, second_ref, lse_ref):
    seq = token_ref.shape[1]
    heads = weight_ref.shape[1] // HEAD_DIM
    step = pl.program_id(0)
    length = lengths[order[step]]
    unit, _ = norm_stats(token_ref[0].astype(F32))
    normed = (unit * gain_ref[...]).astype(BF16)
    normed_ref[0] = normed
    for i in range(3):
        qkv_ref[0, i] = dot(normed, weight_ref[i], 1, 1).astype(BF16)
    cut = 256 if seq > 256 else seq
    mixed = []
    for h in range(heads):
        columns = slice(h * HEAD_DIM, (h + 1) * HEAD_DIM)
        parts = []
        for start, stop in ((0, cut), (cut, seq)):
            if start == stop:
                continue
            queries = qkv_ref[0, 0, start:stop, columns] * jnp.asarray(INV_ROOT, BF16)
            scores = dot(qkv_ref[0, 1, :stop, columns], queries, 1, 1)
            key = lax.broadcasted_iota(jnp.int32, scores.shape, 0)
            query = lax.broadcasted_iota(jnp.int32, scores.shape, 1) + start
            scores = jnp.where((key <= query) & (key < length), scores, NEG_FILL)
            top = jnp.max(scores, axis=0, keepdims=True)
            probs = jnp.exp(scores - top)
            total = jnp.sum(probs, axis=0, keepdims=True)
            out = dot(qkv_ref[0, 2, :stop, columns], probs.astype(BF16), 0, 0) / total
            parts.append(out.T)
            lse_ref[0, h : h + 1, start:stop] = top + jnp.log(total)
        mixed.append(jnp.concatenate(parts, axis=0))
    mixed = jnp.concatenate(mixed, axis=1).astype(BF16)

    @pl.when(step == 0)
    def _():
        first_ref[...] = mixed

    @pl.when(step == 1)
    def _():
        second_ref[...] = mixed


def self_fwd(order, lengths, tokens, gain_row, weights):
    _, seq, width = tokens.shape
    local = weights.shape[1]
    heads = local // HEAD_DIM
    return call(
        self_fwd_body,
        (2,),
        [
            pl.BlockSpec((1, seq, width), lambda i, order, lengths: (order[i], 0, 0)),
            whole((1, width)),
            whole((3, local, width)),
        ],
        [
            pl.BlockSpec((1, seq, width), lambda i, *_: (i, 0, 0)),
            pl.BlockSpec((1, 3, seq, local), lambda i, *_: (i, 0, 0, 0)),
            whole((seq, local)),
            whole((seq, local)),
            pl.BlockSpec((1, heads, seq), lambda i, *_: (i, 0, 0)),
        ],
        [
            shape((2, seq, width)),
            shape((2, 3, seq, local)),
            shape((seq, local)),
            shape((seq, local)),
            shape((2, heads, seq), F32),
        ],
        "self_forward",
        cost(2 * (6 * seq * width * local + 8 * seq * seq * local), 2 * seq * width * 8, 2 * heads * seq * seq),
        prefetch=2,
    )(order, lengths, tokens, gain_row, weights)


def self_bwd_body(order, lengths, qkv_ref, mixed0_ref, mixed1_ref, lse_ref, grad0_ref, grad1_ref, weight_ref, dqkv_ref, first_ref, second_ref):
    seq = qkv_ref.shape[2]
    heads = weight_ref.shape[1] // HEAD_DIM
    step = pl.program_id(0)
    length = lengths[order[step]]
    grad = jnp.where(step == 0, grad0_ref[...], grad1_ref[...])
    mixed = jnp.where(step == 0, mixed0_ref[...], mixed1_ref[...])
    inner = (grad.astype(F32) * mixed.astype(F32)).T
    cut = 256 if seq > 256 else seq
    for h in range(heads):
        columns = slice(h * HEAD_DIM, (h + 1) * HEAD_DIM)
        keys = qkv_ref[0, 1, :, columns]
        values = qkv_ref[0, 2, :, columns]
        dq_parts = []
        dk = jnp.zeros((seq, HEAD_DIM), F32)
        dv = jnp.zeros((seq, HEAD_DIM), F32)
        for start, stop in ((0, cut), (cut, seq)):
            if start == stop:
                continue
            queries = qkv_ref[0, 0, start:stop, columns] * jnp.asarray(INV_ROOT, BF16)
            grads = grad[start:stop, columns]
            scores = dot(keys[:stop], queries, 1, 1)
            key = lax.broadcasted_iota(jnp.int32, scores.shape, 0)
            query = lax.broadcasted_iota(jnp.int32, scores.shape, 1) + start
            allowed = (key <= query) & (key < length)
            probs = jnp.exp(jnp.where(allowed, scores, NEG_FILL) - lse_ref[0, h : h + 1, start:stop])
            dp = dot(values[:stop], grads, 1, 1)
            centre = jnp.sum(inner[columns, start:stop], axis=0, keepdims=True)
            ds = (probs * (dp - centre)).astype(BF16)
            dk_now = dot(ds, queries)
            dv_now = dot(probs.astype(BF16), grads)
            if stop < seq:
                pad = jnp.zeros((seq - stop, HEAD_DIM), F32)
                dk_now = jnp.concatenate((dk_now, pad), axis=0)
                dv_now = jnp.concatenate((dv_now, pad), axis=0)
            dk, dv = dk + dk_now, dv + dv_now
            dq_parts.append((dot(keys[:stop], ds, 0, 0) * INV_ROOT).T)
        dqkv_ref[0, 0, :, columns] = jnp.concatenate(dq_parts, axis=0).astype(BF16)
        dqkv_ref[0, 1, :, columns] = dk.astype(BF16)
        dqkv_ref[0, 2, :, columns] = dv.astype(BF16)
    total = dot(dqkv_ref[0, 0], weight_ref[0])
    total = total + dot(dqkv_ref[0, 1], weight_ref[1])
    total = (total + dot(dqkv_ref[0, 2], weight_ref[2])).astype(BF16)

    @pl.when(step == 0)
    def _():
        first_ref[...] = total

    @pl.when(step == 1)
    def _():
        second_ref[...] = total


def self_bwd(order, lengths, qkv, mixed0, mixed1, lse, grad0, grad1, weights):
    _, _, seq, local = qkv.shape
    width = weights.shape[2]
    heads = local // HEAD_DIM
    return call(
        self_bwd_body,
        (2,),
        [
            pl.BlockSpec((1, 3, seq, local), lambda i, *_: (i, 0, 0, 0)),
            whole((seq, local)),
            whole((seq, local)),
            pl.BlockSpec((1, heads, seq), lambda i, *_: (i, 0, 0)),
            whole((seq, local)),
            whole((seq, local)),
            whole((3, local, width)),
        ],
        [
            pl.BlockSpec((1, 3, seq, local), lambda i, *_: (i, 0, 0, 0)),
            whole((seq, width)),
            whole((seq, width)),
        ],
        [shape((2, 3, seq, local)), shape((seq, width)), shape((seq, width))],
        "self_backward",
        cost(2 * (6 * seq * width * local + 20 * seq * seq * local), 2 * seq * width * 8, 2 * heads * seq * seq),
        prefetch=2,
    )(order, lengths, qkv, mixed0, mixed1, lse, grad0, grad1, weights)


def to_query_body(order, token_ref, m0, m1, m2, m3, p0, p1, p2, p3, gain_ref, after_ref, normed_ref, query_ref):
    local = m0.shape[1]
    rows = token_ref[0].astype(F32)
    for mixed, pack in ((m0, p0), (m1, p1), (m2, p2), (m3, p3)):
        rows = rows + dot(mixed[...], pack[:local])
    after_ref[...] = rows
    unit, _ = norm_stats(rows)
    normed = (unit * gain_ref[...]).astype(BF16)
    normed_ref[...] = normed
    for r, pack in enumerate((p0, p1, p2, p3)):
        query = dot(normed, pack[local:], 1, 1).astype(BF16)
        query_ref[r // 2, :, (r % 2) * local : (r % 2 + 1) * local] = query


def to_query(order, tokens, mixes, packs, gain_row):
    _, seq, width = tokens.shape
    local = mixes[0].shape[1]
    tile = seq // 2
    return call(
        to_query_body,
        (2,),
        [pl.BlockSpec((1, tile, width), lambda i, order: (order[0], i, 0))]
        + [pl.BlockSpec((tile, local), lambda i, *_: (i, 0))] * 4
        + [whole((2 * local, width))] * 4
        + [whole((1, width))],
        [
            pl.BlockSpec((tile, width), lambda i, *_: (i, 0)),
            pl.BlockSpec((tile, width), lambda i, *_: (i, 0)),
            pl.BlockSpec((2, tile, 2 * local), lambda i, *_: (0, i, 0)),
        ],
        [shape((seq, width), F32), shape((seq, width)), shape((2, seq, 2 * local))],
        "self_out_to_query",
        cost(4 * seq * width * width, seq * width * 12 + 4 * width * width),
        prefetch=1,
    )(order, tokens, *mixes, *packs, gain_row)


def head_places(local):
    for r in range(2):
        for h in range(local // HEAD_DIM):
            at = r * local + h * HEAD_DIM
            key = 2 * r * local + h * HEAD_DIM
            yield (
                at // HEAD_DIM,
                slice(at, at + HEAD_DIM),
                slice(key, key + HEAD_DIM),
                slice(key + local, key + local + HEAD_DIM),
            )


def cross_first_body(query_ref, encoded_ref, w0, w1, w2, w3, kv_ref, acc_ref, top_ref, total_ref, *, valid):
    make_keys_values(encoded_ref, (w0, w1, w2, w3), kv_ref)
    frames = kv_ref.shape[0]
    for head, columns, key, value in head_places(query_ref.shape[2] // 2):
        queries = query_ref[0, :, columns] * jnp.asarray(INV_ROOT, BF16)
        scores = dot(kv_ref[:, key], queries, 1, 1)
        if valid < frames:
            frame = lax.broadcasted_iota(jnp.int32, scores.shape, 0)
            scores = jnp.where(frame < valid, scores, NEG_FILL)
        top = jnp.max(scores, axis=0, keepdims=True)
        probs = jnp.exp(scores - top)
        acc_ref[0, columns, :] = dot(kv_ref[:, value], probs.astype(BF16), 0, 0)
        top_ref[0, head : head + 1, :] = top
        total_ref[0, head : head + 1, :] = jnp.sum(probs, axis=0, keepdims=True)


def make_keys_values(encoded_ref, weights, kv_ref):
    pair = weights[0].shape[0]
    for step in range(2):

        @pl.when(pl.program_id(0) == step)
        def _():
            for r in range(2):
                kv = dot(encoded_ref[...], weights[2 * step + r][...], 1, 1)
                kv_ref[:, r * pair : (r + 1) * pair] = kv.astype(BF16)


def cross_second_body(
    query_ref, encoded_ref, w0, w1, w2, w3, acc_in, top_in, total_in, after_ref, o0, o1, o2, o3, gain_ref,
    kv_ref, mixed_ref, lse_ref, next_ref, normed_ref, *, valid,
):
    make_keys_values(encoded_ref, (w0, w1, w2, w3), kv_ref)
    frames = kv_ref.shape[0]
    local = o0.shape[0]
    for head, columns, key, value in head_places(local):
        queries = query_ref[0, :, columns] * jnp.asarray(INV_ROOT, BF16)
        scores = dot(kv_ref[:, key], queries, 1, 1)
        if valid < frames:
            frame = lax.broadcasted_iota(jnp.int32, scores.shape, 0)
            scores = jnp.where(frame < valid, scores, NEG_FILL)
        before = top_in[0, head : head + 1, :]
        top = jnp.maximum(jnp.max(scores, axis=0, keepdims=True), before)
        probs = jnp.exp(scores - top)
        fade = jnp.exp(before - top)
        total = jnp.sum(probs, axis=0, keepdims=True) + total_in[0, head : head + 1, :] * fade
        out = dot(kv_ref[:, value], probs.astype(BF16), 0, 0) + acc_in[0, columns, :] * fade
        mixed_ref[0, :, columns] = (out / total).T.astype(BF16)
        lse_ref[0, head : head + 1, :] = top + jnp.log(total)
    outs = (o0, o1, o2, o3)
    for step in range(2):

        @pl.when(pl.program_id(0) == step)
        def _():
            rows = after_ref[...] if step == 0 else next_ref[...]
            for r in range(2):
                rows = rows + dot(mixed_ref[0, :, r * local : (r + 1) * local], outs[2 * step + r][...])
            next_ref[...] = rows
            if step == 1:
                unit, _ = norm_stats(rows)
                normed_ref[...] = (unit * gain_ref[...]).astype(BF16)


def pack_specs(packs, rows, index):
    width = packs[0].shape[1]
    return [pl.BlockSpec((rows, width), lambda *_: (index, 0))] * 4


def cross_first(query, encoded, packs, valid):
    _, seq, pair = query.shape
    frames, width = encoded.shape
    heads = pair // HEAD_DIM
    stats = pl.BlockSpec((1, heads, seq), lambda i: (i, 0, 0))
    return call(
        functools.partial(cross_first_body, valid=valid),
        (2,),
        [pl.BlockSpec((1, seq, pair), lambda i: (i, 0, 0)), whole((frames, width))] + pack_specs(packs, pair, 0),
        [
            pl.BlockSpec((frames, 2 * pair), lambda i: (0, i)),
            pl.BlockSpec((1, pair, seq), lambda i: (i, 0, 0)),
            stats,
            stats,
        ],
        [
            shape((frames, 4 * pair)),
            shape((2, pair, seq), F32),
            shape((2, heads, seq), F32),
            shape((2, heads, seq), F32),
        ],
        "cross_first",
        cost(4 * frames * width * width + 40 * seq * frames * pair, 8 * frames * width, 2 * heads * seq * frames),
    )(query, encoded, *packs)


def cross_second(query, encoded, packs, packs_out, valid, before, after, gain_row):
    _, seq, pair = query.shape
    frames, width = encoded.shape
    heads = pair // HEAD_DIM
    rows = pl.BlockSpec((1, seq, pair), lambda i: (i, 0, 0))
    stats = pl.BlockSpec((1, heads, seq), lambda i: (i, 0, 0))
    acc = pl.BlockSpec((1, pair, seq), lambda i: (i, 0, 0))
    return call(
        functools.partial(cross_second_body, valid=valid),
        (2,),
        [rows, whole((frames, width))]
        + pack_specs(packs, pair, 0)
        + [acc, stats, stats, whole((seq, width))]
        + pack_specs(packs_out, pair // 2, 0)
        + [whole((1, width))],
        [pl.BlockSpec((frames, 2 * pair), lambda i: (0, i)), rows, stats, whole((seq, width)), whole((seq, width))],
        [
            shape((frames, 4 * pair)),
            shape((2, seq, pair)),
            shape((2, heads, seq), F32),
            shape((seq, width), F32),
            shape((seq, width)),
        ],
        "cross_second",
        cost(4 * frames * width * width + 40 * seq * frames * pair, 10 * frames * width, 2 * heads * seq * frames),
    )(query, encoded, *packs, *before, after, *packs_out, gain_row)


def feed_body(order, lengths, *refs, count):
    row_refs, (grad_ref, in_ref, out_ref, hidden_ref, pre_ref, live_ref) = refs[:count], refs[count : count + 6]
    outs = refs[count + 6 :]
    step = pl.program_id(0)
    tile = grad_ref.shape[1]
    rows = row_refs[0][...]
    if count == 2:
        rows = jnp.where(step == 0, rows, row_refs[1][...])
    place = lax.broadcasted_iota(jnp.int32, grad_ref.shape[1:], 0) + pl.program_id(1) * tile
    grads = jnp.where(place < lengths[order[step]], grad_ref[0], jnp.zeros((), BF16))
    live_ref[0] = grads
    pre = dot(rows, in_ref[...])
    half = 0.5 * (1.0 + lax.erf(pre * (0.5**0.5)))
    hidden = (pre * half).astype(BF16)
    slope = half + pre * jnp.exp(-0.5 * pre * pre) * 0.3989422804014327
    hidden_ref[0] = hidden
    grad_pre = (dot(grads, out_ref[...], 1, 1) * slope).astype(BF16)
    pre_ref[0] = grad_pre
    part = dot(grad_pre, in_ref[...], 1, 1).astype(BF16)
    feed = dot(hidden, out_ref[...]).astype(BF16)
    for i in range(count):

        @pl.when(step == i)
        def _():
            outs[2 * i][...] = part
            outs[2 * i + 1][...] = feed


def feed_forward(order, lengths, rows, out_grad, fc_in, fc_out):
    count = len(rows)
    seq, width = rows[0].shape
    units = fc_in.shape[1]
    tiles = 2
    tile = seq // tiles
    block = lambda last: pl.BlockSpec((1, tile, last), lambda i, j, *_: (i, j, 0))
    single = [
        pl.BlockSpec((tile, width), lambda i, j, *_: (jnp.where(i == 0, j, tiles - 1), 0)),
        pl.BlockSpec((tile, width), lambda i, j, *_: (jnp.where(i == 0, 0, j), 0)),
    ]
    if count == 1:
        single = [pl.BlockSpec((tile, width), lambda i, j, *_: (j, 0))]
    return call(
        functools.partial(feed_body, count=count),
        (count, tiles),
        single
        + [
            pl.BlockSpec((1, tile, width), lambda i, j, order, lengths: (order[i], j, 0)),
            whole((width, units)),
            whole((units, width)),
        ],
        [block(units), block(units), block(width)] + [spec for spec in single for _ in range(2)],
        [shape((count, seq, units)), shape((count, seq, units)), shape((count, seq, width))]
        + [shape((seq, width))] * (2 * count),
        "feed_forward",
        cost(8 * count * seq * width * units, count * seq * width * 14, 2 * count * seq * units),
        prefetch=2,
    )(order, lengths, *rows, out_grad, fc_in, fc_out)


def add_gain(gain_out, term):
    @pl.when(pl.program_id(0) == 0)
    def _():
        gain_out[...] = jnp.zeros_like(gain_out)

    gain_out[...] += term


def cross_back(queries_ref, kv_ref, grads_ref, mixed_ref, lse_ref, dkv_ref, local, valid, store):
    frames = kv_ref.shape[0]
    inner = (grads_ref.astype(F32) * mixed_ref[0].astype(F32)).T
    for head, columns, key, value in head_places(local):
        queries = queries_ref[0, :, columns] * jnp.asarray(INV_ROOT, BF16)
        grads = grads_ref[:, columns]
        centre = jnp.sum(inner[columns, :], axis=0, keepdims=True)
        keys = kv_ref[:, key]
        probs = jnp.exp(dot(keys, queries, 1, 1) - lse_ref[0, head : head + 1, :])
        if valid < frames:
            frame = lax.broadcasted_iota(jnp.int32, probs.shape, 0)
            probs = jnp.where(frame < valid, probs, 0.0)
        dp = dot(kv_ref[:, value], grads, 1, 1)
        ds = (probs * (dp - centre)).astype(BF16)
        dkv_ref[:, value] = dot(probs.astype(BF16), grads).astype(BF16)
        dkv_ref[:, key] = dot(ds, queries).astype(BF16)
        store(columns, dot(keys, ds, 0, 0))


def encoded_back(dkv_ref, weights, out_ref, acc):
    pair = weights[0].shape[0]
    for step in range(2):

        @pl.when(pl.program_id(0) == step)
        def _():
            total = dot(dkv_ref[:, :pair], weights[2 * step][...]) + dot(dkv_ref[:, pair:], weights[2 * step + 1][...])
            if step == 0:
                acc[...] = total
            else:
                out_ref[...] = (acc[...] + total).astype(BF16)


def cross_first_back_body(
    order, lengths, grad_ref, own_ref, near_ref, far_ref, after_ref, gain_ref, o0, o1, o2, o3,
    query_ref, kv_ref, mixed_ref, lse_ref, w0, w1, w2, w3,
    cross_ref, two_ref, grads_ref, gain_out, dq_ref, dkv_ref, encoded_ref, acc, *, valid,
):
    local = o0.shape[0]
    step = pl.program_id(0)

    @pl.when(step == 0)
    def _():
        place = lax.broadcasted_iota(jnp.int32, own_ref.shape, 0)
        grads = jnp.where(place < lengths[order[0]], grad_ref[0].astype(F32), 0.0)
        normed_grad = own_ref[...].astype(F32) + near_ref[...].astype(F32) + far_ref[...].astype(F32)
        unit, inverse = norm_stats(after_ref[...])
        total = grads + norm_back(unit, inverse, gain_ref[...], normed_grad)
        cross_ref[...] = total
        low = total.astype(BF16)
        two_ref[...] = low
        for r, weight in enumerate((o0, o1, o2, o3)):
            mixed = dot(low, weight[...], 1, 1).astype(BF16)
            grads_ref[r // 2, :, (r % 2) * local : (r % 2 + 1) * local] = mixed
        gain_out[...] = jnp.sum(normed_grad * unit, axis=0, keepdims=True)

    def store(columns, dq):
        dq_ref[0, columns, :] = dq

    cross_back(query_ref, kv_ref, grads_ref[step], mixed_ref, lse_ref, dkv_ref, local, valid, store)
    encoded_back(dkv_ref, (w0, w1, w2, w3), encoded_ref, acc)


def cross_first_back(order, lengths, out_grad, parts, after, gain_row, packs, packs_out, query, kv, mixed, lse, valid):
    seq, width = after.shape
    frames = kv.shape[0]
    pair = query.shape[2]
    heads = pair // HEAD_DIM
    rows = whole((seq, width))
    head_rows = pl.BlockSpec((1, seq, pair), lambda i, *_: (i, 0, 0))
    both = pl.BlockSpec((frames, 2 * pair), lambda i, *_: (0, i))
    return call(
        functools.partial(cross_first_back_body, valid=valid),
        (2,),
        [pl.BlockSpec((1, seq, width), lambda i, order, lengths: (order[0], 0, 0)), rows, rows, rows, rows]
        + [whole((1, width))]
        + pack_specs(packs_out, pair // 2, 0)
        + [head_rows, both, head_rows, pl.BlockSpec((1, heads, seq), lambda i, *_: (i, 0, 0))]
        + pack_specs(packs, pair, 0),
        [
            rows,
            rows,
            whole((2, seq, pair)),
            whole((1, width)),
            pl.BlockSpec((1, pair, seq), lambda i, *_: (i, 0, 0)),
            both,
            whole((frames, width)),
        ],
        [
            shape((seq, width), F32),
            shape((seq, width)),
            shape((2, seq, pair)),
            shape((1, width), F32),
            shape((2, pair, seq), F32),
            shape((frames, 2 * width)),
            shape((frames, width)),
        ],
        "cross_first_back",
        cost(4 * frames * width * width + 120 * seq * frames * pair, 20 * frames * width, 2 * heads * seq * frames),
        prefetch=2,
        scratch=[pltpu.VMEM((frames, width), F32)],
    )(order, lengths, out_grad, *parts, after, gain_row, *packs_out, query, kv, mixed, lse, *packs)


def cross_second_back_body(
    query_ref, kv_ref, grads_ref, mixed_ref, lse_ref, dq_in, w0, w1, w2, w3,
    p0, p1, p2, p3, after_ref, gain_ref, cross_ref,
    dq_ref, dkv_ref, encoded_ref, self_ref, one_ref, h0, h1, h2, h3, gain_out, acc, *, valid,
):
    local = h0.shape[1]
    step = pl.program_id(0)

    def store(columns, dq):
        dq_ref[step, :, columns] = ((dq + dq_in[0, columns, :]) * INV_ROOT).T.astype(BF16)

    cross_back(query_ref, kv_ref, grads_ref[0], mixed_ref, lse_ref, dkv_ref, local, valid, store)
    encoded_back(dkv_ref, (w0, w1, w2, w3), encoded_ref, acc)

    @pl.when(step == 1)
    def _():
        packs = (p0, p1, p2, p3)
        normed_grad = 0.0
        for r, pack in enumerate(packs):
            normed_grad = normed_grad + dot(dq_ref[r // 2, :, (r % 2) * local : (r % 2 + 1) * local], pack[local:])
        unit, inverse = norm_stats(after_ref[...])
        total = cross_ref[...] + norm_back(unit, inverse, gain_ref[...], normed_grad)
        self_ref[...] = total
        low = total.astype(BF16)
        one_ref[...] = low
        for out, pack in zip((h0, h1, h2, h3), packs):
            out[...] = dot(low, pack[:local], 1, 1).astype(BF16)
        gain_out[...] = jnp.sum(normed_grad * unit, axis=0, keepdims=True)


def cross_second_back(query, kv, grads, mixed, lse, dq, packs_two, packs_one, after, gain_row, cross, valid):
    seq, width = after.shape
    frames = kv.shape[0]
    pair = query.shape[2]
    local = pair // 2
    heads = pair // HEAD_DIM
    rows = whole((seq, width))
    head_rows = pl.BlockSpec((1, seq, pair), lambda i: (i, 0, 0))
    both = pl.BlockSpec((frames, 2 * pair), lambda i: (0, i))
    return call(
        functools.partial(cross_second_back_body, valid=valid),
        (2,),
        [head_rows, both, head_rows, head_rows, pl.BlockSpec((1, heads, seq), lambda i: (i, 0, 0))]
        + [pl.BlockSpec((1, pair, seq), lambda i: (i, 0, 0))]
        + pack_specs(packs_two, pair, 0)
        + pack_specs(packs_one, pair, 0)
        + [rows, whole((1, width)), rows],
        [whole((2, seq, pair)), both, whole((frames, width)), rows, rows]
        + [whole((seq, local))] * 4
        + [whole((1, width))],
        [
            shape((2, seq, pair)),
            shape((frames, 2 * width)),
            shape((frames, width)),
            shape((seq, width), F32),
            shape((seq, width)),
        ]
        + [shape((seq, local))] * 4
        + [shape((1, width), F32)],
        "cross_second_back",
        cost(4 * frames * width * width + 120 * seq * frames * pair, 20 * frames * width, 2 * heads * seq * frames),
        scratch=[pltpu.VMEM((frames, width), F32)],
    )(query, kv, grads, mixed, lse, dq, *packs_two, *packs_one, after, gain_row, cross)


def add_gain(gain_out, term):
    @pl.when(pl.program_id(0) == 0)
    def _():
        gain_out[...] = jnp.zeros_like(gain_out)

    gain_out[...] += term

def to_tokens_grad_body(order, token_ref, own_ref, near_ref, far_ref, self_ref, gain_ref, out_ref, gain_out):
    normed_grad = own_ref[...].astype(F32) + near_ref[...].astype(F32) + far_ref[...].astype(F32)
    unit, inverse = norm_stats(token_ref[0].astype(F32))
    out_ref[...] = (self_ref[...] + norm_back(unit, inverse, gain_ref[...], normed_grad)).astype(BF16)
    add_gain(gain_out, jnp.sum(normed_grad * unit, axis=0, keepdims=True))


def to_tokens_grad(order, tokens, own, near, far, grad_self, gain_row):
    _, seq, width = tokens.shape
    tile = seq // 2
    rows = pl.BlockSpec((tile, width), lambda i, *_: (i, 0))
    return call(
        to_tokens_grad_body,
        (2,),
        [pl.BlockSpec((1, tile, width), lambda i, order: (order[0], i, 0)), rows, rows, rows, rows, whole((1, width))],
        [rows, whole((1, width))],
        [shape((seq, width)), shape((1, width), F32)],
        "norm_one_back",
        cost(0, seq * width * 14),
        prefetch=1,
    )(order, tokens, own, near, far, grad_self, gain_row)


def split_store(total, mine, keep_ref, give_ref, scratch, lead=()):
    scratch[...] = total
    parts, depth = keep_ref.shape[-3], keep_ref.shape[-2]
    for j in range(parts):
        at = pl.multiple_of((2 * j + mine) * depth, 8)
        keep_ref[lead + (j,)] = scratch[pl.ds(at, depth), :].astype(BF16)
        at = pl.multiple_of((2 * j + 1 - mine) * depth, 8)
        give_ref[lead + (j,)] = scratch[pl.ds(at, depth), :].astype(BF16)


def feed_weights_body(bits, *refs):
    rows, pres, lives, hiddens = refs[:4], refs[4:7], refs[7:10], refs[10:13]
    keep_ref, give_ref, scratch = refs[13:]
    three = lambda items: (items[0][0], items[0][1], items[1][0], items[2][0])
    total = 0.0
    for left, right in zip(rows, three(pres)):
        total = total + dot(left[...], right, 0, 0)
    split_store(total, bits[0], keep_ref, give_ref, scratch, (0,))
    total = 0.0
    for left, right in zip(three(lives), three(hiddens)):
        total = total + dot(left, right, 0, 0)
    split_store(total, bits[0], keep_ref, give_ref, scratch, (1,))


def feed_weights(bits, rows, pres, lives, hiddens, wide):
    seq, width = rows[0].shape
    units = pres[0].shape[2]
    tile = width // 2
    depth = width // wide
    column = lambda count: pl.BlockSpec((count, seq, tile), lambda i, *_: (0, 0, i))
    full = lambda count: whole((count, seq, units))
    out = pl.BlockSpec((2, wide // 4, depth, units), lambda i, *_: (0, i, 0, 0))
    return call(
        feed_weights_body,
        (2,),
        [pl.BlockSpec((seq, tile), lambda i, *_: (0, i))] * 4
        + [full(2), full(1), full(1), column(2), column(1), column(1), full(2), full(1), full(1)],
        [out, out],
        [shape((2, wide // 2, depth, units))] * 2,
        "feed_weight_grads",
        cost(16 * seq * width * units, 24 * seq * width),
        prefetch=1,
        scratch=[pltpu.VMEM((tile, units), F32)],
    )(bits, *rows, *pres, *lives, *hiddens)


def head_weights_body(*refs):
    enc0, enc1, dkv0, dkv1, two, dq_ref, one, grad_two, cross_mixed = refs[:9]
    mixes = refs[9:13]
    keep_ref, give_ref, self_keep, self_give = refs[13:]
    local = mixes[0].shape[1]
    for r in range(4):
        out = (keep_ref, give_ref)[r % 2]
        columns = slice((r % 2) * local, (r % 2 + 1) * local)
        pair = slice(2 * r * local, 2 * (r + 1) * local)
        kv = dot(enc0[...], dkv0[:, pair], 0, 0) + dot(enc1[...], dkv1[:, pair], 0, 0)
        out[r // 2, :, : 2 * local] = kv.astype(BF16)
        query = dot(two[...], dq_ref[r // 2, :, columns], 0, 0)
        cross = dot(grad_two[...], cross_mixed[r // 2, :, columns], 0, 0)
        out[r // 2, :, 2 * local :] = jnp.concatenate((query, cross), axis=1).astype(BF16)
        (self_keep, self_give)[r % 2][r // 2] = dot(mixes[r][...], one[...], 0, 0).astype(BF16)


def head_weights(encs, dkvs, normed_two, dq, grad_one, grad_two, cross_mixed, mixes):
    seq, width = normed_two.shape
    local = mixes[0].shape[1]
    tile = width // 2
    rows = pl.BlockSpec((seq, tile), lambda i: (0, i))
    out = pl.BlockSpec((2, tile, width), lambda i: (0, i, 0))
    turned = pl.BlockSpec((2, local, tile), lambda i: (0, 0, i))
    frames = encs[0].shape[0] + encs[1].shape[0]
    return call(
        head_weights_body,
        (2,),
        [pl.BlockSpec((item.shape[0], tile), lambda i: (0, i)) for item in encs]
        + [whole(item.shape) for item in dkvs]
        + [rows, whole(dq.shape), rows, rows, whole(cross_mixed.shape)]
        + [whole(item.shape) for item in mixes],
        [out, out, turned, turned],
        [shape((2, width, width))] * 2 + [shape((2, local, width))] * 2,
        "head_weight_grads",
        cost(4 * frames * width * width + 6 * seq * width * width, 6 * frames * width),
    )(*encs, *dkvs, normed_two, dq, grad_one, grad_two, cross_mixed, *mixes)


def self_weights_body(bits, near, far, dnear, dfar, own, core, other, keep_ref, give_ref, scratch):
    totals = []
    for i in range(3):
        total = 0.0
        for c in range(2):
            total = total + dot(near[c], dnear[c, i], 0, 0) + dot(far[c], dfar[c, i], 0, 0)
        totals.append(total)
    totals.append((own[0].astype(F32) + core[0].astype(F32) + other[...].astype(F32)).T)
    split_store(jnp.concatenate(totals, axis=1), bits[0], keep_ref, give_ref, scratch)


def self_weights(bits, near, far, dnear, dfar, own, core, other, wide):
    _, seq, width = near.shape
    local = dnear.shape[3]
    tile = width // 2
    depth = width // wide
    rows = pl.BlockSpec((2, seq, tile), lambda i, *_: (0, 0, i))
    turned = pl.BlockSpec((1, local, tile), lambda i, *_: (0, 0, i))
    out = pl.BlockSpec((wide // 4, depth, 4 * local), lambda i, *_: (i, 0, 0))
    return call(
        self_weights_body,
        (2,),
        [rows, rows, whole(dnear.shape), whole(dfar.shape), turned, turned]
        + [pl.BlockSpec((local, tile), lambda i, *_: (0, i))],
        [out, out],
        [shape((wide // 2, depth, 4 * local))] * 2,
        "self_weight_grads",
        cost(24 * seq * width * local, 16 * seq * width),
        prefetch=1,
        scratch=[pltpu.VMEM((tile, 4 * local), F32)],
    )(bits, near, far, dnear, dfar, own, core, other)


def merge_body(bits, keep_in, got_in, keep_out, give_out, *, which):
    mine = bits[which] if which >= 0 else 0
    keep_out[:, 0] = (keep_in[:, mine].astype(F32) + got_in[:, mine].astype(F32)).astype(BF16)
    give_out[:, 0] = (keep_in[:, 1 - mine].astype(F32) + got_in[:, 1 - mine].astype(F32)).astype(BF16)


def merge(bits, keep, got, which):
    groups, _, rows, columns = keep.shape
    tile = rows // 2 if rows % 32 == 0 else rows
    both = pl.BlockSpec((groups, 2, tile, columns), lambda i, *_: (0, 0, i, 0))
    out = pl.BlockSpec((groups, 1, tile, columns), lambda i, *_: (0, 0, i, 0))
    return call(
        functools.partial(merge_body, which=which),
        (rows // tile,),
        [both, both],
        [out, out],
        [shape((groups, 1, rows, columns))] * 2,
        "merge",
        cost(0, 12 * groups * rows * columns),
        prefetch=1,
    )(bits, keep, got)


def scatter_wide(bits, then, keep, give, which, got):
    dims = keep.shape[-2:]
    parts = lax.axis_size("wide") >> which
    lead = keep.size // (parts * dims[0] * dims[1])
    while parts > 1:
        parts //= 2
        view = (lead * parts, 2) + dims
        keep, give = merge(then(bits), keep.reshape(view), got.reshape(view), which)
        then.last = keep
        which += 1
        got = swap(give, "wide", 1 << (which - 1))
    view = (lead,) + dims
    return keep.reshape(view).astype(F32) + got.reshape(view).astype(F32)


def place_body(order, a, b, c, d, *refs, start):
    out, held, reads, writes = refs[-4:]
    blocks = (a, b, c, d)
    loads = [pltpu.make_async_copy(item, held.at[r], reads.at[r]) for r, item in enumerate(blocks)]
    for item in loads:
        item.start()
    stores = []
    for r, item in enumerate(loads):
        item.wait()
        if start is None:
            target = out.at[order[r]]
        else:
            target = out.at[:, order[r], pl.ds(start, held.shape[2])]
        stores.append(pltpu.make_async_copy(held.at[r], target, writes.at[r]))
        stores[-1].start()
    for item in stores:
        item.wait()


def place_blocks(order, blocks, dims, start=None, before=None):
    anywhere = pl.BlockSpec(memory_space=pl.ANY)
    extra = () if before is None else (before,)
    return pl.pallas_call(
        functools.partial(place_body, start=start),
        grid_spec=pltpu.PrefetchScalarGridSpec(
            num_scalar_prefetch=1,
            grid=(1,),
            in_specs=[anywhere] * (4 + len(extra)),
            out_specs=anywhere,
            scratch_shapes=[
                pltpu.VMEM((4,) + blocks[0].shape, BF16),
                pltpu.SemaphoreType.DMA((4,)),
                pltpu.SemaphoreType.DMA((4,)),
            ],
        ),
        out_shape=shape(dims),
        input_output_aliases={5: 0} if extra else {},
        compiler_params=pltpu.CompilerParams(vmem_limit_bytes=VMEM_LIMIT),
        cost_estimate=cost(0, 16 * blocks[0].size),
        name="place_blocks",
    )(order, *blocks, *extra)


def on_device(
    tokens, lengths, memory, gains, self_qkv, self_out, cross_q, cross_kv, cross_out, fc_in, fc_out, out_grad
):
    clips, seq, width = tokens.shape
    wide = lax.axis_size("wide")
    narrow = lax.axis_size("narrow")
    me = lax.axis_index("narrow")
    place = lax.axis_index("wide")
    bits = ((place >> jnp.arange(8)) & 1).astype(jnp.int32)
    share = memory.shape[1]
    local = self_qkv.shape[2]
    depth = width // wide
    order = (me ^ jnp.arange(4)).astype(jnp.int32)
    near_order = (me ^ jnp.array([1, 0])).astype(jnp.int32)
    far_order = (me ^ jnp.array([3, 2])).astype(jnp.int32)
    gain_row = [gains[i : i + 1] for i in range(4)]
    then = Order()

    by_clip = memory.reshape(wide, narrow, share, width)
    sizes = (-(-share // 32) * 16, share - -(-share // 32) * 16)
    starts = (0, sizes[0])
    last = AUDIO - (wide - 1) * share
    valid = [(wide - 1) * size + min(max(last - start, 0), size) for start, size in zip(starts, sizes)]

    def encoder_rows(part, *named):
        block = encode(then(order, *named), by_clip, gain_row[0], starts[part], sizes[part])
        then.last = block
        block = lax.all_to_all(block, "wide", 0, 0, tiled=True)
        return block.reshape(wide * sizes[part], width)

    encoded_first = encoder_rows(0)
    self_qkv = self_qkv.transpose(0, 2, 1)
    pack_kv = cross_kv.transpose(0, 2, 1).reshape(2 * local, width)
    packs_one = gather_narrow(jnp.concatenate((self_out, then(cross_q).T)))

    normed_far, qkv_far, mixed_three, mixed_two, lse_far = self_fwd(
        then(far_order), lengths, tokens, gain_row[1], self_qkv
    )
    then.last = mixed_two
    mix_two = swap(mixed_two, "narrow", 2)
    crossing = swap(mixed_three, "narrow", 1)
    normed_near, qkv_near, mixed_one, mixed_zero, lse_near = self_fwd(
        then(near_order), lengths, tokens, gain_row[1], self_qkv
    )
    then.last = mixed_zero
    mix_three = swap(then(crossing), "narrow", 2)
    packs_kv = gather_narrow(then(pack_kv))
    mixes = [mixed_zero, swap(mixed_one, "narrow", 1), mix_two, mix_three]
    packs_one = finish(packs_one, then)
    encoded_second = encoder_rows(1, mix_two, packs_one[2])
    encoded = (encoded_first, encoded_second)
    after_self, normed_two, query = to_query(then(order), tokens, mixes, packs_one, gain_row[2])
    then.last = query
    packs_kv = finish(packs_kv, then)
    packs_out = gather_narrow(then(cross_out))
    kv_first, *before = cross_first(then(query), encoded_first, packs_kv, valid[0])
    then.last = kv_first
    packs_out = finish(packs_out, then)
    kv_second, cross_mixed, cross_lse, after_cross, normed_three = cross_second(
        query, encoded_second, packs_kv, packs_out, valid[1], before, after_self, gain_row[3]
    )
    then.last = normed_three

    rows = gather_narrow(normed_three)
    hidden_a, pre_a, live_a, part_zero, feed_zero, part_one, feed_one = feed_forward(
        order[:2], lengths, rows[:2], out_grad, fc_in, fc_out
    )
    then.last = part_one
    rows = finish(rows, then)
    part_near = swap(part_one, "narrow", 1)
    feed_near = swap(feed_one, "narrow", 1)
    hidden_c, pre_c, live_c, part_three, feed_three = feed_forward(
        order[3:], lengths, rows[3:], out_grad, fc_in, fc_out
    )
    then.last = part_three
    part_cross = swap(part_three, "narrow", 1)
    feed_cross = swap(feed_three, "narrow", 1)
    hidden_b, pre_b, live_b, part_two, feed_two = feed_forward(
        then(order[2:3]), lengths, rows[2:3], out_grad, fc_in, fc_out
    )
    part_far = (part_two.astype(F32) + part_cross.astype(F32)).astype(BF16)
    then.last = part_far
    part_far = swap(part_far, "narrow", 2)
    feed_keep, feed_give = feed_weights(
        then(bits, part_near, feed_near, feed_cross),
        rows, (pre_a, pre_b, pre_c), (live_a, live_b, live_c), (hidden_a, hidden_b, hidden_c), wide,
    )
    then.last = feed_give
    feed_far = (then(feed_two).astype(F32) + feed_cross.astype(F32)).astype(BF16)
    then.last = feed_far
    feed_far = swap(then(feed_far, part_far), "narrow", 2)
    feed_got = swap(feed_give, "wide", 1)

    grad_cross, grad_two, grad_mixed, gain_three, dq, dkv_first, frames_first = cross_first_back(
        then(order), lengths, out_grad, (part_zero, part_near, part_far), after_cross, gain_row[3],
        packs_kv, packs_out, query, kv_first, cross_mixed, cross_lse, valid[0],
    )
    then.last = dkv_first

    def frames_sent(block, part):
        block = block.reshape(wide, sizes[part], width)
        return lax.all_to_all(block, "wide", 0, 0, tiled=True)

    frames_first = frames_sent(frames_first, 0)
    block_own = (
        then(after_cross) + (feed_zero.astype(F32) + feed_near.astype(F32) + feed_far.astype(F32))
    ).astype(BF16)
    then.last = block_own
    block_all = gather_narrow(block_own)
    view = (2 * (wide // 4), 2, depth, width)
    feed_keep, feed_give = merge(then(bits), feed_keep.reshape(view), feed_got.reshape(view), 1)
    then.last = feed_keep
    feed_got = swap(feed_give, "wide", 2)
    dq, dkv_second, frames_second, grad_self, grad_one, head0, head1, head2, head3, gain_two = cross_second_back(
        query, kv_second, grad_mixed, cross_mixed, cross_lse, dq, packs_kv, packs_one, after_self,
        then(gain_row[2]), grad_cross, valid[1],
    )
    then.last = dq
    heads_one = swap(head1, "narrow", 1)
    heads_two = swap(head2, "narrow", 2)
    head3 = swap(head3, "narrow", 2)
    frames_second = frames_sent(frames_second, 1)
    block_all = finish(block_all, then)

    back_first, gain_first = memory_back(then(order), by_clip, gain_row[0], frames_first, starts[0])
    then.last = back_first
    dqkv_near, part_one, part_zero = self_bwd(
        then(near_order, heads_two, head3), lengths, qkv_near, mixed_one, mixed_zero, lse_near, heads_one, head0,
        self_qkv,
    )
    then.last = part_one
    heads_three = swap(then(head3), "narrow", 1)
    back_first = gather_narrow(back_first)
    part_near = swap(part_one, "narrow", 1)
    feed_grads = scatter_wide(bits, then, feed_keep, feed_give, 2, feed_got)
    dqkv_far, part_three, part_two = self_bwd(
        then(far_order), lengths, qkv_far, mixed_three, mixed_two, lse_far, heads_three, heads_two, self_qkv
    )
    then.last = part_three
    part_cross = swap(part_three, "narrow", 1)
    block_out = place_blocks(then(order), block_all, (clips, seq, width))
    then.last = block_out
    part_far = (then(part_two).astype(F32) + part_cross.astype(F32)).astype(BF16)
    then.last = part_far
    part_far = swap(part_far, "narrow", 2)
    keep, give, self_keep, self_give = head_weights(
        encoded, (dkv_first, dkv_second), then(normed_two), dq, grad_one, grad_two, cross_mixed, mixes
    )
    then.last = keep
    got = swap(give, "narrow", 1)
    self_got = swap(self_give, "narrow", 1)
    back_second, gain_second = memory_back(then(order), by_clip, gain_row[0], frames_second, starts[1])
    then.last = back_second
    self_other = (self_keep[1].astype(F32) + self_got[1].astype(F32)).astype(BF16)
    then.last = self_other
    self_other = swap(self_other, "narrow", 2)
    view = (wide, 2, depth, width)
    keep, give = merge(then(bits), keep.reshape(view), got.reshape(view), 0)
    then.last = keep
    got = swap(give, "wide", 1)
    tokens_own, gain_one = to_tokens_grad(
        then(order), tokens, part_zero, part_near, part_far, grad_self, gain_row[1]
    )
    then.last = tokens_own
    tokens_all = gather_narrow(tokens_own)
    self_keep, self_give = self_weights(
        then(bits), normed_near, normed_far, dqkv_near, dqkv_far, self_keep, self_got, self_other, wide
    )
    then.last = self_keep
    self_got = swap(self_give, "wide", 1)
    back_second = gather_narrow(back_second)
    back_first = finish(back_first, then)
    view = (2 * (wide // 4), 2, depth, width)
    keep, give = merge(then(bits), keep.reshape(view), got.reshape(view), 1)
    then.last = keep
    got = swap(give, "wide", 2)
    memory_grad = place_blocks(then(order), back_first, (wide, narrow, share, width), starts[0])
    then.last = memory_grad
    view = (wide // 4, 2, depth, width)
    self_keep, self_give = merge(then(bits), self_keep.reshape(view), self_got.reshape(view), 1)
    then.last = self_keep
    self_got = swap(self_give, "wide", 2)
    tokens_all = finish(tokens_all, then)
    keep = scatter_wide(bits, then, keep, give, 2, got).astype(BF16)
    then.last = keep
    other = swap(keep[1], "narrow", 2)
    tokens_grad = place_blocks(then(order), tokens_all, (clips, seq, width))
    then.last = tokens_grad
    self_grads = scatter_wide(bits, then, self_keep, self_give, 2, self_got)[0]
    back_second = finish(back_second, then)
    head_grads = keep[0].astype(F32) + other.astype(F32)
    memory_grad = place_blocks(
        then(order), back_second, (wide, narrow, share, width), starts[1], memory_grad
    ).reshape(memory.shape)

    gain_terms = jnp.concatenate((gain_first + gain_second, gain_one, gain_two, gain_three))
    gain_terms = gain_terms + swap(gain_terms, "narrow", 1)
    gain_terms = gain_terms + swap(gain_terms, "narrow", 2)
    gain_terms = gain_terms.reshape(4, wide, depth).transpose(1, 0, 2)
    gains_grad = jnp.sum(lax.all_to_all(gain_terms, "wide", 0, 0, tiled=True), axis=0)

    heads = lambda i: head_grads[:, i * local : (i + 1) * local]
    own = lambda i: self_grads[:, i * local : (i + 1) * local]
    return (
        block_out,
        tokens_grad,
        memory_grad,
        gains_grad,
        jnp.stack([own(i) for i in range(3)]),
        own(3).T,
        heads(2),
        jnp.stack((heads(0), heads(1))),
        heads(3).T,
        feed_grads[0],
        feed_grads[1].T,
    )


def solution(mesh):
    placed = (
        P("wide", None, None),
        P("wide"),
        P(None, "wide", None),
        P(),
        P(None, None, "narrow"),
        P("narrow", None),
        P(None, "narrow"),
        P(None, None, "narrow"),
        P("narrow", None),
        P(None, "narrow"),
        P("narrow", None),
        P("wide", None, None),
    )
    return jax.shard_map(
        on_device,
        mesh=mesh,
        in_specs=placed,
        out_specs=(
            P("wide", None, None),
            P("wide", None, None),
            P(None, "wide", None),
            P(None, "wide"),
            P(None, "wide", "narrow"),
            P("narrow", "wide"),
            P("wide", "narrow"),
            P(None, "wide", "narrow"),
            P("narrow", "wide"),
            P("wide", "narrow"),
            P("narrow", "wide"),
        ),
        check_vma=False,
    )
```

```python
import functools

import jax
import jax.numpy as jnp
from jax import lax
from jax.experimental import pallas as pl
from jax.experimental.pallas import tpu as pltpu
from jax.sharding import PartitionSpec as P

HEAD_DIM = 64
AUDIO = 1500
EPSILON = 1e-05
NEG_FILL = -1e30
INV_ROOT = HEAD_DIM**-0.5
F32 = jnp.float32
BF16 = jnp.bfloat16
VMEM_LIMIT = 56 << 20
COST_SCALE = 1.0
LONG = 50.0
SHORT = 1e-6
SPLIT = 32


def dot(left, right, left_dim=1, right_dim=0):
    return lax.dot_general(
        left, right, (((left_dim,), (right_dim,)), ((), ())), preferred_element_type=F32
    )


def call(body, grid, in_specs, out_specs, out_shape, name, estimate, prefetch=0, scratch=()):
    return pl.pallas_call(
        body,
        grid_spec=pltpu.PrefetchScalarGridSpec(
            num_scalar_prefetch=prefetch,
            grid=grid,
            in_specs=in_specs,
            out_specs=out_specs,
            scratch_shapes=list(scratch),
        ),
        out_shape=out_shape,
        compiler_params=pltpu.CompilerParams(vmem_limit_bytes=VMEM_LIMIT),
        cost_estimate=estimate,
        name=name,
    )


def shape(dims, dtype=BF16):
    return jax.ShapeDtypeStruct(dims, dtype)


def cost(flops, moved, exps=0, scale=None):
    scale = COST_SCALE if scale is None else scale
    return pl.CostEstimate(
        flops=int(flops * scale), bytes_accessed=int(moved * scale), transcendentals=int(exps * scale)
    )


def whole(shape):
    return pl.BlockSpec(shape, lambda *_: (0,) * len(shape))


def norm_stats(values):
    center = values - jnp.mean(values, axis=-1, keepdims=True)
    spread = jnp.mean(center * center, axis=-1, keepdims=True)
    inverse = lax.rsqrt(spread + EPSILON)
    return center * inverse, inverse


def norm_back(unit, inverse, gains_all, grad):
    scaled = grad * gains_all
    first = jnp.mean(scaled, axis=-1, keepdims=True)
    second = jnp.mean(scaled * unit, axis=-1, keepdims=True)
    return (scaled - first - unit * second) * inverse


def swap(values, axis, bit):
    size = lax.axis_size(axis)
    return lax.ppermute(values, axis, [(i, i ^ bit) for i in range(size)])


def gather_narrow(own):
    other = swap(own, "narrow", 2)
    return [own, swap(own, "narrow", 1), other]


def finish(blocks, then):
    return blocks + [swap(then(blocks[2]), "narrow", 1)]


class Order:
    def __init__(self):
        self.last = None

    def __call__(self, item, *named):
        named = named if self.last is None else named + (self.last,)
        if named:
            item, _ = lax.optimization_barrier((item, named))
        return item

    def join(self, *items):
        items = lax.optimization_barrier(items)
        self.last = items[0]
        return items


def encode_body(order, memory_ref, gain_ref, out_ref):
    unit, _ = norm_stats(memory_ref[:, 0].astype(F32))
    out_ref[...] = (unit * gain_ref[0 : 1]).astype(BF16)


def encode(order, memory, gains_all, start, size):
    wide, _, _, width = memory.shape
    group = min(4, wide)
    return call(
        encode_body,
        (wide // group,),
        [
            pl.BlockSpec((group, 1, size, width), lambda i, order: (i, order[0], start // size, 0)),
            whole(gains_all.shape),
        ],
        pl.BlockSpec((group, size, width), lambda i, *_: (i, 0, 0)),
        shape((wide, size, width)),
        "encode",
        cost(0, 4 * wide * size * width),
        prefetch=1,
    )(order, memory, gains_all)


def memory_back_body(order, memory_ref, gain_ref, grad_ref, out_ref, gain_out):
    unit, inverse = norm_stats(memory_ref[:, 0].astype(F32))
    grad = grad_ref[...].astype(F32)
    out_ref[...] = norm_back(unit, inverse, gain_ref[0 : 1], grad).astype(BF16)

    @pl.when(pl.program_id(0) == 0)
    def _():
        gain_out[...] = jnp.zeros_like(gain_out)

    gain_out[...] += jnp.sum(jnp.sum(grad * unit, axis=0), axis=0, keepdims=True)


def memory_back(order, memory, gains_all, grad, start, scale):
    wide, _, _, width = memory.shape
    size = grad.shape[1]
    group = min(4, wide)
    rows = pl.BlockSpec((group, size, width), lambda i, *_: (i, 0, 0))
    return call(
        memory_back_body,
        (wide // group,),
        [
            pl.BlockSpec((group, 1, size, width), lambda i, order: (i, order[0], start // size, 0)),
            whole(gains_all.shape),
            rows,
        ],
        [rows, whole((1, width))],
        [shape((wide, size, width)), shape((1, width), F32)],
        "memory_back",
        cost(0, 6 * wide * size * width, scale=scale),
        prefetch=1,
    )(order, memory, gains_all, grad)


def self_fwd_body(order, lengths, token_ref, gain_ref, weight_ref, normed_ref, qkv_ref, first_ref, second_ref, lse_ref):
    seq = token_ref.shape[1]
    heads = weight_ref.shape[1] // HEAD_DIM
    step = pl.program_id(0)
    length = lengths[order[step]]
    unit, _ = norm_stats(token_ref[0].astype(F32))
    normed = (unit * gain_ref[1 : 2]).astype(BF16)
    normed_ref[0] = normed
    for i in range(3):
        qkv_ref[0, i] = dot(normed, weight_ref[i], 1, 1).astype(BF16)
    cut = 256 if seq > 256 else seq
    mixed = []
    for h in range(heads):
        columns = slice(h * HEAD_DIM, (h + 1) * HEAD_DIM)
        parts = []
        for start, stop in ((0, cut), (cut, seq)):
            if start == stop:
                continue
            queries = qkv_ref[0, 0, start:stop, columns] * jnp.asarray(INV_ROOT, BF16)
            scores = dot(qkv_ref[0, 1, :stop, columns], queries, 1, 1)
            key = lax.broadcasted_iota(jnp.int32, scores.shape, 0)
            query = lax.broadcasted_iota(jnp.int32, scores.shape, 1) + start
            scores = jnp.where((key <= query) & (key < length), scores, NEG_FILL)
            top = jnp.max(scores, axis=0, keepdims=True)
            probs = jnp.exp(scores - top)
            total = jnp.sum(probs, axis=0, keepdims=True)
            out = dot(qkv_ref[0, 2, :stop, columns], probs.astype(BF16), 0, 0) / total
            parts.append(out.T)
            lse_ref[0, h : h + 1, start:stop] = top + jnp.log(total)
        mixed.append(jnp.concatenate(parts, axis=0))
    mixed = jnp.concatenate(mixed, axis=1).astype(BF16)

    @pl.when(step == 0)
    def _():
        first_ref[...] = mixed

    @pl.when(step == 1)
    def _():
        second_ref[...] = mixed


def self_fwd(order, lengths, tokens, gains_all, weights):
    _, seq, width = tokens.shape
    local = weights.shape[1]
    heads = local // HEAD_DIM
    return call(
        self_fwd_body,
        (2,),
        [
            pl.BlockSpec((1, seq, width), lambda i, order, lengths: (order[i], 0, 0)),
            whole(gains_all.shape),
            whole((3, local, width)),
        ],
        [
            pl.BlockSpec((1, seq, width), lambda i, *_: (i, 0, 0)),
            pl.BlockSpec((1, 3, seq, local), lambda i, *_: (i, 0, 0, 0)),
            whole((seq, local)),
            whole((seq, local)),
            pl.BlockSpec((1, heads, seq), lambda i, *_: (i, 0, 0)),
        ],
        [
            shape((2, seq, width)),
            shape((2, 3, seq, local)),
            shape((seq, local)),
            shape((seq, local)),
            shape((2, heads, seq), F32),
        ],
        "self_forward",
        cost(2 * (6 * seq * width * local + 8 * seq * seq * local), 2 * seq * width * 8, 2 * heads * seq * seq),
        prefetch=2,
    )(order, lengths, tokens, gains_all, weights)


def self_bwd_body(order, lengths, qkv_ref, mixed0_ref, mixed1_ref, lse_ref, grad0_ref, grad1_ref, weight_ref, dqkv_ref, first_ref, second_ref):
    seq = qkv_ref.shape[2]
    heads = weight_ref.shape[1] // HEAD_DIM
    step = pl.program_id(0)
    length = lengths[order[step]]
    grad = jnp.where(step == 0, grad0_ref[...], grad1_ref[...])
    mixed = jnp.where(step == 0, mixed0_ref[...], mixed1_ref[...])
    inner = (grad.astype(F32) * mixed.astype(F32)).T
    cut = 256 if seq > 256 else seq
    for h in range(heads):
        columns = slice(h * HEAD_DIM, (h + 1) * HEAD_DIM)
        keys = qkv_ref[0, 1, :, columns]
        values = qkv_ref[0, 2, :, columns]
        dq_parts = []
        dk = jnp.zeros((seq, HEAD_DIM), F32)
        dv = jnp.zeros((seq, HEAD_DIM), F32)
        for start, stop in ((0, cut), (cut, seq)):
            if start == stop:
                continue
            queries = qkv_ref[0, 0, start:stop, columns] * jnp.asarray(INV_ROOT, BF16)
            grads = grad[start:stop, columns]
            scores = dot(keys[:stop], queries, 1, 1)
            key = lax.broadcasted_iota(jnp.int32, scores.shape, 0)
            query = lax.broadcasted_iota(jnp.int32, scores.shape, 1) + start
            allowed = (key <= query) & (key < length)
            probs = jnp.exp(jnp.where(allowed, scores, NEG_FILL) - lse_ref[0, h : h + 1, start:stop])
            dp = dot(values[:stop], grads, 1, 1)
            centre = jnp.sum(inner[columns, start:stop], axis=0, keepdims=True)
            ds = (probs * (dp - centre)).astype(BF16)
            dk_now = dot(ds, queries)
            dv_now = dot(probs.astype(BF16), grads)
            if stop < seq:
                pad = jnp.zeros((seq - stop, HEAD_DIM), F32)
                dk_now = jnp.concatenate((dk_now, pad), axis=0)
                dv_now = jnp.concatenate((dv_now, pad), axis=0)
            dk, dv = dk + dk_now, dv + dv_now
            dq_parts.append((dot(keys[:stop], ds, 0, 0) * INV_ROOT).T)
        dqkv_ref[0, 0, :, columns] = jnp.concatenate(dq_parts, axis=0).astype(BF16)
        dqkv_ref[0, 1, :, columns] = dk.astype(BF16)
        dqkv_ref[0, 2, :, columns] = dv.astype(BF16)
    total = dot(dqkv_ref[0, 0], weight_ref[0])
    total = total + dot(dqkv_ref[0, 1], weight_ref[1])
    total = (total + dot(dqkv_ref[0, 2], weight_ref[2])).astype(BF16)

    @pl.when(step == 0)
    def _():
        first_ref[...] = total

    @pl.when(step == 1)
    def _():
        second_ref[...] = total


def self_bwd(order, lengths, qkv, mixed0, mixed1, lse, grad0, grad1, weights, scale):
    _, _, seq, local = qkv.shape
    width = weights.shape[2]
    heads = local // HEAD_DIM
    return call(
        self_bwd_body,
        (2,),
        [
            pl.BlockSpec((1, 3, seq, local), lambda i, *_: (i, 0, 0, 0)),
            whole((seq, local)),
            whole((seq, local)),
            pl.BlockSpec((1, heads, seq), lambda i, *_: (i, 0, 0)),
            whole((seq, local)),
            whole((seq, local)),
            whole((3, local, width)),
        ],
        [
            pl.BlockSpec((1, 3, seq, local), lambda i, *_: (i, 0, 0, 0)),
            whole((seq, width)),
            whole((seq, width)),
        ],
        [shape((2, 3, seq, local)), shape((seq, width)), shape((seq, width))],
        "self_backward",
        cost(2 * (6 * seq * width * local + 20 * seq * seq * local), 2 * seq * width * 8, 2 * heads * seq * seq, scale=scale),
        prefetch=2,
    )(order, lengths, qkv, mixed0, mixed1, lse, grad0, grad1, weights)


def to_query_body(order, token_ref, m0, m1, m2, m3, p0, p1, p2, p3, gain_ref, after_ref, normed_ref, query_ref):
    local = m0.shape[1]
    rows = token_ref[0].astype(F32)
    for mixed, pack in ((m0, p0), (m1, p1), (m2, p2), (m3, p3)):
        rows = rows + dot(mixed[...], pack[:local])
    after_ref[...] = rows
    unit, _ = norm_stats(rows)
    normed = (unit * gain_ref[2 : 3]).astype(BF16)
    normed_ref[...] = normed
    for r, pack in enumerate((p0, p1, p2, p3)):
        query = dot(normed, pack[local:], 1, 1).astype(BF16)
        query_ref[r // 2, :, (r % 2) * local : (r % 2 + 1) * local] = query


def to_query(order, tokens, mixes, packs, gains_all):
    _, seq, width = tokens.shape
    local = mixes[0].shape[1]
    tile = seq // 2
    return call(
        to_query_body,
        (2,),
        [pl.BlockSpec((1, tile, width), lambda i, order: (order[0], i, 0))]
        + [pl.BlockSpec((tile, local), lambda i, *_: (i, 0))] * 4
        + [whole((2 * local, width))] * 4
        + [whole(gains_all.shape)],
        [
            pl.BlockSpec((tile, width), lambda i, *_: (i, 0)),
            pl.BlockSpec((tile, width), lambda i, *_: (i, 0)),
            pl.BlockSpec((2, tile, 2 * local), lambda i, *_: (0, i, 0)),
        ],
        [shape((seq, width), F32), shape((seq, width)), shape((2, seq, 2 * local))],
        "self_out_to_query",
        cost(4 * seq * width * width, seq * width * 12 + 4 * width * width),
        prefetch=1,
    )(order, tokens, *mixes, *packs, gains_all)


def head_places(local):
    for r in range(2):
        for h in range(local // HEAD_DIM):
            at = r * local + h * HEAD_DIM
            key = 2 * r * local + h * HEAD_DIM
            yield (
                at // HEAD_DIM,
                slice(at, at + HEAD_DIM),
                slice(key, key + HEAD_DIM),
                slice(key + local, key + local + HEAD_DIM),
            )


def cross_first_body(query_ref, encoded_ref, w0, w1, w2, w3, kv_ref, acc_ref, top_ref, total_ref, *, valid):
    make_keys_values(encoded_ref, (w0, w1, w2, w3), kv_ref)
    frames = kv_ref.shape[0]
    for head, columns, key, value in head_places(query_ref.shape[2] // 2):
        queries = query_ref[0, :, columns] * jnp.asarray(INV_ROOT, BF16)
        scores = dot(kv_ref[:, key], queries, 1, 1)
        if valid < frames:
            frame = lax.broadcasted_iota(jnp.int32, scores.shape, 0)
            scores = jnp.where(frame < valid, scores, NEG_FILL)
        top = jnp.max(scores, axis=0, keepdims=True)
        probs = jnp.exp(scores - top)
        acc_ref[0, columns, :] = dot(kv_ref[:, value], probs.astype(BF16), 0, 0)
        top_ref[0, head : head + 1, :] = top
        total_ref[0, head : head + 1, :] = jnp.sum(probs, axis=0, keepdims=True)


def make_keys_values(encoded_ref, weights, kv_ref):
    pair = weights[0].shape[0]
    for step in range(2):

        @pl.when(pl.program_id(0) == step)
        def _():
            for r in range(2):
                kv = dot(encoded_ref[...], weights[2 * step + r][...], 1, 1)
                kv_ref[:, r * pair : (r + 1) * pair] = kv.astype(BF16)


def cross_second_body(
    query_ref, encoded_ref, w0, w1, w2, w3, acc_in, top_in, total_in, after_ref, o0, o1, o2, o3, gain_ref,
    kv_ref, mixed_ref, lse_ref, next_ref, normed_ref, *, valid,
):
    make_keys_values(encoded_ref, (w0, w1, w2, w3), kv_ref)
    frames = kv_ref.shape[0]
    local = o0.shape[0]
    for head, columns, key, value in head_places(local):
        queries = query_ref[0, :, columns] * jnp.asarray(INV_ROOT, BF16)
        scores = dot(kv_ref[:, key], queries, 1, 1)
        if valid < frames:
            frame = lax.broadcasted_iota(jnp.int32, scores.shape, 0)
            scores = jnp.where(frame < valid, scores, NEG_FILL)
        before = top_in[0, head : head + 1, :]
        top = jnp.maximum(jnp.max(scores, axis=0, keepdims=True), before)
        probs = jnp.exp(scores - top)
        fade = jnp.exp(before - top)
        total = jnp.sum(probs, axis=0, keepdims=True) + total_in[0, head : head + 1, :] * fade
        out = dot(kv_ref[:, value], probs.astype(BF16), 0, 0) + acc_in[0, columns, :] * fade
        mixed_ref[0, :, columns] = (out / total).T.astype(BF16)
        lse_ref[0, head : head + 1, :] = top + jnp.log(total)
    outs = (o0, o1, o2, o3)
    for step in range(2):

        @pl.when(pl.program_id(0) == step)
        def _():
            rows = after_ref[...] if step == 0 else next_ref[...]
            for r in range(2):
                rows = rows + dot(mixed_ref[0, :, r * local : (r + 1) * local], outs[2 * step + r][...])
            next_ref[...] = rows
            if step == 1:
                unit, _ = norm_stats(rows)
                normed_ref[...] = (unit * gain_ref[3 : 4]).astype(BF16)


def pack_specs(packs, rows, index):
    width = packs[0].shape[1]
    return [pl.BlockSpec((rows, width), lambda *_: (index, 0))] * 4


def cross_first(query, encoded, packs, valid):
    _, seq, pair = query.shape
    frames, width = encoded.shape
    heads = pair // HEAD_DIM
    stats = pl.BlockSpec((1, heads, seq), lambda i: (i, 0, 0))
    return call(
        functools.partial(cross_first_body, valid=valid),
        (2,),
        [pl.BlockSpec((1, seq, pair), lambda i: (i, 0, 0)), whole((frames, width))] + pack_specs(packs, pair, 0),
        [
            pl.BlockSpec((frames, 2 * pair), lambda i: (0, i)),
            pl.BlockSpec((1, pair, seq), lambda i: (i, 0, 0)),
            stats,
            stats,
        ],
        [
            shape((frames, 4 * pair)),
            shape((2, pair, seq), F32),
            shape((2, heads, seq), F32),
            shape((2, heads, seq), F32),
        ],
        "cross_first",
        cost(4 * frames * width * width + 40 * seq * frames * pair, 8 * frames * width, 2 * heads * seq * frames),
    )(query, encoded, *packs)


def cross_second(query, encoded, packs, packs_out, valid, before, after, gains_all):
    _, seq, pair = query.shape
    frames, width = encoded.shape
    heads = pair // HEAD_DIM
    rows = pl.BlockSpec((1, seq, pair), lambda i: (i, 0, 0))
    stats = pl.BlockSpec((1, heads, seq), lambda i: (i, 0, 0))
    acc = pl.BlockSpec((1, pair, seq), lambda i: (i, 0, 0))
    return call(
        functools.partial(cross_second_body, valid=valid),
        (2,),
        [rows, whole((frames, width))]
        + pack_specs(packs, pair, 0)
        + [acc, stats, stats, whole((seq, width))]
        + pack_specs(packs_out, pair // 2, 0)
        + [whole(gains_all.shape)],
        [pl.BlockSpec((frames, 2 * pair), lambda i: (0, i)), rows, stats, whole((seq, width)), whole((seq, width))],
        [
            shape((frames, 4 * pair)),
            shape((2, seq, pair)),
            shape((2, heads, seq), F32),
            shape((seq, width), F32),
            shape((seq, width)),
        ],
        "cross_second",
        cost(4 * frames * width * width + 40 * seq * frames * pair, 10 * frames * width, 2 * heads * seq * frames),
    )(query, encoded, *packs, *before, after, *packs_out, gains_all)


def feed_body(order, lengths, *refs, count):
    row_refs, (grad_ref, in_ref, out_ref, hidden_ref, pre_ref, live_ref) = refs[:count], refs[count : count + 6]
    outs = refs[count + 6 :]
    step = pl.program_id(0)
    tile = grad_ref.shape[1]
    rows = row_refs[0][...]
    if count == 2:
        rows = jnp.where(step == 0, rows, row_refs[1][...])
    place = lax.broadcasted_iota(jnp.int32, grad_ref.shape[1:], 0) + pl.program_id(1) * tile
    grads = jnp.where(place < lengths[order[step]], grad_ref[0], jnp.zeros((), BF16))
    live_ref[0] = grads
    pre = dot(rows, in_ref[...])
    half = 0.5 * (1.0 + lax.erf(pre * (0.5**0.5)))
    hidden = (pre * half).astype(BF16)
    slope = half + pre * jnp.exp(-0.5 * pre * pre) * 0.3989422804014327
    hidden_ref[0] = hidden
    grad_pre = (dot(grads, out_ref[...], 1, 1) * slope).astype(BF16)
    pre_ref[0] = grad_pre
    part = dot(grad_pre, in_ref[...], 1, 1).astype(BF16)
    feed = dot(hidden, out_ref[...]).astype(BF16)
    for i in range(count):

        @pl.when(step == i)
        def _():
            outs[2 * i][...] = part
            outs[2 * i + 1][...] = feed


def feed_forward(order, lengths, rows, out_grad, fc_in, fc_out):
    count = len(rows)
    seq, width = rows[0].shape
    units = fc_in.shape[1]
    tiles = 2
    tile = seq // tiles
    block = lambda last: pl.BlockSpec((1, tile, last), lambda i, j, *_: (i, j, 0))
    single = [
        pl.BlockSpec((tile, width), lambda i, j, *_: (jnp.where(i == 0, j, tiles - 1), 0)),
        pl.BlockSpec((tile, width), lambda i, j, *_: (jnp.where(i == 0, 0, j), 0)),
    ]
    if count == 1:
        single = [pl.BlockSpec((tile, width), lambda i, j, *_: (j, 0))]
    return call(
        functools.partial(feed_body, count=count),
        (count, tiles),
        single
        + [
            pl.BlockSpec((1, tile, width), lambda i, j, order, lengths: (order[i], j, 0)),
            whole((width, units)),
            whole((units, width)),
        ],
        [block(units), block(units), block(width)] + [spec for spec in single for _ in range(2)],
        [shape((count, seq, units)), shape((count, seq, units)), shape((count, seq, width))]
        + [shape((seq, width))] * (2 * count),
        "feed_forward",
        cost(8 * count * seq * width * units, count * seq * width * 14, 2 * count * seq * units),
        prefetch=2,
    )(order, lengths, *rows, out_grad, fc_in, fc_out)


def add_gain(gain_out, term):
    @pl.when(pl.program_id(0) == 0)
    def _():
        gain_out[...] = jnp.zeros_like(gain_out)

    gain_out[...] += term


def cross_back(queries_ref, kv_ref, grads_ref, mixed_ref, lse_ref, dkv_ref, local, valid, store):
    frames = kv_ref.shape[0]
    inner = (grads_ref.astype(F32) * mixed_ref[0].astype(F32)).T
    for head, columns, key, value in head_places(local):
        queries = queries_ref[0, :, columns] * jnp.asarray(INV_ROOT, BF16)
        grads = grads_ref[:, columns]
        centre = jnp.sum(inner[columns, :], axis=0, keepdims=True)
        keys = kv_ref[:, key]
        probs = jnp.exp(dot(keys, queries, 1, 1) - lse_ref[0, head : head + 1, :])
        if valid < frames:
            frame = lax.broadcasted_iota(jnp.int32, probs.shape, 0)
            probs = jnp.where(frame < valid, probs, 0.0)
        dp = dot(kv_ref[:, value], grads, 1, 1)
        ds = (probs * (dp - centre)).astype(BF16)
        dkv_ref[:, value] = dot(probs.astype(BF16), grads).astype(BF16)
        dkv_ref[:, key] = dot(ds, queries).astype(BF16)
        store(columns, dot(keys, ds, 0, 0))


def encoded_back(dkv_ref, weights, out_ref, acc):
    pair = weights[0].shape[0]
    for step in range(2):

        @pl.when(pl.program_id(0) == step)
        def _():
            total = dot(dkv_ref[:, :pair], weights[2 * step][...]) + dot(dkv_ref[:, pair:], weights[2 * step + 1][...])
            if step == 0:
                acc[...] = total
            else:
                out_ref[...] = (acc[...] + total).astype(BF16)


def cross_first_back_body(
    order, lengths, grad_ref, own_ref, near_ref, far_ref, after_ref, gain_ref, o0, o1, o2, o3,
    query_ref, kv_ref, mixed_ref, lse_ref, w0, w1, w2, w3,
    cross_ref, two_ref, grads_ref, gain_out, dq_ref, dkv_ref, encoded_ref, acc, *, valid,
):
    local = o0.shape[0]
    step = pl.program_id(0)

    @pl.when(step == 0)
    def _():
        place = lax.broadcasted_iota(jnp.int32, own_ref.shape, 0)
        grads = jnp.where(place < lengths[order[0]], grad_ref[0].astype(F32), 0.0)
        normed_grad = own_ref[...].astype(F32) + near_ref[...].astype(F32) + far_ref[...].astype(F32)
        unit, inverse = norm_stats(after_ref[...])
        total = grads + norm_back(unit, inverse, gain_ref[3 : 4], normed_grad)
        cross_ref[...] = total
        low = total.astype(BF16)
        two_ref[...] = low
        for r, weight in enumerate((o0, o1, o2, o3)):
            mixed = dot(low, weight[...], 1, 1).astype(BF16)
            grads_ref[r // 2, :, (r % 2) * local : (r % 2 + 1) * local] = mixed
        gain_out[...] = jnp.sum(normed_grad * unit, axis=0, keepdims=True)

    def store(columns, dq):
        dq_ref[0, columns, :] = dq

    cross_back(query_ref, kv_ref, grads_ref[step], mixed_ref, lse_ref, dkv_ref, local, valid, store)
    encoded_back(dkv_ref, (w0, w1, w2, w3), encoded_ref, acc)


def cross_first_back(order, lengths, out_grad, parts, after, gains_all, packs, packs_out, query, kv, mixed, lse, valid):
    seq, width = after.shape
    frames = kv.shape[0]
    pair = query.shape[2]
    heads = pair // HEAD_DIM
    rows = whole((seq, width))
    head_rows = pl.BlockSpec((1, seq, pair), lambda i, *_: (i, 0, 0))
    both = pl.BlockSpec((frames, 2 * pair), lambda i, *_: (0, i))
    return call(
        functools.partial(cross_first_back_body, valid=valid),
        (2,),
        [pl.BlockSpec((1, seq, width), lambda i, order, lengths: (order[0], 0, 0)), rows, rows, rows, rows]
        + [whole(gains_all.shape)]
        + pack_specs(packs_out, pair // 2, 0)
        + [head_rows, both, head_rows, pl.BlockSpec((1, heads, seq), lambda i, *_: (i, 0, 0))]
        + pack_specs(packs, pair, 0),
        [
            rows,
            rows,
            whole((2, seq, pair)),
            whole((1, width)),
            pl.BlockSpec((1, pair, seq), lambda i, *_: (i, 0, 0)),
            both,
            whole((frames, width)),
        ],
        [
            shape((seq, width), F32),
            shape((seq, width)),
            shape((2, seq, pair)),
            shape((1, width), F32),
            shape((2, pair, seq), F32),
            shape((frames, 2 * width)),
            shape((frames, width)),
        ],
        "cross_first_back",
        cost(4 * frames * width * width + 120 * seq * frames * pair, 20 * frames * width, 2 * heads * seq * frames),
        prefetch=2,
        scratch=[pltpu.VMEM((frames, width), F32)],
    )(order, lengths, out_grad, *parts, after, gains_all, *packs_out, query, kv, mixed, lse, *packs)


def cross_second_back_body(
    query_ref, kv_ref, grads_ref, mixed_ref, lse_ref, dq_in, w0, w1, w2, w3,
    p0, p1, p2, p3, after_ref, gain_ref, cross_ref,
    dq_ref, dkv_ref, encoded_ref, self_ref, one_ref, h0, h1, h2, h3, gain_out, acc, *, valid,
):
    local = h0.shape[1]
    step = pl.program_id(0)

    def store(columns, dq):
        dq_ref[step, :, columns] = ((dq + dq_in[0, columns, :]) * INV_ROOT).T.astype(BF16)

    cross_back(query_ref, kv_ref, grads_ref[0], mixed_ref, lse_ref, dkv_ref, local, valid, store)
    encoded_back(dkv_ref, (w0, w1, w2, w3), encoded_ref, acc)

    @pl.when(step == 1)
    def _():
        packs = (p0, p1, p2, p3)
        normed_grad = 0.0
        for r, pack in enumerate(packs):
            normed_grad = normed_grad + dot(dq_ref[r // 2, :, (r % 2) * local : (r % 2 + 1) * local], pack[local:])
        unit, inverse = norm_stats(after_ref[...])
        total = cross_ref[...] + norm_back(unit, inverse, gain_ref[2 : 3], normed_grad)
        self_ref[...] = total
        low = total.astype(BF16)
        one_ref[...] = low
        for out, pack in zip((h0, h1, h2, h3), packs):
            out[...] = dot(low, pack[:local], 1, 1).astype(BF16)
        gain_out[...] = jnp.sum(normed_grad * unit, axis=0, keepdims=True)


def cross_second_back(query, kv, grads, mixed, lse, dq, packs_two, packs_one, after, gains_all, cross, valid):
    seq, width = after.shape
    frames = kv.shape[0]
    pair = query.shape[2]
    local = pair // 2
    heads = pair // HEAD_DIM
    rows = whole((seq, width))
    head_rows = pl.BlockSpec((1, seq, pair), lambda i: (i, 0, 0))
    both = pl.BlockSpec((frames, 2 * pair), lambda i: (0, i))
    return call(
        functools.partial(cross_second_back_body, valid=valid),
        (2,),
        [head_rows, both, head_rows, head_rows, pl.BlockSpec((1, heads, seq), lambda i: (i, 0, 0))]
        + [pl.BlockSpec((1, pair, seq), lambda i: (i, 0, 0))]
        + pack_specs(packs_two, pair, 0)
        + pack_specs(packs_one, pair, 0)
        + [rows, whole(gains_all.shape), rows],
        [whole((2, seq, pair)), both, whole((frames, width)), rows, rows]
        + [whole((seq, local))] * 4
        + [whole((1, width))],
        [
            shape((2, seq, pair)),
            shape((frames, 2 * width)),
            shape((frames, width)),
            shape((seq, width), F32),
            shape((seq, width)),
        ]
        + [shape((seq, local))] * 4
        + [shape((1, width), F32)],
        "cross_second_back",
        cost(4 * frames * width * width + 120 * seq * frames * pair, 20 * frames * width, 2 * heads * seq * frames),
        scratch=[pltpu.VMEM((frames, width), F32)],
    )(query, kv, grads, mixed, lse, dq, *packs_two, *packs_one, after, gains_all, cross)


def add_gain(gain_out, term):
    @pl.when(pl.program_id(0) == 0)
    def _():
        gain_out[...] = jnp.zeros_like(gain_out)

    gain_out[...] += term

def to_tokens_grad_body(order, token_ref, own_ref, near_ref, far_ref, self_ref, gain_ref, out_ref, gain_out):
    normed_grad = own_ref[...].astype(F32) + near_ref[...].astype(F32) + far_ref[...].astype(F32)
    unit, inverse = norm_stats(token_ref[0].astype(F32))
    out_ref[...] = (self_ref[...] + norm_back(unit, inverse, gain_ref[1 : 2], normed_grad)).astype(BF16)
    add_gain(gain_out, jnp.sum(normed_grad * unit, axis=0, keepdims=True))


def to_tokens_grad(order, tokens, own, near, far, grad_self, gains_all, scale):
    _, seq, width = tokens.shape
    tile = seq // 2
    rows = pl.BlockSpec((tile, width), lambda i, *_: (i, 0))
    return call(
        to_tokens_grad_body,
        (2,),
        [pl.BlockSpec((1, tile, width), lambda i, order: (order[0], i, 0)), rows, rows, rows, rows, whole(gains_all.shape)],
        [rows, whole((1, width))],
        [shape((seq, width)), shape((1, width), F32)],
        "norm_one_back",
        cost(0, seq * width * 14, scale=scale),
        prefetch=1,
    )(order, tokens, own, near, far, grad_self, gains_all)


def split_store(total, mine, keep_ref, give_ref, scratch, lead=()):
    scratch[...] = total
    parts, depth = keep_ref.shape[-3], keep_ref.shape[-2]
    for j in range(parts):
        at = pl.multiple_of((2 * j + mine) * depth, 8)
        keep_ref[lead + (j,)] = scratch[pl.ds(at, depth), :].astype(BF16)
        at = pl.multiple_of((2 * j + 1 - mine) * depth, 8)
        give_ref[lead + (j,)] = scratch[pl.ds(at, depth), :].astype(BF16)


def feed_weights_body(bits, *refs):
    rows, pres, lives, hiddens = refs[:4], refs[4:7], refs[7:10], refs[10:13]
    keep_ref, give_ref, scratch = refs[13:]
    three = lambda items: (items[0][0], items[0][1], items[1][0], items[2][0])
    total = 0.0
    for left, right in zip(rows, three(pres)):
        total = total + dot(left[...], right, 0, 0)
    split_store(total, bits[0], keep_ref, give_ref, scratch, (0,))
    total = 0.0
    for left, right in zip(three(lives), three(hiddens)):
        total = total + dot(left, right, 0, 0)
    split_store(total, bits[0], keep_ref, give_ref, scratch, (1,))


def feed_weights(bits, rows, pres, lives, hiddens, wide):
    seq, width = rows[0].shape
    units = pres[0].shape[2]
    tile = width // 2
    depth = width // wide
    column = lambda count: pl.BlockSpec((count, seq, tile), lambda i, *_: (0, 0, i))
    full = lambda count: whole((count, seq, units))
    out = pl.BlockSpec((2, wide // 4, depth, units), lambda i, *_: (0, i, 0, 0))
    return call(
        feed_weights_body,
        (2,),
        [pl.BlockSpec((seq, tile), lambda i, *_: (0, i))] * 4
        + [full(2), full(1), full(1), column(2), column(1), column(1), full(2), full(1), full(1)],
        [out, out],
        [shape((2, wide // 2, depth, units))] * 2,
        "feed_weight_grads",
        cost(16 * seq * width * units, 24 * seq * width),
        prefetch=1,
        scratch=[pltpu.VMEM((tile, units), F32)],
    )(bits, *rows, *pres, *lives, *hiddens)


def head_weights_body(enc0, enc1, dkv0, dkv1, two, dq_ref, grad_two, cross_mixed, keep_ref, give_ref):
    local = dq_ref.shape[2] // 2
    for r in range(4):
        out = (keep_ref, give_ref)[r % 2]
        columns = slice((r % 2) * local, (r % 2 + 1) * local)
        pair = slice(2 * r * local, 2 * (r + 1) * local)
        kv = dot(enc0[...], dkv0[:, pair], 0, 0) + dot(enc1[...], dkv1[:, pair], 0, 0)
        out[r // 2, :, : 2 * local] = kv.astype(BF16)
        query = dot(two[...], dq_ref[r // 2, :, columns], 0, 0)
        cross = dot(grad_two[...], cross_mixed[r // 2, :, columns], 0, 0)
        out[r // 2, :, 2 * local :] = jnp.concatenate((query, cross), axis=1).astype(BF16)


def head_weights(encs, dkvs, normed_two, dq, grad_two, cross_mixed, scale):
    seq, width = normed_two.shape
    tile = width // 2
    rows = pl.BlockSpec((seq, tile), lambda i: (0, i))
    out = pl.BlockSpec((2, tile, width), lambda i: (0, i, 0))
    frames = encs[0].shape[0] + encs[1].shape[0]
    return call(
        head_weights_body,
        (2,),
        [pl.BlockSpec((item.shape[0], tile), lambda i: (0, i)) for item in encs]
        + [whole(item.shape) for item in dkvs]
        + [rows, whole(dq.shape), rows, whole(cross_mixed.shape)],
        [out, out],
        [shape((2, width, width))] * 2,
        "head_weight_grads",
        cost(4 * frames * width * width + 4 * seq * width * width, 6 * frames * width, scale=scale),
    )(*encs, *dkvs, normed_two, dq, grad_two, cross_mixed)


def out_weights_body(one, m0, m1, m2, m3, keep_ref, give_ref):
    for r, mixed in enumerate((m0, m1, m2, m3)):
        (keep_ref, give_ref)[r % 2][r // 2] = dot(mixed[...], one[...], 0, 0).astype(BF16)


def out_weights(grad_one, mixes, scale):
    seq, width = grad_one.shape
    local = mixes[0].shape[1]
    return call(
        out_weights_body,
        (1,),
        [whole(item.shape) for item in (grad_one, *mixes)],
        [whole((2, local, width))] * 2,
        [shape((2, local, width))] * 2,
        "out_weight_grads",
        cost(2 * seq * width * width, 8 * seq * width, scale=scale),
    )(grad_one, *mixes)


def self_weights_body(bits, near, far, dnear, dfar, own, core, other, keep_ref, give_ref, scratch):
    totals = []
    for i in range(3):
        total = 0.0
        for c in range(2):
            total = total + dot(near[c], dnear[c, i], 0, 0) + dot(far[c], dfar[c, i], 0, 0)
        totals.append(total)
    totals.append((own[0].astype(F32) + core[0].astype(F32) + other[...].astype(F32)).T)
    split_store(jnp.concatenate(totals, axis=1), bits[0], keep_ref, give_ref, scratch)


def self_weights(bits, near, far, dnear, dfar, own, core, other, wide, scale):
    _, seq, width = near.shape
    local = dnear.shape[3]
    tile = width // 2
    depth = width // wide
    rows = pl.BlockSpec((2, seq, tile), lambda i, *_: (0, 0, i))
    turned = pl.BlockSpec((1, local, tile), lambda i, *_: (0, 0, i))
    out = pl.BlockSpec((wide // 4, depth, 4 * local), lambda i, *_: (i, 0, 0))
    return call(
        self_weights_body,
        (2,),
        [rows, rows, whole(dnear.shape), whole(dfar.shape), turned, turned]
        + [pl.BlockSpec((local, tile), lambda i, *_: (0, i))],
        [out, out],
        [shape((wide // 2, depth, 4 * local))] * 2,
        "self_weight_grads",
        cost(24 * seq * width * local, 16 * seq * width, scale=scale),
        prefetch=1,
        scratch=[pltpu.VMEM((tile, 4 * local), F32)],
    )(bits, near, far, dnear, dfar, own, core, other)


def add_low(keep, got):
    return (keep.astype(F32) + got.astype(F32)).astype(BF16)


def merge_body(bits, *refs, which, joined):
    ins, outs = refs[: 2 * len(which)], refs[2 * len(which) :]
    at = 0
    for i, bit in enumerate(which):
        keep_in, got_in = ins[2 * i], ins[2 * i + 1]
        mine = bits[bit]
        keep_out, give_out = outs if joined else outs[2 * i : 2 * i + 2]
        groups = slice(at, at + keep_in.shape[0])
        at += keep_in.shape[0] if joined else 0
        keep_out[groups, 0] = add_low(keep_in[:, mine], got_in[:, mine])
        give_out[groups, 0] = add_low(keep_in[:, 1 - mine], got_in[:, 1 - mine])


def merge(bits, which, *pairs, scale=None, joined=False):
    rows, columns = pairs[0][0].shape[2:]
    tile = rows // 2 if rows % 32 == 0 else rows
    both = [
        pl.BlockSpec((item.shape[0], 2, tile, columns), lambda i, *_: (0, 0, i, 0)) for pair in pairs for item in pair
    ]
    groups = [keep.shape[0] for keep, _ in pairs]
    total = sum(groups)
    groups = [total] if joined else groups
    return call(
        functools.partial(merge_body, which=which, joined=joined),
        (rows // tile,),
        both,
        [pl.BlockSpec((count, 1, tile, columns), lambda i, *_: (0, 0, i, 0)) for count in groups for _ in range(2)],
        [shape((count, 1, rows, columns)) for count in groups for _ in range(2)],
        "merge",
        cost(0, 12 * total * rows * columns, scale=scale),
        prefetch=1,
    )(bits, *[item for pair in pairs for item in pair])


def merge_heads_body(bits, keep_in, got_in, keep_a, give_a, keep_b, give_b):
    low, high = bits[0], bits[1]
    for j in range(keep_a.shape[0]):
        keep_a[j] = add_low(keep_in[0, 2 * j + low], got_in[0, 2 * j + low])
        give_a[j] = add_low(keep_in[0, 2 * j + 1 - low], got_in[0, 2 * j + 1 - low])
        at = 4 * (j // 2) + j % 2
        keep_b[j] = add_low(keep_in[1, at + 2 * high], got_in[1, at + 2 * high])
        give_b[j] = add_low(keep_in[1, at + 2 * (1 - high)], got_in[1, at + 2 * (1 - high)])


def merge_heads(bits, keep, got):
    _, parts, rows, columns = keep.shape
    tile = rows // 2 if rows % 32 == 0 else rows
    both = pl.BlockSpec((2, parts, tile, columns), lambda i, *_: (0, 0, i, 0))
    out = pl.BlockSpec((parts // 2, tile, columns), lambda i, *_: (0, i, 0))
    return call(
        merge_heads_body,
        (rows // tile,),
        [both, both],
        [out] * 4,
        [shape((parts // 2, rows, columns))] * 4,
        "merge_heads",
        cost(0, 12 * parts * rows * columns, scale=SHORT),
        prefetch=1,
    )(bits, keep, got)


def scatter_wide(bits, then, keep, give, which, got):
    dims = keep.shape[-2:]
    parts = lax.axis_size("wide") >> which
    lead = keep.size // (parts * dims[0] * dims[1])
    while parts > 1:
        parts //= 2
        view = (lead * parts, 2) + dims
        keep, give = merge(then(bits), (which,), (keep.reshape(view), got.reshape(view)), scale=SHORT)
        then.last = keep
        which += 1
        got = swap(give, "wide", 1 << (which - 1))
    view = (lead,) + dims
    return keep.reshape(view).astype(F32) + got.reshape(view).astype(F32)


def place_body(order, a, b, c, d, *refs, start):
    out, held, reads, writes = refs[-4:]
    blocks = (a, b, c, d)
    loads = [pltpu.make_async_copy(item, held.at[r], reads.at[r]) for r, item in enumerate(blocks)]
    for item in loads:
        item.start()
    stores = []
    for r, item in enumerate(loads):
        item.wait()
        if start is None:
            target = out.at[order[r]]
        else:
            target = out.at[:, order[r], pl.ds(start, held.shape[2])]
        stores.append(pltpu.make_async_copy(held.at[r], target, writes.at[r]))
        stores[-1].start()
    for item in stores:
        item.wait()


def place_blocks(order, blocks, dims, start=None, before=None, scale=None):
    anywhere = pl.BlockSpec(memory_space=pl.ANY)
    extra = () if before is None else (before,)
    return pl.pallas_call(
        functools.partial(place_body, start=start),
        grid_spec=pltpu.PrefetchScalarGridSpec(
            num_scalar_prefetch=1,
            grid=(1,),
            in_specs=[anywhere] * (4 + len(extra)),
            out_specs=anywhere,
            scratch_shapes=[
                pltpu.VMEM((4,) + blocks[0].shape, BF16),
                pltpu.SemaphoreType.DMA((4,)),
                pltpu.SemaphoreType.DMA((4,)),
            ],
        ),
        out_shape=shape(dims),
        input_output_aliases={5: 0} if extra else {},
        compiler_params=pltpu.CompilerParams(vmem_limit_bytes=VMEM_LIMIT),
        cost_estimate=cost(0, 16 * blocks[0].size, scale=SHORT if scale is None else scale),
        name="place_blocks",
    )(order, *blocks, *extra)


def on_device(
    tokens, lengths, memory, gains, self_qkv, self_out, cross_q, cross_kv, cross_out, fc_in, fc_out, out_grad
):
    clips, seq, width = tokens.shape
    wide = lax.axis_size("wide")
    narrow = lax.axis_size("narrow")
    me = lax.axis_index("narrow")
    place = lax.axis_index("wide")
    bits = ((place >> jnp.arange(8)) & 1).astype(jnp.int32)
    share = memory.shape[1]
    local = self_qkv.shape[2]
    depth = width // wide
    order = (me ^ jnp.arange(4)).astype(jnp.int32)
    near_order = (me ^ jnp.array([1, 0])).astype(jnp.int32)
    far_order = (me ^ jnp.array([3, 2])).astype(jnp.int32)
    then = Order()

    by_clip = memory.reshape(wide, narrow, share, width)
    first = -(-share // SPLIT) * 16
    sizes = (first, share - first)
    starts = (0, first)
    last = AUDIO - (wide - 1) * share
    valid = [(wide - 1) * size + min(max(last - start, 0), size) for start, size in zip(starts, sizes)]

    def encoder_rows(part, *named):
        block = encode(then(order, *named), by_clip, gains, starts[part], sizes[part])
        then.last = block
        block = lax.all_to_all(block, "wide", 0, 0, tiled=True)
        return block.reshape(wide * sizes[part], width)

    encoded_first = encoder_rows(0)
    self_qkv = self_qkv.transpose(0, 2, 1)
    pack_kv = cross_kv.transpose(0, 2, 1).reshape(2 * local, width)
    packs_one = gather_narrow(jnp.concatenate((self_out, then(cross_q).T)))

    normed_far, qkv_far, mixed_three, mixed_two, lse_far = self_fwd(
        then(far_order), lengths, tokens, gains, self_qkv
    )
    then.last = mixed_two
    mix_two = swap(mixed_two, "narrow", 2)
    crossing = swap(mixed_three, "narrow", 1)
    normed_near, qkv_near, mixed_one, mixed_zero, lse_near = self_fwd(
        then(near_order), lengths, tokens, gains, self_qkv
    )
    then.last = mixed_zero
    mix_three = swap(then(crossing), "narrow", 2)
    packs_kv = gather_narrow(then(pack_kv))
    mixes = [mixed_zero, swap(mixed_one, "narrow", 1), mix_two, mix_three]
    packs_one = finish(packs_one, then)
    encoded_second = encoder_rows(1, mix_two, packs_one[2])
    encoded = (encoded_first, encoded_second)
    after_self, normed_two, query = to_query(then(order), tokens, mixes, packs_one, gains)
    then.last = query
    packs_kv = finish(packs_kv, then)
    packs_out = gather_narrow(then(cross_out))
    kv_first, *before = cross_first(then(query), encoded_first, packs_kv, valid[0])
    then.last = kv_first
    packs_out = finish(packs_out, then)
    kv_second, cross_mixed, cross_lse, after_cross, normed_three = cross_second(
        query, encoded_second, packs_kv, packs_out, valid[1], before, after_self, gains
    )
    then.last = normed_three

    rows = gather_narrow(normed_three)
    hidden_a, pre_a, live_a, part_zero, feed_zero, part_one, feed_one = feed_forward(
        order[:2], lengths, rows[:2], out_grad, fc_in, fc_out
    )
    then.last = part_one
    rows = finish(rows, then)
    part_near = swap(part_one, "narrow", 1)
    feed_near = swap(feed_one, "narrow", 1)
    hidden_c, pre_c, live_c, part_three, feed_three = feed_forward(
        order[3:], lengths, rows[3:], out_grad, fc_in, fc_out
    )
    then.last = part_three
    part_cross = swap(part_three, "narrow", 1)
    feed_cross = swap(feed_three, "narrow", 1)
    hidden_b, pre_b, live_b, part_two, feed_two = feed_forward(
        then(order[2:3]), lengths, rows[2:3], out_grad, fc_in, fc_out
    )
    part_far = (part_two.astype(F32) + part_cross.astype(F32)).astype(BF16)
    then.last = part_far
    part_far = swap(part_far, "narrow", 2)
    feed_keep, feed_give = feed_weights(
        then(bits, part_near, feed_near, feed_cross),
        rows, (pre_a, pre_b, pre_c), (live_a, live_b, live_c), (hidden_a, hidden_b, hidden_c), wide,
    )
    then.last = feed_give
    feed_far = (then(feed_two).astype(F32) + feed_cross.astype(F32)).astype(BF16)
    then.last = feed_far
    feed_far = swap(then(feed_far, part_far), "narrow", 2)
    feed_got = swap(feed_give, "wide", 1)

    grad_cross, grad_two, grad_mixed, gain_three, dq, dkv_first, frames_first = cross_first_back(
        then(order), lengths, out_grad, (part_zero, part_near, part_far), after_cross, gains,
        packs_kv, packs_out, query, kv_first, cross_mixed, cross_lse, valid[0],
    )
    then.last = dkv_first

    def frames_sent(block, part):
        block = block.reshape(wide, sizes[part], width)
        return lax.all_to_all(block, "wide", 0, 0, tiled=True)

    frames_first = frames_sent(frames_first, 0)
    block_own = (
        then(after_cross) + (feed_zero.astype(F32) + feed_near.astype(F32) + feed_far.astype(F32))
    ).astype(BF16)
    then.last = block_own
    block_all = gather_narrow(block_own)
    view = (2 * (wide // 4), 2, depth, width)
    feed_keep, feed_give = merge(then(bits), (1,), (feed_keep.reshape(view), feed_got.reshape(view)))
    then.last = feed_keep
    feed_got = swap(feed_give, "wide", 2)
    dq, dkv_second, frames_second, grad_self, grad_one, head0, head1, head2, head3, gain_two = cross_second_back(
        query, kv_second, grad_mixed, cross_mixed, cross_lse, dq, packs_kv, packs_one, after_self,
        then(gains), grad_cross, valid[1],
    )
    then.last = dq
    head1, head2, head3, frames_second, feed_got, *block_all = then.join(
        head1, head2, head3, frames_second, feed_got, *block_all
    )
    feed_view = (2 * (wide // 8), 2, depth, width)
    feed_keep, feed_give = merge(
        then(bits), (2,), (feed_keep.reshape(feed_view), feed_got.reshape(feed_view)), scale=SHORT
    )
    feed_give, head1, head2, head3 = then.join(feed_give, head1, head2, head3)
    feed_got = swap(feed_give, "wide", 4)
    heads_one = swap(head1, "narrow", 1)
    heads_two = swap(head2, "narrow", 2)
    head3 = swap(head3, "narrow", 2)
    block_all = block_all + [swap(block_all[2], "narrow", 1)]

    self_keep, self_give = out_weights(then(grad_one), mixes, LONG)
    then.last = self_give
    self_got = swap(self_give, "narrow", 1)
    back_first, gain_first = memory_back(then(order), by_clip, gains, frames_first, starts[0], SHORT)
    back_first, frames_second, heads_one, heads_two, head3, feed_got = then.join(
        back_first, frames_second, heads_one, heads_two, head3, feed_got
    )
    frames_second = frames_sent(frames_second, 1)
    heads_three = swap(head3, "narrow", 1)
    back_first = gather_narrow(back_first)
    keep, give = head_weights(
        encoded, (dkv_first, dkv_second), then(normed_two), dq, grad_two, cross_mixed, LONG
    )
    give, keep, heads_three, *block_all = then.join(give, keep, heads_three, *block_all)
    got = swap(give, "narrow", 1)
    dqkv_near, part_one, part_zero = self_bwd(
        then(near_order), lengths, qkv_near, mixed_one, mixed_zero, lse_near, heads_one, head0, self_qkv, SHORT
    )
    then.last = part_one
    part_near = swap(part_one, "narrow", 1)
    dqkv_far, part_three, part_two = self_bwd(
        then(far_order), lengths, qkv_far, mixed_three, mixed_two, lse_far, heads_three, heads_two, self_qkv, SHORT
    )
    part_three, part_two, self_got, frames_second, *back_first = then.join(
        part_three, part_two, self_got, frames_second, *back_first
    )
    part_cross = swap(part_three, "narrow", 1)
    back_first = back_first + [swap(back_first[2], "narrow", 1)]
    feed_grads = scatter_wide(bits, then, feed_keep, feed_give, 3, feed_got)
    self_other = (then(self_keep)[1].astype(F32) + self_got[1].astype(F32)).astype(BF16)
    then.last = self_other
    self_other = swap(self_other, "narrow", 2)
    back_second, gain_second = memory_back(then(order), by_clip, gains, frames_second, starts[1], LONG)
    back_second, part_two, part_cross, part_near, got, *back_first = then.join(
        back_second, part_two, part_cross, part_near, got, *back_first
    )
    view = (2, wide, depth, width)
    keep_a, give_a, keep_b, give_b = merge_heads(then(bits), keep.reshape(view), got.reshape(view))
    then.last = give_a
    got_a, got_b = swap(give_a, "wide", 1), swap(give_b, "wide", 2)
    part_far = (then(part_two).astype(F32) + part_cross.astype(F32)).astype(BF16)
    then.last = part_far
    part_far = swap(part_far, "narrow", 2)
    self_keep, self_give = self_weights(
        then(bits), normed_near, normed_far, dqkv_near, dqkv_far, self_keep, self_got, self_other, wide, LONG
    )
    then.last = self_give
    self_got = swap(self_give, "wide", 1)
    tokens_own, gain_one = to_tokens_grad(
        then(order), tokens, part_zero, part_near, part_far, grad_self, gains, SHORT
    )
    then.last = tokens_own
    tokens_all = gather_narrow(tokens_own)
    gain_terms = jnp.concatenate((gain_first + gain_second, gain_one, gain_two, gain_three))
    gain_other = swap(gain_terms, "narrow", 1)
    view = (wide // 4, 2, depth, width)
    pair = lambda keep, got: (keep.reshape(view), got.reshape(view))
    keep_a, give_a, keep_b, give_b = merge(then(bits), (1, 0), pair(keep_a, got_a), pair(keep_b, got_b), scale=LONG)
    give_a, give_b, keep_a, keep_b, gain_terms, gain_other = then.join(
        give_a, give_b, keep_a, keep_b, gain_terms, gain_other
    )
    got_a, got_b = swap(give_a, "wide", 2), swap(give_b, "wide", 1)
    gain_terms = gain_terms + gain_other
    gain_other = swap(gain_terms, "narrow", 2)
    block_out = place_blocks(then(order), block_all, (clips, seq, width), scale=LONG)
    block_out, self_got, gain_other = then.join(block_out, self_got, gain_other)
    gain_terms = gain_terms + gain_other
    gain_other = swap(gain_terms, "wide", 1)
    self_keep, self_give = merge(then(bits), (1,), pair(self_keep, self_got), scale=SHORT)
    then.last = self_give
    self_got = swap(self_give, "wide", 2)
    view = (wide // 8, 2, depth, width)
    keep, give = merge(
        then(bits), (2, 2, 2), pair(keep_a, got_a), pair(keep_b, got_b), pair(self_keep, self_got), scale=SHORT, joined=True
    )
    give, keep, back_second, gain_other, gain_terms, *tokens_all = then.join(
        give, keep, back_second, gain_other, gain_terms, *tokens_all
    )
    got = swap(give, "wide", 4)
    back_second = gather_narrow(back_second)
    tokens_all = tokens_all + [swap(tokens_all[2], "narrow", 1)]
    gain_terms = gain_terms + gain_other
    gain_other = swap(gain_terms, "wide", 2)
    memory_grad = place_blocks(
        then(order), back_first, (wide, narrow, share, width), starts[0], scale=LONG
    )
    memory_grad, gain_other, gain_terms, *tokens_all = then.join(memory_grad, gain_other, gain_terms, *tokens_all)
    gain_terms = gain_terms + gain_other
    gain_other = swap(gain_terms, "wide", 4)
    tokens_grad = place_blocks(then(order), tokens_all, (clips, seq, width))
    tokens_grad, got, *back_second = then.join(tokens_grad, got, *back_second)
    back_second = back_second + [swap(back_second[2], "narrow", 1)]
    total = scatter_wide(bits, then, keep, give, 3, got)
    other = swap(total[1].astype(BF16), "narrow", 2)
    memory_grad = place_blocks(
        then(order), back_second, (wide, narrow, share, width), starts[1], memory_grad, scale=LONG
    )
    memory_grad, other, gain_other = then.join(memory_grad, other, gain_other)
    memory_grad = memory_grad.reshape(memory.shape)
    head_grads = total[0] + other.astype(F32)
    self_grads = total[2]
    gain_terms = gain_terms + gain_other
    bit = 8
    while bit < wide:
        gain_terms = gain_terms + swap(gain_terms, "wide", bit)
        bit *= 2
    gains_grad = lax.dynamic_slice_in_dim(gain_terms, place * depth, depth, 1)

    heads = lambda i: head_grads[:, i * local : (i + 1) * local]
    own = lambda i: self_grads[:, i * local : (i + 1) * local]
    return (
        block_out,
        tokens_grad,
        memory_grad,
        gains_grad,
        jnp.stack([own(i) for i in range(3)]),
        own(3).T,
        heads(2),
        jnp.stack((heads(0), heads(1))),
        heads(3).T,
        feed_grads[0],
        feed_grads[1].T,
    )


def solution(mesh):
    placed = (
        P("wide", None, None),
        P("wide"),
        P(None, "wide", None),
        P(),
        P(None, None, "narrow"),
        P("narrow", None),
        P(None, "narrow"),
        P(None, None, "narrow"),
        P("narrow", None),
        P(None, "narrow"),
        P("narrow", None),
        P("wide", None, None),
    )
    return jax.shard_map(
        on_device,
        mesh=mesh,
        in_specs=placed,
        out_specs=(
            P("wide", None, None),
            P("wide", None, None),
            P(None, "wide", None),
            P(None, "wide"),
            P(None, "wide", "narrow"),
            P("narrow", "wide"),
            P("wide", "narrow"),
            P(None, "wide", "narrow"),
            P("narrow", "wide"),
            P("wide", "narrow"),
            P("narrow", "wide"),
        ),
        check_vma=False,
    )
```

```python
import functools

import jax
import jax.numpy as jnp
from jax import lax
from jax.experimental import pallas as pl
from jax.experimental.pallas import tpu as pltpu
from jax.sharding import PartitionSpec as P

HEAD_DIM = 64
AUDIO = 1500
EPSILON = 1e-05
NEG_FILL = -1e30
INV_ROOT = HEAD_DIM**-0.5
F32 = jnp.float32
BF16 = jnp.bfloat16
VMEM_LIMIT = 56 << 20
COST_SCALE = 1.0
LONG = 50.0
SHORT = 1e-6
SPLIT = 32


def dot(left, right, left_dim=1, right_dim=0):
    return lax.dot_general(
        left, right, (((left_dim,), (right_dim,)), ((), ())), preferred_element_type=F32
    )


def call(body, grid, in_specs, out_specs, out_shape, name, estimate, prefetch=0, scratch=()):
    return pl.pallas_call(
        body,
        grid_spec=pltpu.PrefetchScalarGridSpec(
            num_scalar_prefetch=prefetch,
            grid=grid,
            in_specs=in_specs,
            out_specs=out_specs,
            scratch_shapes=list(scratch),
        ),
        out_shape=out_shape,
        compiler_params=pltpu.CompilerParams(vmem_limit_bytes=VMEM_LIMIT),
        cost_estimate=estimate,
        name=name,
    )


def shape(dims, dtype=BF16):
    return jax.ShapeDtypeStruct(dims, dtype)


def cost(flops, moved, exps=0, scale=None):
    scale = COST_SCALE if scale is None else scale
    return pl.CostEstimate(
        flops=int(flops * scale), bytes_accessed=int(moved * scale), transcendentals=int(exps * scale)
    )


def whole(shape):
    return pl.BlockSpec(shape, lambda *_: (0,) * len(shape))


def norm_stats(values):
    center = values - jnp.mean(values, axis=-1, keepdims=True)
    spread = jnp.mean(center * center, axis=-1, keepdims=True)
    inverse = lax.rsqrt(spread + EPSILON)
    return center * inverse, inverse


def norm_back(unit, inverse, gains_all, grad):
    scaled = grad * gains_all
    first = jnp.mean(scaled, axis=-1, keepdims=True)
    second = jnp.mean(scaled * unit, axis=-1, keepdims=True)
    return (scaled - first - unit * second) * inverse


def swap(values, axis, bit):
    size = lax.axis_size(axis)
    return lax.ppermute(values, axis, [(i, i ^ bit) for i in range(size)])


def gather_narrow(own):
    other = swap(own, "narrow", 2)
    return [own, swap(own, "narrow", 1), other]


def finish(blocks, then):
    return blocks + [swap(then(blocks[2]), "narrow", 1)]


class Order:
    def __init__(self):
        self.last = None

    def __call__(self, item, *named):
        named = named if self.last is None else named + (self.last,)
        if named:
            item, _ = lax.optimization_barrier((item, named))
        return item

    def join(self, *items):
        items = lax.optimization_barrier(items)
        self.last = items[0]
        return items


def encode_body(order, memory_ref, gain_ref, out_ref):
    unit, _ = norm_stats(memory_ref[:, 0].astype(F32))
    out_ref[...] = (unit * gain_ref[0 : 1]).astype(BF16)


def encode(order, memory, gains_all, start, size, scale=None):
    wide, _, _, width = memory.shape
    group = min(4, wide)
    return call(
        encode_body,
        (wide // group,),
        [
            pl.BlockSpec((group, 1, size, width), lambda i, order: (i, order[0], start // size, 0)),
            whole(gains_all.shape),
        ],
        pl.BlockSpec((group, size, width), lambda i, *_: (i, 0, 0)),
        shape((wide, size, width)),
        "encode",
        cost(0, 4 * wide * size * width, scale=scale),
        prefetch=1,
    )(order, memory, gains_all)


def memory_back_body(order, memory_ref, gain_ref, grad_ref, out_ref, gain_out):
    unit, inverse = norm_stats(memory_ref[:, 0].astype(F32))
    grad = grad_ref[...].astype(F32)
    out_ref[...] = norm_back(unit, inverse, gain_ref[0 : 1], grad).astype(BF16)

    @pl.when(pl.program_id(0) == 0)
    def _():
        gain_out[...] = jnp.zeros_like(gain_out)

    gain_out[...] += jnp.sum(jnp.sum(grad * unit, axis=0), axis=0, keepdims=True)


def memory_back(order, memory, gains_all, grad, start, scale):
    wide, _, _, width = memory.shape
    size = grad.shape[1]
    group = min(4, wide)
    rows = pl.BlockSpec((group, size, width), lambda i, *_: (i, 0, 0))
    return call(
        memory_back_body,
        (wide // group,),
        [
            pl.BlockSpec((group, 1, size, width), lambda i, order: (i, order[0], start // size, 0)),
            whole(gains_all.shape),
            rows,
        ],
        [rows, whole((1, width))],
        [shape((wide, size, width)), shape((1, width), F32)],
        "memory_back",
        cost(0, 6 * wide * size * width, scale=scale),
        prefetch=1,
    )(order, memory, gains_all, grad)


def self_fwd_body(order, lengths, token_ref, gain_ref, weight_ref, normed_ref, qkv_ref, first_ref, second_ref, lse_ref):
    seq = token_ref.shape[1]
    heads = weight_ref.shape[1] // HEAD_DIM
    step = pl.program_id(0)
    length = lengths[order[step]]
    unit, _ = norm_stats(token_ref[0].astype(F32))
    normed = (unit * gain_ref[1 : 2]).astype(BF16)
    normed_ref[0] = normed
    for i in range(3):
        qkv_ref[0, i] = dot(normed, weight_ref[i], 1, 1).astype(BF16)
    cut = 256 if seq > 256 else seq
    mixed = []
    for h in range(heads):
        columns = slice(h * HEAD_DIM, (h + 1) * HEAD_DIM)
        parts = []
        for start, stop in ((0, cut), (cut, seq)):
            if start == stop:
                continue
            queries = qkv_ref[0, 0, start:stop, columns] * jnp.asarray(INV_ROOT, BF16)
            scores = dot(qkv_ref[0, 1, :stop, columns], queries, 1, 1)
            key = lax.broadcasted_iota(jnp.int32, scores.shape, 0)
            query = lax.broadcasted_iota(jnp.int32, scores.shape, 1) + start
            scores = jnp.where((key <= query) & (key < length), scores, NEG_FILL)
            top = jnp.max(scores, axis=0, keepdims=True)
            probs = jnp.exp(scores - top)
            total = jnp.sum(probs, axis=0, keepdims=True)
            out = dot(qkv_ref[0, 2, :stop, columns], probs.astype(BF16), 0, 0) / total
            parts.append(out.T)
            lse_ref[0, h : h + 1, start:stop] = top + jnp.log(total)
        mixed.append(jnp.concatenate(parts, axis=0))
    mixed = jnp.concatenate(mixed, axis=1).astype(BF16)

    @pl.when(step == 0)
    def _():
        first_ref[...] = mixed

    @pl.when(step == 1)
    def _():
        second_ref[...] = mixed


def self_fwd(order, lengths, tokens, gains_all, weights, scale=None):
    _, seq, width = tokens.shape
    local = weights.shape[1]
    heads = local // HEAD_DIM
    return call(
        self_fwd_body,
        (2,),
        [
            pl.BlockSpec((1, seq, width), lambda i, order, lengths: (order[i], 0, 0)),
            whole(gains_all.shape),
            whole((3, local, width)),
        ],
        [
            pl.BlockSpec((1, seq, width), lambda i, *_: (i, 0, 0)),
            pl.BlockSpec((1, 3, seq, local), lambda i, *_: (i, 0, 0, 0)),
            whole((seq, local)),
            whole((seq, local)),
            pl.BlockSpec((1, heads, seq), lambda i, *_: (i, 0, 0)),
        ],
        [
            shape((2, seq, width)),
            shape((2, 3, seq, local)),
            shape((seq, local)),
            shape((seq, local)),
            shape((2, heads, seq), F32),
        ],
        "self_forward",
        cost(2 * (6 * seq * width * local + 8 * seq * seq * local), 2 * seq * width * 8, 2 * heads * seq * seq, scale=scale),
        prefetch=2,
    )(order, lengths, tokens, gains_all, weights)


def self_bwd_body(
    order, lengths, qkv_ref, mixed0_ref, mixed1_ref, lse_ref, grad0_ref, grad1_ref, weight_ref,
    dq_ref, dkv_ref, first_ref, second_ref,
):
    seq = qkv_ref.shape[2]
    local = weight_ref.shape[1]
    heads = local // HEAD_DIM
    step = pl.program_id(0)
    length = lengths[order[step]]
    grad = jnp.where(step == 0, grad0_ref[...], grad1_ref[...])
    mixed = jnp.where(step == 0, mixed0_ref[...], mixed1_ref[...])
    inner = grad.astype(F32) * mixed.astype(F32)
    totals = jnp.concatenate((lse_ref[0], jnp.zeros((8 - heads % 8, seq), F32)), axis=0).T
    cut = 256 if seq > 256 else seq
    for h in range(heads):
        columns = slice(h * HEAD_DIM, (h + 1) * HEAD_DIM)
        keys = qkv_ref[0, 1, :, columns]
        values = qkv_ref[0, 2, :, columns]
        dq_parts = []
        dk, dv = 0.0, 0.0
        for start, stop in ((0, cut), (cut, seq)):
            if start == stop:
                continue
            queries = qkv_ref[0, 0, start:stop, columns] * jnp.asarray(INV_ROOT, BF16)
            grads = grad[start:stop, columns]
            scores = dot(queries, keys[:stop], 1, 1)
            key = lax.broadcasted_iota(jnp.int32, scores.shape, 1)
            query = lax.broadcasted_iota(jnp.int32, scores.shape, 0) + start
            allowed = (key <= query) & (key < length)
            probs = jnp.exp(jnp.where(allowed, scores, NEG_FILL) - totals[start:stop, h : h + 1])
            dp = dot(grads, values[:stop], 1, 1)
            centre = jnp.sum(inner[start:stop, columns], axis=1, keepdims=True)
            ds = (probs * (dp - centre)).astype(BF16)
            dk_now = dot(queries, ds, 0, 0)
            dv_now = dot(grads, probs.astype(BF16), 0, 0)
            if stop < seq:
                pad = jnp.zeros((HEAD_DIM, seq - stop), F32)
                dk_now = jnp.concatenate((dk_now, pad), axis=1)
                dv_now = jnp.concatenate((dv_now, pad), axis=1)
            dk, dv = dk + dk_now, dv + dv_now
            dq_parts.append(dot(ds, keys[:stop]) * INV_ROOT)
        dq_ref[0, :, columns] = jnp.concatenate(dq_parts, axis=0).astype(BF16)
        dkv_ref[0, columns, :] = dk.astype(BF16)
        dkv_ref[0, local + h * HEAD_DIM : local + (h + 1) * HEAD_DIM, :] = dv.astype(BF16)
    total = dot(dq_ref[0], weight_ref[0])
    total = total + dot(dkv_ref[0, :local, :], weight_ref[1], 0, 0)
    total = (total + dot(dkv_ref[0, local:, :], weight_ref[2], 0, 0)).astype(BF16)

    @pl.when(step == 0)
    def _():
        first_ref[...] = total

    @pl.when(step == 1)
    def _():
        second_ref[...] = total


def self_bwd(order, lengths, qkv, mixed0, mixed1, lse, grad0, grad1, weights, scale):
    _, _, seq, local = qkv.shape
    width = weights.shape[2]
    heads = local // HEAD_DIM
    return call(
        self_bwd_body,
        (2,),
        [
            pl.BlockSpec((1, 3, seq, local), lambda i, *_: (i, 0, 0, 0)),
            whole((seq, local)),
            whole((seq, local)),
            pl.BlockSpec((1, heads, seq), lambda i, *_: (i, 0, 0)),
            whole((seq, local)),
            whole((seq, local)),
            whole((3, local, width)),
        ],
        [
            pl.BlockSpec((1, seq, local), lambda i, *_: (i, 0, 0)),
            pl.BlockSpec((1, 2 * local, seq), lambda i, *_: (i, 0, 0)),
            whole((seq, width)),
            whole((seq, width)),
        ],
        [shape((2, seq, local)), shape((2, 2 * local, seq)), shape((seq, width)), shape((seq, width))],
        "self_backward",
        cost(2 * (6 * seq * width * local + 20 * seq * seq * local), 2 * seq * width * 8, 2 * heads * seq * seq, scale=scale),
        prefetch=2,
    )(order, lengths, qkv, mixed0, mixed1, lse, grad0, grad1, weights)


def to_query_body(order, token_ref, m0, m1, m2, m3, p0, p1, p2, p3, gain_ref, after_ref, normed_ref, query_ref):
    local = m0.shape[1]
    rows = token_ref[0].astype(F32)
    for mixed, pack in ((m0, p0), (m1, p1), (m2, p2), (m3, p3)):
        rows = rows + dot(mixed[...], pack[:local])
    after_ref[...] = rows
    unit, _ = norm_stats(rows)
    normed = (unit * gain_ref[2 : 3]).astype(BF16)
    normed_ref[...] = normed
    for r, pack in enumerate((p0, p1, p2, p3)):
        query = dot(normed, pack[local:], 1, 1).astype(BF16)
        query_ref[r // 2, :, (r % 2) * local : (r % 2 + 1) * local] = query


def to_query(order, tokens, mixes, packs, gains_all):
    _, seq, width = tokens.shape
    local = mixes[0].shape[1]
    tile = seq // 2
    return call(
        to_query_body,
        (2,),
        [pl.BlockSpec((1, tile, width), lambda i, order: (order[0], i, 0))]
        + [pl.BlockSpec((tile, local), lambda i, *_: (i, 0))] * 4
        + [whole((2 * local, width))] * 4
        + [whole(gains_all.shape)],
        [
            pl.BlockSpec((tile, width), lambda i, *_: (i, 0)),
            pl.BlockSpec((tile, width), lambda i, *_: (i, 0)),
            pl.BlockSpec((2, tile, 2 * local), lambda i, *_: (0, i, 0)),
        ],
        [shape((seq, width), F32), shape((seq, width)), shape((2, seq, 2 * local))],
        "self_out_to_query",
        cost(4 * seq * width * width, seq * width * 12 + 4 * width * width),
        prefetch=1,
    )(order, tokens, *mixes, *packs, gains_all)


def head_places(local):
    for r in range(2):
        for h in range(local // HEAD_DIM):
            at = r * local + h * HEAD_DIM
            key = 2 * r * local + h * HEAD_DIM
            yield (
                at // HEAD_DIM,
                slice(at, at + HEAD_DIM),
                slice(key, key + HEAD_DIM),
                slice(key + local, key + local + HEAD_DIM),
            )


def cross_first_body(query_ref, encoded_ref, w0, w1, w2, w3, kv_ref, acc_ref, top_ref, total_ref, *, valid):
    make_keys_values(encoded_ref, (w0, w1, w2, w3), kv_ref)
    frames = kv_ref.shape[0]
    for head, columns, key, value in head_places(query_ref.shape[2] // 2):
        queries = query_ref[0, :, columns] * jnp.asarray(INV_ROOT, BF16)
        scores = dot(kv_ref[:, key], queries, 1, 1)
        if valid < frames:
            frame = lax.broadcasted_iota(jnp.int32, scores.shape, 0)
            scores = jnp.where(frame < valid, scores, NEG_FILL)
        top = jnp.max(scores, axis=0, keepdims=True)
        probs = jnp.exp(scores - top)
        acc_ref[0, columns, :] = dot(kv_ref[:, value], probs.astype(BF16), 0, 0)
        top_ref[0, head : head + 1, :] = top
        total_ref[0, head : head + 1, :] = jnp.sum(probs, axis=0, keepdims=True)


def make_keys_values(encoded_ref, weights, kv_ref):
    pair = weights[0].shape[0]
    for step in range(2):

        @pl.when(pl.program_id(0) == step)
        def _():
            for r in range(2):
                kv = dot(encoded_ref[...], weights[2 * step + r][...], 1, 1)
                kv_ref[:, r * pair : (r + 1) * pair] = kv.astype(BF16)


def cross_second_body(
    query_ref, encoded_ref, w0, w1, w2, w3, acc_in, top_in, total_in, after_ref, o0, o1, o2, o3, gain_ref,
    kv_ref, mixed_ref, lse_ref, next_ref, normed_ref, *, valid,
):
    make_keys_values(encoded_ref, (w0, w1, w2, w3), kv_ref)
    frames = kv_ref.shape[0]
    local = o0.shape[0]
    for head, columns, key, value in head_places(local):
        queries = query_ref[0, :, columns] * jnp.asarray(INV_ROOT, BF16)
        scores = dot(kv_ref[:, key], queries, 1, 1)
        if valid < frames:
            frame = lax.broadcasted_iota(jnp.int32, scores.shape, 0)
            scores = jnp.where(frame < valid, scores, NEG_FILL)
        before = top_in[0, head : head + 1, :]
        top = jnp.maximum(jnp.max(scores, axis=0, keepdims=True), before)
        probs = jnp.exp(scores - top)
        fade = jnp.exp(before - top)
        total = jnp.sum(probs, axis=0, keepdims=True) + total_in[0, head : head + 1, :] * fade
        out = dot(kv_ref[:, value], probs.astype(BF16), 0, 0) + acc_in[0, columns, :] * fade
        mixed_ref[0, :, columns] = (out / total).T.astype(BF16)
        lse_ref[0, head : head + 1, :] = top + jnp.log(total)
    outs = (o0, o1, o2, o3)
    for step in range(2):

        @pl.when(pl.program_id(0) == step)
        def _():
            rows = after_ref[...] if step == 0 else next_ref[...]
            for r in range(2):
                rows = rows + dot(mixed_ref[0, :, r * local : (r + 1) * local], outs[2 * step + r][...])
            next_ref[...] = rows
            if step == 1:
                unit, _ = norm_stats(rows)
                normed_ref[...] = (unit * gain_ref[3 : 4]).astype(BF16)


def pack_specs(packs, rows, index):
    width = packs[0].shape[1]
    return [pl.BlockSpec((rows, width), lambda *_: (index, 0))] * 4


def cross_first(query, encoded, packs, valid):
    _, seq, pair = query.shape
    frames, width = encoded.shape
    heads = pair // HEAD_DIM
    stats = pl.BlockSpec((1, heads, seq), lambda i: (i, 0, 0))
    return call(
        functools.partial(cross_first_body, valid=valid),
        (2,),
        [pl.BlockSpec((1, seq, pair), lambda i: (i, 0, 0)), whole((frames, width))] + pack_specs(packs, pair, 0),
        [
            pl.BlockSpec((frames, 2 * pair), lambda i: (0, i)),
            pl.BlockSpec((1, pair, seq), lambda i: (i, 0, 0)),
            stats,
            stats,
        ],
        [
            shape((frames, 4 * pair)),
            shape((2, pair, seq), F32),
            shape((2, heads, seq), F32),
            shape((2, heads, seq), F32),
        ],
        "cross_first",
        cost(4 * frames * width * width + 40 * seq * frames * pair, 8 * frames * width, 2 * heads * seq * frames),
    )(query, encoded, *packs)


def cross_second(query, encoded, packs, packs_out, valid, before, after, gains_all):
    _, seq, pair = query.shape
    frames, width = encoded.shape
    heads = pair // HEAD_DIM
    rows = pl.BlockSpec((1, seq, pair), lambda i: (i, 0, 0))
    stats = pl.BlockSpec((1, heads, seq), lambda i: (i, 0, 0))
    acc = pl.BlockSpec((1, pair, seq), lambda i: (i, 0, 0))
    return call(
        functools.partial(cross_second_body, valid=valid),
        (2,),
        [rows, whole((frames, width))]
        + pack_specs(packs, pair, 0)
        + [acc, stats, stats, whole((seq, width))]
        + pack_specs(packs_out, pair // 2, 0)
        + [whole(gains_all.shape)],
        [pl.BlockSpec((frames, 2 * pair), lambda i: (0, i)), rows, stats, whole((seq, width)), whole((seq, width))],
        [
            shape((frames, 4 * pair)),
            shape((2, seq, pair)),
            shape((2, heads, seq), F32),
            shape((seq, width), F32),
            shape((seq, width)),
        ],
        "cross_second",
        cost(4 * frames * width * width + 40 * seq * frames * pair, 10 * frames * width, 2 * heads * seq * frames),
    )(query, encoded, *packs, *before, after, *packs_out, gains_all)


def feed_body(order, lengths, *refs, count):
    row_refs, (grad_ref, in_ref, out_ref, hidden_ref, pre_ref, live_ref) = refs[:count], refs[count : count + 6]
    outs = refs[count + 6 :]
    step = pl.program_id(0)
    tile = grad_ref.shape[1]
    rows = row_refs[0][...]
    if count == 2:
        rows = jnp.where(step == 0, rows, row_refs[1][...])
    place = lax.broadcasted_iota(jnp.int32, grad_ref.shape[1:], 0) + pl.program_id(1) * tile
    grads = jnp.where(place < lengths[order[step]], grad_ref[0], jnp.zeros((), BF16))
    live_ref[0] = grads
    pre = dot(rows, in_ref[...])
    half = 0.5 * (1.0 + lax.erf(pre * (0.5**0.5)))
    hidden = (pre * half).astype(BF16)
    slope = half + pre * jnp.exp(-0.5 * pre * pre) * 0.3989422804014327
    hidden_ref[0] = hidden
    grad_pre = (dot(grads, out_ref[...], 1, 1) * slope).astype(BF16)
    pre_ref[0] = grad_pre
    part = dot(grad_pre, in_ref[...], 1, 1).astype(BF16)
    feed = dot(hidden, out_ref[...]).astype(BF16)
    for i in range(count):

        @pl.when(step == i)
        def _():
            outs[2 * i][...] = part
            outs[2 * i + 1][...] = feed


def feed_forward(order, lengths, rows, out_grad, fc_in, fc_out):
    count = len(rows)
    seq, width = rows[0].shape
    units = fc_in.shape[1]
    tiles = 2
    tile = seq // tiles
    block = lambda last: pl.BlockSpec((1, tile, last), lambda i, j, *_: (i, j, 0))
    single = [
        pl.BlockSpec((tile, width), lambda i, j, *_: (jnp.where(i == 0, j, tiles - 1), 0)),
        pl.BlockSpec((tile, width), lambda i, j, *_: (jnp.where(i == 0, 0, j), 0)),
    ]
    if count == 1:
        single = [pl.BlockSpec((tile, width), lambda i, j, *_: (j, 0))]
    return call(
        functools.partial(feed_body, count=count),
        (count, tiles),
        single
        + [
            pl.BlockSpec((1, tile, width), lambda i, j, order, lengths: (order[i], j, 0)),
            whole((width, units)),
            whole((units, width)),
        ],
        [block(units), block(units), block(width)] + [spec for spec in single for _ in range(2)],
        [shape((count, seq, units)), shape((count, seq, units)), shape((count, seq, width))]
        + [shape((seq, width))] * (2 * count),
        "feed_forward",
        cost(8 * count * seq * width * units, count * seq * width * 14, 2 * count * seq * units),
        prefetch=2,
    )(order, lengths, *rows, out_grad, fc_in, fc_out)


def add_gain(gain_out, term):
    @pl.when(pl.program_id(0) == 0)
    def _():
        gain_out[...] = jnp.zeros_like(gain_out)

    gain_out[...] += term


def cross_back(queries_ref, kv_ref, grads_ref, mixed_ref, lse_ref, dkv_ref, local, valid, store):
    frames = kv_ref.shape[0]
    inner = grads_ref.astype(F32) * mixed_ref[0].astype(F32)
    heads, seq = lse_ref.shape[1:]
    totals = jnp.concatenate((lse_ref[0], jnp.zeros((8 - heads % 8, seq), F32)), axis=0).T
    for head, columns, key, value in head_places(local):
        queries = queries_ref[0, :, columns] * jnp.asarray(INV_ROOT, BF16)
        grads = grads_ref[:, columns]
        centre = jnp.sum(inner[:, columns], axis=1, keepdims=True)
        keys = kv_ref[:, key]
        probs = jnp.exp(dot(queries, keys, 1, 1) - totals[:, head : head + 1])
        if valid < frames:
            frame = lax.broadcasted_iota(jnp.int32, probs.shape, 1)
            probs = jnp.where(frame < valid, probs, 0.0)
        dp = dot(grads, kv_ref[:, value], 1, 1)
        ds = (probs * (dp - centre)).astype(BF16)
        dkv_ref[value, :] = dot(grads, probs.astype(BF16), 0, 0).astype(BF16)
        dkv_ref[key, :] = dot(queries, ds, 0, 0).astype(BF16)
        store(columns, dot(ds, keys))


def encoded_back(dkv_ref, weights, out_ref, acc):
    pair = weights[0].shape[0]
    for step in range(2):

        @pl.when(pl.program_id(0) == step)
        def _():
            total = dot(dkv_ref[:pair, :], weights[2 * step][...], 0, 0)
            total = total + dot(dkv_ref[pair:, :], weights[2 * step + 1][...], 0, 0)
            if step == 0:
                acc[...] = total
            else:
                out_ref[...] = (acc[...] + total).astype(BF16)


def cross_first_back_body(
    order, lengths, grad_ref, own_ref, near_ref, far_ref, after_ref, gain_ref, o0, o1, o2, o3,
    query_ref, kv_ref, mixed_ref, lse_ref, w0, w1, w2, w3,
    cross_ref, two_ref, grads_ref, gain_out, dq_ref, dkv_ref, encoded_ref, acc, *, valid,
):
    local = o0.shape[0]
    step = pl.program_id(0)

    @pl.when(step == 0)
    def _():
        place = lax.broadcasted_iota(jnp.int32, own_ref.shape, 0)
        grads = jnp.where(place < lengths[order[0]], grad_ref[0].astype(F32), 0.0)
        normed_grad = own_ref[...].astype(F32) + near_ref[...].astype(F32) + far_ref[...].astype(F32)
        unit, inverse = norm_stats(after_ref[...])
        total = grads + norm_back(unit, inverse, gain_ref[3 : 4], normed_grad)
        cross_ref[...] = total
        low = total.astype(BF16)
        two_ref[...] = low
        for r, weight in enumerate((o0, o1, o2, o3)):
            mixed = dot(low, weight[...], 1, 1).astype(BF16)
            grads_ref[r // 2, :, (r % 2) * local : (r % 2 + 1) * local] = mixed
        gain_out[...] = jnp.sum(normed_grad * unit, axis=0, keepdims=True)

    def store(columns, dq):
        dq_ref[0, :, columns] = dq

    cross_back(query_ref, kv_ref, grads_ref[step], mixed_ref, lse_ref, dkv_ref, local, valid, store)
    encoded_back(dkv_ref, (w0, w1, w2, w3), encoded_ref, acc)


def cross_first_back(order, lengths, out_grad, parts, after, gains_all, packs, packs_out, query, kv, mixed, lse, valid):
    seq, width = after.shape
    frames = kv.shape[0]
    pair = query.shape[2]
    heads = pair // HEAD_DIM
    rows = whole((seq, width))
    head_rows = pl.BlockSpec((1, seq, pair), lambda i, *_: (i, 0, 0))
    both = pl.BlockSpec((frames, 2 * pair), lambda i, *_: (0, i))
    return call(
        functools.partial(cross_first_back_body, valid=valid),
        (2,),
        [pl.BlockSpec((1, seq, width), lambda i, order, lengths: (order[0], 0, 0)), rows, rows, rows, rows]
        + [whole(gains_all.shape)]
        + pack_specs(packs_out, pair // 2, 0)
        + [head_rows, both, head_rows, pl.BlockSpec((1, heads, seq), lambda i, *_: (i, 0, 0))]
        + pack_specs(packs, pair, 0),
        [
            rows,
            rows,
            whole((2, seq, pair)),
            whole((1, width)),
            head_rows,
            pl.BlockSpec((2 * pair, frames), lambda i, *_: (i, 0)),
            whole((frames, width)),
        ],
        [
            shape((seq, width), F32),
            shape((seq, width)),
            shape((2, seq, pair)),
            shape((1, width), F32),
            shape((2, seq, pair), F32),
            shape((2 * width, frames)),
            shape((frames, width)),
        ],
        "cross_first_back",
        cost(4 * frames * width * width + 120 * seq * frames * pair, 20 * frames * width, 2 * heads * seq * frames),
        prefetch=2,
        scratch=[pltpu.VMEM((frames, width), F32)],
    )(order, lengths, out_grad, *parts, after, gains_all, *packs_out, query, kv, mixed, lse, *packs)


def cross_second_back_body(
    query_ref, kv_ref, grads_ref, mixed_ref, lse_ref, dq_in, w0, w1, w2, w3,
    p0, p1, p2, p3, after_ref, gain_ref, cross_ref,
    dq_ref, dkv_ref, encoded_ref, self_ref, one_ref, h0, h1, h2, h3, gain_out, acc, *, valid,
):
    local = h0.shape[1]
    step = pl.program_id(0)

    def store(columns, dq):
        dq_ref[step, :, columns] = ((dq + dq_in[0, :, columns]) * INV_ROOT).astype(BF16)

    cross_back(query_ref, kv_ref, grads_ref[0], mixed_ref, lse_ref, dkv_ref, local, valid, store)
    encoded_back(dkv_ref, (w0, w1, w2, w3), encoded_ref, acc)

    @pl.when(step == 1)
    def _():
        packs = (p0, p1, p2, p3)
        normed_grad = 0.0
        for r, pack in enumerate(packs):
            normed_grad = normed_grad + dot(dq_ref[r // 2, :, (r % 2) * local : (r % 2 + 1) * local], pack[local:])
        unit, inverse = norm_stats(after_ref[...])
        total = cross_ref[...] + norm_back(unit, inverse, gain_ref[2 : 3], normed_grad)
        self_ref[...] = total
        low = total.astype(BF16)
        one_ref[...] = low
        for out, pack in zip((h0, h1, h2, h3), packs):
            out[...] = dot(low, pack[:local], 1, 1).astype(BF16)
        gain_out[...] = jnp.sum(normed_grad * unit, axis=0, keepdims=True)


def cross_second_back(query, kv, grads, mixed, lse, dq, packs_two, packs_one, after, gains_all, cross, valid):
    seq, width = after.shape
    frames = kv.shape[0]
    pair = query.shape[2]
    local = pair // 2
    heads = pair // HEAD_DIM
    rows = whole((seq, width))
    head_rows = pl.BlockSpec((1, seq, pair), lambda i: (i, 0, 0))
    both = pl.BlockSpec((frames, 2 * pair), lambda i: (0, i))
    return call(
        functools.partial(cross_second_back_body, valid=valid),
        (2,),
        [head_rows, both, head_rows, head_rows, pl.BlockSpec((1, heads, seq), lambda i: (i, 0, 0))]
        + [head_rows]
        + pack_specs(packs_two, pair, 0)
        + pack_specs(packs_one, pair, 0)
        + [rows, whole(gains_all.shape), rows],
        [whole((2, seq, pair)), pl.BlockSpec((2 * pair, frames), lambda i: (i, 0)), whole((frames, width)), rows, rows]
        + [whole((seq, local))] * 4
        + [whole((1, width))],
        [
            shape((2, seq, pair)),
            shape((2 * width, frames)),
            shape((frames, width)),
            shape((seq, width), F32),
            shape((seq, width)),
        ]
        + [shape((seq, local))] * 4
        + [shape((1, width), F32)],
        "cross_second_back",
        cost(4 * frames * width * width + 120 * seq * frames * pair, 20 * frames * width, 2 * heads * seq * frames),
        scratch=[pltpu.VMEM((frames, width), F32)],
    )(query, kv, grads, mixed, lse, dq, *packs_two, *packs_one, after, gains_all, cross)


def add_gain(gain_out, term):
    @pl.when(pl.program_id(0) == 0)
    def _():
        gain_out[...] = jnp.zeros_like(gain_out)

    gain_out[...] += term

def to_tokens_grad_body(order, token_ref, own_ref, near_ref, far_ref, self_ref, gain_ref, out_ref, gain_out):
    normed_grad = own_ref[...].astype(F32) + near_ref[...].astype(F32) + far_ref[...].astype(F32)
    unit, inverse = norm_stats(token_ref[0].astype(F32))
    out_ref[...] = (self_ref[...] + norm_back(unit, inverse, gain_ref[1 : 2], normed_grad)).astype(BF16)
    add_gain(gain_out, jnp.sum(normed_grad * unit, axis=0, keepdims=True))


def to_tokens_grad(order, tokens, own, near, far, grad_self, gains_all, scale):
    _, seq, width = tokens.shape
    tile = seq // 2
    rows = pl.BlockSpec((tile, width), lambda i, *_: (i, 0))
    return call(
        to_tokens_grad_body,
        (2,),
        [pl.BlockSpec((1, tile, width), lambda i, order: (order[0], i, 0)), rows, rows, rows, rows, whole(gains_all.shape)],
        [rows, whole((1, width))],
        [shape((seq, width)), shape((1, width), F32)],
        "norm_one_back",
        cost(0, seq * width * 14, scale=scale),
        prefetch=1,
    )(order, tokens, own, near, far, grad_self, gains_all)


def split_store(total, mine, keep_ref, give_ref, scratch, lead=()):
    scratch[...] = total
    parts, depth = keep_ref.shape[-3], keep_ref.shape[-2]
    for j in range(parts):
        at = pl.multiple_of((2 * j + mine) * depth, 8)
        keep_ref[lead + (j,)] = scratch[pl.ds(at, depth), :].astype(BF16)
        at = pl.multiple_of((2 * j + 1 - mine) * depth, 8)
        give_ref[lead + (j,)] = scratch[pl.ds(at, depth), :].astype(BF16)


def feed_weights_body(bits, *refs):
    rows, pres, lives, hiddens = refs[:4], refs[4:7], refs[7:10], refs[10:13]
    keep_ref, give_ref, scratch = refs[13:]
    three = lambda items: (items[0][0], items[0][1], items[1][0], items[2][0])
    total = 0.0
    for left, right in zip(rows, three(pres)):
        total = total + dot(left[...], right, 0, 0)
    split_store(total, bits[0], keep_ref, give_ref, scratch, (0,))
    total = 0.0
    for left, right in zip(three(lives), three(hiddens)):
        total = total + dot(left, right, 0, 0)
    split_store(total, bits[0], keep_ref, give_ref, scratch, (1,))


def feed_weights(bits, rows, pres, lives, hiddens, wide):
    seq, width = rows[0].shape
    units = pres[0].shape[2]
    tile = width // 2
    depth = width // wide
    column = lambda count: pl.BlockSpec((count, seq, tile), lambda i, *_: (0, 0, i))
    full = lambda count: whole((count, seq, units))
    out = pl.BlockSpec((2, wide // 4, depth, units), lambda i, *_: (0, i, 0, 0))
    return call(
        feed_weights_body,
        (2,),
        [pl.BlockSpec((seq, tile), lambda i, *_: (0, i))] * 4
        + [full(2), full(1), full(1), column(2), column(1), column(1), full(2), full(1), full(1)],
        [out, out],
        [shape((2, wide // 2, depth, units))] * 2,
        "feed_weight_grads",
        cost(16 * seq * width * units, 24 * seq * width),
        prefetch=1,
        scratch=[pltpu.VMEM((tile, units), F32)],
    )(bits, *rows, *pres, *lives, *hiddens)


def head_weights_body(enc0, enc1, dkv0, dkv1, two, grad_two, dq_ref, cross_mixed, keep_ref, give_ref):
    local = dq_ref.shape[2] // 2
    for r, out in enumerate((keep_ref, give_ref)):
        columns = slice(r * local, (r + 1) * local)
        pair = slice(2 * r * local, 2 * (r + 1) * local)
        kv = dot(dkv0[pair, :], enc0[...]) + dot(dkv1[pair, :], enc1[...])
        out[0, :, : 2 * local] = kv.T.astype(BF16)
        query = dot(two[...], dq_ref[0, :, columns], 0, 0)
        cross = dot(grad_two[...], cross_mixed[0, :, columns], 0, 0)
        out[0, :, 2 * local :] = jnp.concatenate((query, cross), axis=1).astype(BF16)


def head_weights(encs, dkvs, normed_two, dq, grad_two, cross_mixed, scale):
    seq, width = normed_two.shape
    heads = pl.BlockSpec((1, seq, width // 2), lambda i: (i, 0, 0))
    out = pl.BlockSpec((1, width, width), lambda i: (i, 0, 0))
    frames = encs[0].shape[0] + encs[1].shape[0]
    return call(
        head_weights_body,
        (2,),
        [whole(item.shape) for item in encs]
        + [pl.BlockSpec((width, item.shape[1]), lambda i: (i, 0)) for item in dkvs]
        + [whole((seq, width))] * 2
        + [heads] * 2,
        [out, out],
        [shape((2, width, width))] * 2,
        "head_weight_grads",
        cost(4 * frames * width * width + 4 * seq * width * width, 6 * frames * width, scale=scale),
    )(*encs, *dkvs, normed_two, grad_two, dq, cross_mixed)


def out_weights_body(one, m0, m1, m2, m3, keep_ref, give_ref):
    for r, mixed in enumerate((m0, m1, m2, m3)):
        (keep_ref, give_ref)[r % 2][r // 2] = dot(mixed[...], one[...], 0, 0).astype(BF16)


def out_weights(grad_one, mixes, scale):
    seq, width = grad_one.shape
    local = mixes[0].shape[1]
    return call(
        out_weights_body,
        (1,),
        [whole(item.shape) for item in (grad_one, *mixes)],
        [whole((2, local, width))] * 2,
        [shape((2, local, width))] * 2,
        "out_weight_grads",
        cost(2 * seq * width * width, 8 * seq * width, scale=scale),
    )(grad_one, *mixes)


def self_weights_body(bits, near, far, dq_near, dkv_near, dq_far, dkv_far, own, core, other, keep_ref, give_ref, scratch):
    local = dq_near.shape[2]
    totals = [0.0, 0.0, 0.0]
    for rows, dq, dkv in ((near, dq_near, dkv_near), (far, dq_far, dkv_far)):
        for c in range(2):
            totals[0] = totals[0] + dot(rows[c], dq[c], 0, 0)
            totals[1] = totals[1] + dot(rows[c], dkv[c, :local, :], 0, 1)
            totals[2] = totals[2] + dot(rows[c], dkv[c, local:, :], 0, 1)
    totals.append((own[0].astype(F32) + core[0].astype(F32) + other[...].astype(F32)).T)
    split_store(jnp.concatenate(totals, axis=1), bits[0], keep_ref, give_ref, scratch)


def self_weights(bits, near, far, dq_near, dkv_near, dq_far, dkv_far, own, core, other, wide, scale):
    _, seq, width = near.shape
    local = dq_near.shape[2]
    tile = width // 2
    depth = width // wide
    rows = pl.BlockSpec((2, seq, tile), lambda i, *_: (0, 0, i))
    turned = pl.BlockSpec((1, local, tile), lambda i, *_: (0, 0, i))
    out = pl.BlockSpec((wide // 4, depth, 4 * local), lambda i, *_: (i, 0, 0))
    return call(
        self_weights_body,
        (2,),
        [rows, rows] + [whole(item.shape) for item in (dq_near, dkv_near, dq_far, dkv_far)] + [turned, turned]
        + [pl.BlockSpec((local, tile), lambda i, *_: (0, i))],
        [out, out],
        [shape((wide // 2, depth, 4 * local))] * 2,
        "self_weight_grads",
        cost(24 * seq * width * local, 16 * seq * width, scale=scale),
        prefetch=1,
        scratch=[pltpu.VMEM((tile, 4 * local), F32)],
    )(bits, near, far, dq_near, dkv_near, dq_far, dkv_far, own, core, other)


def add_low(keep, got):
    return (keep.astype(F32) + got.astype(F32)).astype(BF16)


def merge_body(bits, *refs, which, joined):
    ins, outs = refs[: 2 * len(which)], refs[2 * len(which) :]
    at = 0
    for i, bit in enumerate(which):
        keep_in, got_in = ins[2 * i], ins[2 * i + 1]
        mine = bits[bit]
        keep_out, give_out = outs if joined else outs[2 * i : 2 * i + 2]
        groups = slice(at, at + keep_in.shape[0])
        at += keep_in.shape[0] if joined else 0
        keep_out[groups, 0] = add_low(keep_in[:, mine], got_in[:, mine])
        give_out[groups, 0] = add_low(keep_in[:, 1 - mine], got_in[:, 1 - mine])


def merge(bits, which, *pairs, scale=None, joined=False):
    rows, columns = pairs[0][0].shape[2:]
    tile = rows // 2 if rows % 32 == 0 else rows
    both = [
        pl.BlockSpec((item.shape[0], 2, tile, columns), lambda i, *_: (0, 0, i, 0)) for pair in pairs for item in pair
    ]
    groups = [keep.shape[0] for keep, _ in pairs]
    total = sum(groups)
    groups = [total] if joined else groups
    return call(
        functools.partial(merge_body, which=which, joined=joined),
        (rows // tile,),
        both,
        [pl.BlockSpec((count, 1, tile, columns), lambda i, *_: (0, 0, i, 0)) for count in groups for _ in range(2)],
        [shape((count, 1, rows, columns)) for count in groups for _ in range(2)],
        "merge",
        cost(0, 12 * total * rows * columns, scale=scale),
        prefetch=1,
    )(bits, *[item for pair in pairs for item in pair])


def merge_heads_body(bits, keep_in, got_in, keep_a, give_a, keep_b, give_b):
    low, high = bits[0], bits[1]
    for j in range(keep_a.shape[0]):
        keep_a[j] = add_low(keep_in[0, 2 * j + low], got_in[0, 2 * j + low])
        give_a[j] = add_low(keep_in[0, 2 * j + 1 - low], got_in[0, 2 * j + 1 - low])
        at = 4 * (j // 2) + j % 2
        keep_b[j] = add_low(keep_in[1, at + 2 * high], got_in[1, at + 2 * high])
        give_b[j] = add_low(keep_in[1, at + 2 * (1 - high)], got_in[1, at + 2 * (1 - high)])


def merge_heads(bits, keep, got):
    _, parts, rows, columns = keep.shape
    tile = rows // 2 if rows % 32 == 0 else rows
    both = pl.BlockSpec((2, parts, tile, columns), lambda i, *_: (0, 0, i, 0))
    out = pl.BlockSpec((parts // 2, tile, columns), lambda i, *_: (0, i, 0))
    return call(
        merge_heads_body,
        (rows // tile,),
        [both, both],
        [out] * 4,
        [shape((parts // 2, rows, columns))] * 4,
        "merge_heads",
        cost(0, 12 * parts * rows * columns, scale=SHORT),
        prefetch=1,
    )(bits, keep, got)


def scatter_wide(bits, then, keep, give, which, got):
    dims = keep.shape[-2:]
    parts = lax.axis_size("wide") >> which
    lead = keep.size // (parts * dims[0] * dims[1])
    while parts > 1:
        parts //= 2
        view = (lead * parts, 2) + dims
        keep, give = merge(then(bits), (which,), (keep.reshape(view), got.reshape(view)), scale=SHORT)
        then.last = keep
        which += 1
        got = swap(give, "wide", 1 << (which - 1))
    return keep.reshape((lead,) + dims), got.reshape((lead,) + dims)


def finish_self_body(keep_ref, got_ref, give_ref, heads_ref, qkv_ref, out_ref):
    local = out_ref.shape[0]
    heads_ref[...] = keep_ref[0].astype(F32) + got_ref[0].astype(F32)
    give_ref[...] = (keep_ref[1].astype(F32) + got_ref[1].astype(F32)).astype(BF16)
    own = keep_ref[2].astype(F32) + got_ref[2].astype(F32)
    for i in range(3):
        qkv_ref[i] = own[:, i * local : (i + 1) * local]
    out_ref[...] = own[:, 3 * local :].T


def finish_self(keep, got):
    _, depth, width = keep.shape
    local = width // 4
    dims = [(depth, width), (depth, width), (3, depth, local), (local, depth)]
    return call(
        finish_self_body,
        (1,),
        [whole(keep.shape)] * 2,
        [whole(item) for item in dims],
        [shape(dims[0])] + [shape(item, F32) for item in dims[1:]],
        "finish_self",
        cost(0, 12 * keep.size, scale=SHORT),
    )(keep, got)


def finish_heads_body(own_ref, other_ref, kv_ref, query_ref, out_ref):
    local = out_ref.shape[0]
    total = own_ref[...] + other_ref[...].astype(F32)
    for i in range(2):
        kv_ref[i] = total[:, i * local : (i + 1) * local]
    query_ref[...] = total[:, 2 * local : 3 * local]
    out_ref[...] = total[:, 3 * local :].T


def finish_heads(own, other):
    depth, width = own.shape
    local = width // 4
    dims = [(2, depth, local), (depth, local), (local, depth)]
    return call(
        finish_heads_body,
        (1,),
        [whole(own.shape)] * 2,
        [whole(item) for item in dims],
        [shape(item, F32) for item in dims],
        "finish_heads",
        cost(0, 12 * own.size, scale=SHORT),
    )(own, other)


def place_body(order, a, b, c, d, *refs, start):
    out, held, reads, writes = refs[-4:]
    blocks = (a, b, c, d)
    loads = [pltpu.make_async_copy(item, held.at[r], reads.at[r]) for r, item in enumerate(blocks)]
    for item in loads:
        item.start()
    stores = []
    for r, item in enumerate(loads):
        item.wait()
        if start is None:
            target = out.at[order[r]]
        else:
            target = out.at[:, order[r], pl.ds(start, held.shape[2])]
        stores.append(pltpu.make_async_copy(held.at[r], target, writes.at[r]))
        stores[-1].start()
    for item in stores:
        item.wait()


def place_blocks(order, blocks, dims, start=None, before=None, scale=None):
    anywhere = pl.BlockSpec(memory_space=pl.ANY)
    extra = () if before is None else (before,)
    return pl.pallas_call(
        functools.partial(place_body, start=start),
        grid_spec=pltpu.PrefetchScalarGridSpec(
            num_scalar_prefetch=1,
            grid=(1,),
            in_specs=[anywhere] * (4 + len(extra)),
            out_specs=anywhere,
            scratch_shapes=[
                pltpu.VMEM((4,) + blocks[0].shape, BF16),
                pltpu.SemaphoreType.DMA((4,)),
                pltpu.SemaphoreType.DMA((4,)),
            ],
        ),
        out_shape=shape(dims),
        input_output_aliases={5: 0} if extra else {},
        compiler_params=pltpu.CompilerParams(vmem_limit_bytes=VMEM_LIMIT),
        cost_estimate=cost(0, 16 * blocks[0].size, scale=SHORT if scale is None else scale),
        name="place_blocks",
    )(order, *blocks, *extra)


def on_device(
    tokens, lengths, memory, gains, self_qkv, self_out, cross_q, cross_kv, cross_out, fc_in, fc_out, out_grad
):
    clips, seq, width = tokens.shape
    wide = lax.axis_size("wide")
    narrow = lax.axis_size("narrow")
    me = lax.axis_index("narrow")
    place = lax.axis_index("wide")
    bits = ((place >> jnp.arange(8)) & 1).astype(jnp.int32)
    share = memory.shape[1]
    local = self_qkv.shape[2]
    depth = width // wide
    order = (me ^ jnp.arange(4)).astype(jnp.int32)
    near_order = (me ^ jnp.array([1, 0])).astype(jnp.int32)
    far_order = (me ^ jnp.array([3, 2])).astype(jnp.int32)
    then = Order()

    by_clip = memory.reshape(wide, narrow, share, width)
    first = -(-share // SPLIT) * 16
    sizes = (first, share - first)
    starts = (0, first)
    last = AUDIO - (wide - 1) * share
    valid = [(wide - 1) * size + min(max(last - start, 0), size) for start, size in zip(starts, sizes)]

    def encoder_rows(part, *arrived):
        block = encode(then(order), by_clip, gains, starts[part], sizes[part], LONG if part else None)
        block, *arrived = then.join(block, *arrived)
        block = lax.all_to_all(block, "wide", 0, 0, tiled=True)
        return block.reshape(wide * sizes[part], width), *arrived

    (encoded_first,) = encoder_rows(0)
    self_qkv = self_qkv.transpose(0, 2, 1)
    pack_kv = cross_kv.transpose(0, 2, 1).reshape(2 * local, width)
    packs_one = gather_narrow(jnp.concatenate((self_out, then(cross_q).T)))

    normed_far, qkv_far, mixed_three, mixed_two, lse_far = self_fwd(
        then(far_order), lengths, tokens, gains, self_qkv
    )
    then.last = mixed_two
    mix_two = swap(mixed_two, "narrow", 2)
    crossing = swap(mixed_three, "narrow", 1)
    normed_near, qkv_near, mixed_one, mixed_zero, lse_near = self_fwd(
        then(near_order), lengths, tokens, gains, self_qkv, LONG
    )
    mixed_one, mixed_zero, mix_two, crossing, *packs_one = then.join(
        mixed_one, mixed_zero, mix_two, crossing, *packs_one
    )
    mix_one, mix_three = swap(mixed_one, "narrow", 1), swap(crossing, "narrow", 2)
    packs_one = packs_one + [swap(packs_one[2], "narrow", 1)]
    encoded_second, mix_one, mix_three, *packs_one = encoder_rows(1, mix_one, mix_three, *packs_one)
    encoded = (encoded_first, encoded_second)
    packs_kv = gather_narrow(then(pack_kv))
    mixes = [mixed_zero, mix_one, mix_two, mix_three]
    after_self, normed_two, query = to_query(then(order), tokens, mixes, packs_one, gains)
    query, *packs_kv = then.join(query, *packs_kv)
    packs_kv = packs_kv + [swap(packs_kv[2], "narrow", 1)]
    packs_out = gather_narrow(then(cross_out))
    kv_first, *before = cross_first(then(query), encoded_first, packs_kv, valid[0])
    then.last = kv_first
    packs_out = finish(packs_out, then)
    kv_second, cross_mixed, cross_lse, after_cross, normed_three = cross_second(
        query, encoded_second, packs_kv, packs_out, valid[1], before, after_self, gains
    )
    then.last = normed_three

    rows = gather_narrow(normed_three)
    hidden_a, pre_a, live_a, part_zero, feed_zero, part_one, feed_one = feed_forward(
        order[:2], lengths, rows[:2], out_grad, fc_in, fc_out
    )
    then.last = part_one
    rows = finish(rows, then)
    part_near = swap(part_one, "narrow", 1)
    feed_near = swap(feed_one, "narrow", 1)
    hidden_c, pre_c, live_c, part_three, feed_three = feed_forward(
        order[3:], lengths, rows[3:], out_grad, fc_in, fc_out
    )
    then.last = part_three
    part_cross = swap(part_three, "narrow", 1)
    feed_cross = swap(feed_three, "narrow", 1)
    hidden_b, pre_b, live_b, part_two, feed_two = feed_forward(
        then(order[2:3]), lengths, rows[2:3], out_grad, fc_in, fc_out
    )
    part_far = (part_two.astype(F32) + part_cross.astype(F32)).astype(BF16)
    then.last = part_far
    part_far = swap(part_far, "narrow", 2)
    feed_keep, feed_give = feed_weights(
        then(bits, part_near, feed_near, feed_cross),
        rows, (pre_a, pre_b, pre_c), (live_a, live_b, live_c), (hidden_a, hidden_b, hidden_c), wide,
    )
    then.last = feed_give
    feed_far = (then(feed_two).astype(F32) + feed_cross.astype(F32)).astype(BF16)
    then.last = feed_far
    feed_far = swap(then(feed_far, part_far), "narrow", 2)
    feed_got = swap(feed_give, "wide", 1)

    grad_cross, grad_two, grad_mixed, gain_three, dq, dkv_first, frames_first = cross_first_back(
        then(order), lengths, out_grad, (part_zero, part_near, part_far), after_cross, gains,
        packs_kv, packs_out, query, kv_first, cross_mixed, cross_lse, valid[0],
    )
    then.last = dkv_first

    def frames_sent(block, part):
        block = block.reshape(wide, sizes[part], width)
        return lax.all_to_all(block, "wide", 0, 0, tiled=True)

    frames_first = frames_sent(frames_first, 0)
    block_own = (
        then(after_cross) + (feed_zero.astype(F32) + feed_near.astype(F32) + feed_far.astype(F32))
    ).astype(BF16)
    then.last = block_own
    block_all = gather_narrow(block_own)
    view = (2 * (wide // 4), 2, depth, width)
    feed_keep, feed_give = merge(then(bits), (1,), (feed_keep.reshape(view), feed_got.reshape(view)))
    then.last = feed_keep
    feed_got = swap(feed_give, "wide", 2)
    dq, dkv_second, frames_second, grad_self, grad_one, head0, head1, head2, head3, gain_two = cross_second_back(
        query, kv_second, grad_mixed, cross_mixed, cross_lse, dq, packs_kv, packs_one, after_self,
        then(gains), grad_cross, valid[1],
    )
    then.last = dq
    head1, head2, head3, frames_second, feed_got, *block_all = then.join(
        head1, head2, head3, frames_second, feed_got, *block_all
    )
    feed_view = (2 * (wide // 8), 2, depth, width)
    feed_keep, feed_give = merge(
        then(bits), (2,), (feed_keep.reshape(feed_view), feed_got.reshape(feed_view)), scale=SHORT
    )
    feed_give, head1, head2, head3 = then.join(feed_give, head1, head2, head3)
    feed_got = swap(feed_give, "wide", 4)
    heads_one = swap(head1, "narrow", 1)
    heads_two = swap(head2, "narrow", 2)
    head3 = swap(head3, "narrow", 2)
    block_all = block_all + [swap(block_all[2], "narrow", 1)]

    self_keep, self_give = out_weights(then(grad_one), mixes, LONG)
    then.last = self_give
    self_got = swap(self_give, "narrow", 1)
    back_first, gain_first = memory_back(then(order), by_clip, gains, frames_first, starts[0], SHORT)
    back_first, frames_second, heads_one, heads_two, head3, feed_got = then.join(
        back_first, frames_second, heads_one, heads_two, head3, feed_got
    )
    frames_second = frames_sent(frames_second, 1)
    heads_three = swap(head3, "narrow", 1)
    back_first = gather_narrow(back_first)
    keep, give = head_weights(
        encoded, (dkv_first, dkv_second), then(normed_two), dq, grad_two, cross_mixed, LONG
    )
    give, keep, heads_three, *block_all = then.join(give, keep, heads_three, *block_all)
    got = swap(give, "narrow", 1)
    *dqkv_near, part_one, part_zero = self_bwd(
        then(near_order), lengths, qkv_near, mixed_one, mixed_zero, lse_near, heads_one, head0, self_qkv, SHORT
    )
    then.last = part_one
    part_near = swap(part_one, "narrow", 1)
    *dqkv_far, part_three, part_two = self_bwd(
        then(far_order), lengths, qkv_far, mixed_three, mixed_two, lse_far, heads_three, heads_two, self_qkv, SHORT
    )
    part_three, part_two, self_got, frames_second, *back_first = then.join(
        part_three, part_two, self_got, frames_second, *back_first
    )
    part_cross = swap(part_three, "narrow", 1)
    back_first = back_first + [swap(back_first[2], "narrow", 1)]
    feed_keep, feed_got = scatter_wide(bits, then, feed_keep, feed_give, 3, feed_got)
    feed_grads = feed_keep.astype(F32) + feed_got.astype(F32)
    self_other = (then(self_keep)[1].astype(F32) + self_got[1].astype(F32)).astype(BF16)
    then.last = self_other
    self_other = swap(self_other, "narrow", 2)
    back_second, gain_second = memory_back(then(order), by_clip, gains, frames_second, starts[1], LONG)
    back_second, part_two, part_cross, part_near, got, *back_first = then.join(
        back_second, part_two, part_cross, part_near, got, *back_first
    )
    view = (2, wide, depth, width)
    keep_a, give_a, keep_b, give_b = merge_heads(then(bits), keep.reshape(view), got.reshape(view))
    then.last = give_a
    got_a, got_b = swap(give_a, "wide", 1), swap(give_b, "wide", 2)
    part_far = (then(part_two).astype(F32) + part_cross.astype(F32)).astype(BF16)
    then.last = part_far
    part_far = swap(part_far, "narrow", 2)
    self_keep, self_give = self_weights(
        then(bits), normed_near, normed_far, *dqkv_near, *dqkv_far, self_keep, self_got, self_other, wide, LONG
    )
    then.last = self_give
    self_got = swap(self_give, "wide", 1)
    view = (wide // 4, 2, depth, width)
    pair = lambda keep, got: (keep.reshape(view), got.reshape(view))
    keep_a, give_a, keep_b, give_b = merge(then(bits), (1, 0), pair(keep_a, got_a), pair(keep_b, got_b), scale=SHORT)
    then.last = give_a
    got_a, got_b = swap(give_a, "wide", 2), swap(give_b, "wide", 1)
    tokens_own, gain_one = to_tokens_grad(
        then(order), tokens, part_zero, part_near, part_far, grad_self, gains, LONG
    )
    then.last = tokens_own
    tokens_all = gather_narrow(tokens_own)
    gain_terms = jnp.concatenate((gain_first + gain_second, gain_one, gain_two, gain_three))
    gain_other = swap(gain_terms, "wide", 1)
    block_out = place_blocks(then(order), block_all, (clips, seq, width), scale=LONG)
    block_out, self_got, gain_other, gain_terms = then.join(block_out, self_got, gain_other, gain_terms)
    gain_terms = gain_terms + gain_other
    gain_other = swap(gain_terms, "wide", 2)
    self_keep, self_give = merge(then(bits), (1,), pair(self_keep, self_got), scale=SHORT)
    then.last = self_give
    self_got = swap(self_give, "wide", 2)
    view = (wide // 8, 2, depth, width)
    keep, give = merge(
        then(bits), (2, 2, 2), pair(keep_a, got_a), pair(keep_b, got_b), pair(self_keep, self_got), scale=SHORT, joined=True
    )
    give, keep, back_second, gain_other, gain_terms, *tokens_all = then.join(
        give, keep, back_second, gain_other, gain_terms, *tokens_all
    )
    got = swap(give, "wide", 4)
    back_second = gather_narrow(back_second)
    tokens_all = tokens_all + [swap(tokens_all[2], "narrow", 1)]
    gain_terms = gain_terms + gain_other
    gain_other = swap(gain_terms, "wide", 4)
    memory_grad = place_blocks(
        then(order), back_first, (wide, narrow, share, width), starts[0], scale=LONG
    )
    memory_grad, gain_other, gain_terms, *tokens_all = then.join(memory_grad, gain_other, gain_terms, *tokens_all)
    gain_terms = gain_terms + gain_other
    bit = 8
    while bit < wide:
        gain_terms = gain_terms + swap(gain_terms, "wide", bit)
        bit *= 2
    gain_terms = lax.dynamic_slice_in_dim(gain_terms, place * depth, depth, 1)
    gain_other = swap(gain_terms, "narrow", 1)
    tokens_grad = place_blocks(then(order), tokens_all, (clips, seq, width))
    tokens_grad, got, gain_other, gain_terms, *back_second = then.join(
        tokens_grad, got, gain_other, gain_terms, *back_second
    )
    back_second = back_second + [swap(back_second[2], "narrow", 1)]
    gain_terms = gain_terms + gain_other
    gain_other = swap(gain_terms, "narrow", 2)
    keep, got = scatter_wide(bits, then, keep, give, 3, got)
    give, head_grads, qkv_grad, self_out_grad = finish_self(keep, then(got))
    then.last = give
    other = swap(give, "narrow", 2)
    memory_grad = place_blocks(
        then(order), back_second, (wide, narrow, share, width), starts[1], memory_grad, scale=LONG
    )
    memory_grad, other, gain_other, gain_terms = then.join(memory_grad, other, gain_other, gain_terms)
    kv_grad, query_grad, cross_out_grad = finish_heads(head_grads, other)
    return (
        block_out,
        tokens_grad,
        memory_grad.reshape(memory.shape),
        gain_terms + gain_other,
        qkv_grad,
        self_out_grad,
        query_grad,
        kv_grad,
        cross_out_grad,
        feed_grads[0],
        feed_grads[1].T,
    )


def solution(mesh):
    placed = (
        P("wide", None, None),
        P("wide"),
        P(None, "wide", None),
        P(),
        P(None, None, "narrow"),
        P("narrow", None),
        P(None, "narrow"),
        P(None, None, "narrow"),
        P("narrow", None),
        P(None, "narrow"),
        P("narrow", None),
        P("wide", None, None),
    )
    return jax.shard_map(
        on_device,
        mesh=mesh,
        in_specs=placed,
        out_specs=(
            P("wide", None, None),
            P("wide", None, None),
            P(None, "wide", None),
            P(None, "wide"),
            P(None, "wide", "narrow"),
            P("narrow", "wide"),
            P("wide", "narrow"),
            P(None, "wide", "narrow"),
            P("narrow", "wide"),
            P("wide", "narrow"),
            P("narrow", "wide"),
        ),
        check_vma=False,
    )
```

```python
import functools

import jax
import jax.numpy as jnp
from jax import lax
from jax.experimental import pallas as pl
from jax.experimental.pallas import tpu as pltpu
from jax.sharding import PartitionSpec as P

HEAD_DIM = 64
AUDIO = 1500
EPSILON = 1e-05
NEG_FILL = -1e30
INV_ROOT = HEAD_DIM**-0.5
F32 = jnp.float32
BF16 = jnp.bfloat16
VMEM_LIMIT = 56 << 20
COST_SCALE = 1.0
LONG = 50.0
SHORT = 1e-6
MID = 1e-6
SPLIT = 32


def dot(left, right, left_dim=1, right_dim=0):
    return lax.dot_general(
        left, right, (((left_dim,), (right_dim,)), ((), ())), preferred_element_type=F32
    )


def call(body, grid, in_specs, out_specs, out_shape, name, estimate, prefetch=0, scratch=()):
    return pl.pallas_call(
        body,
        grid_spec=pltpu.PrefetchScalarGridSpec(
            num_scalar_prefetch=prefetch,
            grid=grid,
            in_specs=in_specs,
            out_specs=out_specs,
            scratch_shapes=list(scratch),
        ),
        out_shape=out_shape,
        compiler_params=pltpu.CompilerParams(vmem_limit_bytes=VMEM_LIMIT),
        cost_estimate=estimate,
        name=name,
    )


def shape(dims, dtype=BF16):
    return jax.ShapeDtypeStruct(dims, dtype)


def cost(flops, moved, exps=0, scale=None):
    scale = COST_SCALE if scale is None else scale
    return pl.CostEstimate(
        flops=int(flops * scale), bytes_accessed=int(moved * scale), transcendentals=int(exps * scale)
    )


def whole(shape):
    return pl.BlockSpec(shape, lambda *_: (0,) * len(shape))


def norm_stats(values):
    center = values - jnp.mean(values, axis=-1, keepdims=True)
    spread = jnp.mean(center * center, axis=-1, keepdims=True)
    inverse = lax.rsqrt(spread + EPSILON)
    return center * inverse, inverse


def norm_back(unit, inverse, gains_all, grad):
    scaled = grad * gains_all
    first = jnp.mean(scaled, axis=-1, keepdims=True)
    second = jnp.mean(scaled * unit, axis=-1, keepdims=True)
    return (scaled - first - unit * second) * inverse


def swap(values, axis, bit):
    size = lax.axis_size(axis)
    return lax.ppermute(values, axis, [(i, i ^ bit) for i in range(size)])


def gather_narrow(own):
    other = swap(own, "narrow", 2)
    return [own, swap(own, "narrow", 1), other]


def finish(blocks, then):
    return blocks + [swap(then(blocks[2]), "narrow", 1)]


class Order:
    def __init__(self):
        self.last = None

    def __call__(self, item, *named):
        named = named if self.last is None else named + (self.last,)
        if named:
            item, _ = lax.optimization_barrier((item, named))
        return item

    def join(self, *items):
        items = lax.optimization_barrier(items)
        self.last = items[0]
        return items


def encode_body(order, memory_ref, gain_ref, out_ref):
    unit, _ = norm_stats(memory_ref[:, 0].astype(F32))
    out_ref[...] = (unit * gain_ref[0 : 1]).astype(BF16)


def encode(order, memory, gains_all, start, size, scale=None):
    wide, _, _, width = memory.shape
    group = min(4, wide)
    return call(
        encode_body,
        (wide // group,),
        [
            pl.BlockSpec((group, 1, size, width), lambda i, order: (i, order[0], start // size, 0)),
            whole(gains_all.shape),
        ],
        pl.BlockSpec((group, size, width), lambda i, *_: (i, 0, 0)),
        shape((wide, size, width)),
        "encode",
        cost(0, 4 * wide * size * width, scale=scale),
        prefetch=1,
    )(order, memory, gains_all)


def memory_back_body(order, memory_ref, gain_ref, grad_ref, out_ref, gain_out):
    unit, inverse = norm_stats(memory_ref[:, 0].astype(F32))
    grad = grad_ref[...].astype(F32)
    out_ref[...] = norm_back(unit, inverse, gain_ref[0 : 1], grad).astype(BF16)

    @pl.when(pl.program_id(0) == 0)
    def _():
        gain_out[...] = jnp.zeros_like(gain_out)

    gain_out[...] += jnp.sum(jnp.sum(grad * unit, axis=0), axis=0, keepdims=True)


def memory_back(order, memory, gains_all, grad, start, scale):
    wide, _, _, width = memory.shape
    size = grad.shape[1]
    group = min(4, wide)
    rows = pl.BlockSpec((group, size, width), lambda i, *_: (i, 0, 0))
    return call(
        memory_back_body,
        (wide // group,),
        [
            pl.BlockSpec((group, 1, size, width), lambda i, order: (i, order[0], start // size, 0)),
            whole(gains_all.shape),
            rows,
        ],
        [rows, whole((1, width))],
        [shape((wide, size, width)), shape((1, width), F32)],
        "memory_back",
        cost(0, 6 * wide * size * width, scale=scale),
        prefetch=1,
    )(order, memory, gains_all, grad)


def self_fwd_body(order, lengths, token_ref, gain_ref, weight_ref, normed_ref, qkv_ref, first_ref, second_ref, lse_ref):
    seq = token_ref.shape[1]
    heads = weight_ref.shape[1] // HEAD_DIM
    step = pl.program_id(0)
    length = lengths[order[step]]
    unit, _ = norm_stats(token_ref[0].astype(F32))
    normed = (unit * gain_ref[1 : 2]).astype(BF16)
    normed_ref[0] = normed
    for i in range(3):
        qkv_ref[0, i] = dot(normed, weight_ref[i], 1, 1).astype(BF16)
    cut = 256 if seq > 256 else seq
    mixed = []
    for h in range(heads):
        columns = slice(h * HEAD_DIM, (h + 1) * HEAD_DIM)
        parts = []
        for start, stop in ((0, cut), (cut, seq)):
            if start == stop:
                continue
            queries = qkv_ref[0, 0, start:stop, columns] * jnp.asarray(INV_ROOT, BF16)
            scores = dot(qkv_ref[0, 1, :stop, columns], queries, 1, 1)
            key = lax.broadcasted_iota(jnp.int32, scores.shape, 0)
            query = lax.broadcasted_iota(jnp.int32, scores.shape, 1) + start
            scores = jnp.where((key <= query) & (key < length), scores, NEG_FILL)
            top = jnp.max(scores, axis=0, keepdims=True)
            probs = jnp.exp(scores - top)
            total = jnp.sum(probs, axis=0, keepdims=True)
            out = dot(qkv_ref[0, 2, :stop, columns], probs.astype(BF16), 0, 0) / total
            parts.append(out.T)
            lse_ref[0, h : h + 1, start:stop] = top + jnp.log(total)
        mixed.append(jnp.concatenate(parts, axis=0))
    mixed = jnp.concatenate(mixed, axis=1).astype(BF16)

    @pl.when(step == 0)
    def _():
        first_ref[...] = mixed

    @pl.when(step == 1)
    def _():
        second_ref[...] = mixed


def self_fwd(order, lengths, tokens, gains_all, weights, scale=None):
    _, seq, width = tokens.shape
    local = weights.shape[1]
    heads = local // HEAD_DIM
    return call(
        self_fwd_body,
        (2,),
        [
            pl.BlockSpec((1, seq, width), lambda i, order, lengths: (order[i], 0, 0)),
            whole(gains_all.shape),
            whole((3, local, width)),
        ],
        [
            pl.BlockSpec((1, seq, width), lambda i, *_: (i, 0, 0)),
            pl.BlockSpec((1, 3, seq, local), lambda i, *_: (i, 0, 0, 0)),
            whole((seq, local)),
            whole((seq, local)),
            pl.BlockSpec((1, heads, seq), lambda i, *_: (i, 0, 0)),
        ],
        [
            shape((2, seq, width)),
            shape((2, 3, seq, local)),
            shape((seq, local)),
            shape((seq, local)),
            shape((2, heads, seq), F32),
        ],
        "self_forward",
        cost(2 * (6 * seq * width * local + 8 * seq * seq * local), 2 * seq * width * 8, 2 * heads * seq * seq, scale=scale),
        prefetch=2,
    )(order, lengths, tokens, gains_all, weights)


def self_bwd_body(
    order, lengths, qkv_ref, mixed0_ref, mixed1_ref, lse_ref, grad0_ref, grad1_ref, weight_ref,
    dq_ref, dkv_ref, first_ref, second_ref,
):
    seq = qkv_ref.shape[2]
    local = weight_ref.shape[1]
    heads = local // HEAD_DIM
    step = pl.program_id(0)
    length = lengths[order[step]]
    grad = jnp.where(step == 0, grad0_ref[...], grad1_ref[...])
    mixed = jnp.where(step == 0, mixed0_ref[...], mixed1_ref[...])
    inner = grad.astype(F32) * mixed.astype(F32)
    totals = jnp.concatenate((lse_ref[0], jnp.zeros((8 - heads % 8, seq), F32)), axis=0).T
    cut = 256 if seq > 256 else seq
    for h in range(heads):
        columns = slice(h * HEAD_DIM, (h + 1) * HEAD_DIM)
        keys = qkv_ref[0, 1, :, columns]
        values = qkv_ref[0, 2, :, columns]
        dq_parts = []
        dk, dv = 0.0, 0.0
        for start, stop in ((0, cut), (cut, seq)):
            if start == stop:
                continue
            queries = qkv_ref[0, 0, start:stop, columns] * jnp.asarray(INV_ROOT, BF16)
            grads = grad[start:stop, columns]
            scores = dot(queries, keys[:stop], 1, 1)
            key = lax.broadcasted_iota(jnp.int32, scores.shape, 1)
            query = lax.broadcasted_iota(jnp.int32, scores.shape, 0) + start
            allowed = (key <= query) & (key < length)
            probs = jnp.exp(jnp.where(allowed, scores, NEG_FILL) - totals[start:stop, h : h + 1])
            dp = dot(grads, values[:stop], 1, 1)
            centre = jnp.sum(inner[start:stop, columns], axis=1, keepdims=True)
            ds = (probs * (dp - centre)).astype(BF16)
            dk_now = dot(queries, ds, 0, 0)
            dv_now = dot(grads, probs.astype(BF16), 0, 0)
            if stop < seq:
                pad = jnp.zeros((HEAD_DIM, seq - stop), F32)
                dk_now = jnp.concatenate((dk_now, pad), axis=1)
                dv_now = jnp.concatenate((dv_now, pad), axis=1)
            dk, dv = dk + dk_now, dv + dv_now
            dq_parts.append(dot(ds, keys[:stop]) * INV_ROOT)
        dq_ref[0, :, columns] = jnp.concatenate(dq_parts, axis=0).astype(BF16)
        dkv_ref[0, columns, :] = dk.astype(BF16)
        dkv_ref[0, local + h * HEAD_DIM : local + (h + 1) * HEAD_DIM, :] = dv.astype(BF16)
    total = dot(dq_ref[0], weight_ref[0])
    total = total + dot(dkv_ref[0, :local, :], weight_ref[1], 0, 0)
    total = (total + dot(dkv_ref[0, local:, :], weight_ref[2], 0, 0)).astype(BF16)

    @pl.when(step == 0)
    def _():
        first_ref[...] = total

    @pl.when(step == 1)
    def _():
        second_ref[...] = total


def self_bwd(order, lengths, qkv, mixed0, mixed1, lse, grad0, grad1, weights, scale):
    _, _, seq, local = qkv.shape
    width = weights.shape[2]
    heads = local // HEAD_DIM
    return call(
        self_bwd_body,
        (2,),
        [
            pl.BlockSpec((1, 3, seq, local), lambda i, *_: (i, 0, 0, 0)),
            whole((seq, local)),
            whole((seq, local)),
            pl.BlockSpec((1, heads, seq), lambda i, *_: (i, 0, 0)),
            whole((seq, local)),
            whole((seq, local)),
            whole((3, local, width)),
        ],
        [
            pl.BlockSpec((1, seq, local), lambda i, *_: (i, 0, 0)),
            pl.BlockSpec((1, 2 * local, seq), lambda i, *_: (i, 0, 0)),
            whole((seq, width)),
            whole((seq, width)),
        ],
        [shape((2, seq, local)), shape((2, 2 * local, seq)), shape((seq, width)), shape((seq, width))],
        "self_backward",
        cost(2 * (6 * seq * width * local + 20 * seq * seq * local), 2 * seq * width * 8, 2 * heads * seq * seq, scale=scale),
        prefetch=2,
    )(order, lengths, qkv, mixed0, mixed1, lse, grad0, grad1, weights)


def to_query_body(order, token_ref, m0, m1, m2, m3, p0, p1, p2, p3, gain_ref, after_ref, normed_ref, query_ref):
    local = m0.shape[1]
    rows = token_ref[0].astype(F32)
    for mixed, pack in ((m0, p0), (m1, p1), (m2, p2), (m3, p3)):
        rows = rows + dot(mixed[...], pack[:local])
    after_ref[...] = rows
    unit, _ = norm_stats(rows)
    normed = (unit * gain_ref[2 : 3]).astype(BF16)
    normed_ref[...] = normed
    for r, pack in enumerate((p0, p1, p2, p3)):
        query = dot(normed, pack[local:], 1, 1).astype(BF16)
        query_ref[r // 2, :, (r % 2) * local : (r % 2 + 1) * local] = query


def to_query(order, tokens, mixes, packs, gains_all):
    _, seq, width = tokens.shape
    local = mixes[0].shape[1]
    tile = seq // 2
    return call(
        to_query_body,
        (2,),
        [pl.BlockSpec((1, tile, width), lambda i, order: (order[0], i, 0))]
        + [pl.BlockSpec((tile, local), lambda i, *_: (i, 0))] * 4
        + [whole((2 * local, width))] * 4
        + [whole(gains_all.shape)],
        [
            pl.BlockSpec((tile, width), lambda i, *_: (i, 0)),
            pl.BlockSpec((tile, width), lambda i, *_: (i, 0)),
            pl.BlockSpec((2, tile, 2 * local), lambda i, *_: (0, i, 0)),
        ],
        [shape((seq, width), F32), shape((seq, width)), shape((2, seq, 2 * local))],
        "self_out_to_query",
        cost(4 * seq * width * width, seq * width * 12 + 4 * width * width),
        prefetch=1,
    )(order, tokens, *mixes, *packs, gains_all)


def head_places(local):
    for r in range(2):
        for h in range(local // HEAD_DIM):
            at = r * local + h * HEAD_DIM
            key = 2 * r * local + h * HEAD_DIM
            yield (
                at // HEAD_DIM,
                slice(at, at + HEAD_DIM),
                slice(key, key + HEAD_DIM),
                slice(key + local, key + local + HEAD_DIM),
            )


def cross_first_body(query_ref, encoded_ref, w0, w1, w2, w3, kv_ref, acc_ref, top_ref, total_ref, *, valid):
    make_keys_values(encoded_ref, (w0, w1, w2, w3), kv_ref)
    frames = kv_ref.shape[0]
    for head, columns, key, value in head_places(query_ref.shape[2] // 2):
        queries = query_ref[0, :, columns] * jnp.asarray(INV_ROOT, BF16)
        scores = dot(kv_ref[:, key], queries, 1, 1)
        if valid < frames:
            frame = lax.broadcasted_iota(jnp.int32, scores.shape, 0)
            scores = jnp.where(frame < valid, scores, NEG_FILL)
        top = jnp.max(scores, axis=0, keepdims=True)
        probs = jnp.exp(scores - top)
        acc_ref[0, columns, :] = dot(kv_ref[:, value], probs.astype(BF16), 0, 0)
        top_ref[0, head : head + 1, :] = top
        total_ref[0, head : head + 1, :] = jnp.sum(probs, axis=0, keepdims=True)


def make_keys_values(encoded_ref, weights, kv_ref):
    pair = weights[0].shape[0]
    for step in range(2):

        @pl.when(pl.program_id(0) == step)
        def _():
            for r in range(2):
                kv = dot(encoded_ref[...], weights[2 * step + r][...], 1, 1)
                kv_ref[:, r * pair : (r + 1) * pair] = kv.astype(BF16)


def cross_second_body(
    query_ref, encoded_ref, w0, w1, w2, w3, acc_in, top_in, total_in, after_ref, o0, o1, o2, o3, gain_ref,
    kv_ref, mixed_ref, lse_ref, next_ref, normed_ref, *, valid,
):
    make_keys_values(encoded_ref, (w0, w1, w2, w3), kv_ref)
    frames = kv_ref.shape[0]
    local = o0.shape[0]
    for head, columns, key, value in head_places(local):
        queries = query_ref[0, :, columns] * jnp.asarray(INV_ROOT, BF16)
        scores = dot(kv_ref[:, key], queries, 1, 1)
        if valid < frames:
            frame = lax.broadcasted_iota(jnp.int32, scores.shape, 0)
            scores = jnp.where(frame < valid, scores, NEG_FILL)
        before = top_in[0, head : head + 1, :]
        top = jnp.maximum(jnp.max(scores, axis=0, keepdims=True), before)
        probs = jnp.exp(scores - top)
        fade = jnp.exp(before - top)
        total = jnp.sum(probs, axis=0, keepdims=True) + total_in[0, head : head + 1, :] * fade
        out = dot(kv_ref[:, value], probs.astype(BF16), 0, 0) + acc_in[0, columns, :] * fade
        mixed_ref[0, :, columns] = (out / total).T.astype(BF16)
        lse_ref[0, head : head + 1, :] = top + jnp.log(total)
    outs = (o0, o1, o2, o3)
    for step in range(2):

        @pl.when(pl.program_id(0) == step)
        def _():
            rows = after_ref[...] if step == 0 else next_ref[...]
            for r in range(2):
                rows = rows + dot(mixed_ref[0, :, r * local : (r + 1) * local], outs[2 * step + r][...])
            next_ref[...] = rows
            if step == 1:
                unit, _ = norm_stats(rows)
                normed_ref[...] = (unit * gain_ref[3 : 4]).astype(BF16)


def pack_specs(packs, rows, index):
    width = packs[0].shape[1]
    return [pl.BlockSpec((rows, width), lambda *_: (index, 0))] * 4


def cross_first(query, encoded, packs, valid):
    _, seq, pair = query.shape
    frames, width = encoded.shape
    heads = pair // HEAD_DIM
    stats = pl.BlockSpec((1, heads, seq), lambda i: (i, 0, 0))
    return call(
        functools.partial(cross_first_body, valid=valid),
        (2,),
        [pl.BlockSpec((1, seq, pair), lambda i: (i, 0, 0)), whole((frames, width))] + pack_specs(packs, pair, 0),
        [
            pl.BlockSpec((frames, 2 * pair), lambda i: (0, i)),
            pl.BlockSpec((1, pair, seq), lambda i: (i, 0, 0)),
            stats,
            stats,
        ],
        [
            shape((frames, 4 * pair)),
            shape((2, pair, seq), F32),
            shape((2, heads, seq), F32),
            shape((2, heads, seq), F32),
        ],
        "cross_first",
        cost(4 * frames * width * width + 40 * seq * frames * pair, 8 * frames * width, 2 * heads * seq * frames),
    )(query, encoded, *packs)


def cross_second(query, encoded, packs, packs_out, valid, before, after, gains_all):
    _, seq, pair = query.shape
    frames, width = encoded.shape
    heads = pair // HEAD_DIM
    rows = pl.BlockSpec((1, seq, pair), lambda i: (i, 0, 0))
    stats = pl.BlockSpec((1, heads, seq), lambda i: (i, 0, 0))
    acc = pl.BlockSpec((1, pair, seq), lambda i: (i, 0, 0))
    return call(
        functools.partial(cross_second_body, valid=valid),
        (2,),
        [rows, whole((frames, width))]
        + pack_specs(packs, pair, 0)
        + [acc, stats, stats, whole((seq, width))]
        + pack_specs(packs_out, pair // 2, 0)
        + [whole(gains_all.shape)],
        [pl.BlockSpec((frames, 2 * pair), lambda i: (0, i)), rows, stats, whole((seq, width)), whole((seq, width))],
        [
            shape((frames, 4 * pair)),
            shape((2, seq, pair)),
            shape((2, heads, seq), F32),
            shape((seq, width), F32),
            shape((seq, width)),
        ],
        "cross_second",
        cost(4 * frames * width * width + 40 * seq * frames * pair, 10 * frames * width, 2 * heads * seq * frames),
    )(query, encoded, *packs, *before, after, *packs_out, gains_all)


def feed_body(order, lengths, *refs, count):
    row_refs, (grad_ref, in_ref, out_ref, hidden_ref, pre_ref, live_ref) = refs[:count], refs[count : count + 6]
    outs = refs[count + 6 :]
    step = pl.program_id(0)
    tile = grad_ref.shape[1]
    rows = row_refs[0][...]
    if count == 2:
        rows = jnp.where(step == 0, rows, row_refs[1][...])
    place = lax.broadcasted_iota(jnp.int32, grad_ref.shape[1:], 0) + pl.program_id(1) * tile
    grads = jnp.where(place < lengths[order[step]], grad_ref[0], jnp.zeros((), BF16))
    live_ref[0] = grads
    pre = dot(rows, in_ref[...])
    half = 0.5 * (1.0 + lax.erf(pre * (0.5**0.5)))
    hidden = (pre * half).astype(BF16)
    slope = half + pre * jnp.exp(-0.5 * pre * pre) * 0.3989422804014327
    hidden_ref[0] = hidden
    grad_pre = (dot(grads, out_ref[...], 1, 1) * slope).astype(BF16)
    pre_ref[0] = grad_pre
    part = dot(grad_pre, in_ref[...], 1, 1).astype(BF16)
    feed = dot(hidden, out_ref[...]).astype(BF16)
    for i in range(count):

        @pl.when(step == i)
        def _():
            outs[2 * i][...] = part
            outs[2 * i + 1][...] = feed


def feed_forward(order, lengths, rows, out_grad, fc_in, fc_out):
    count = len(rows)
    seq, width = rows[0].shape
    units = fc_in.shape[1]
    tiles = 2
    tile = seq // tiles
    block = lambda last: pl.BlockSpec((1, tile, last), lambda i, j, *_: (i, j, 0))
    single = [
        pl.BlockSpec((tile, width), lambda i, j, *_: (jnp.where(i == 0, j, tiles - 1), 0)),
        pl.BlockSpec((tile, width), lambda i, j, *_: (jnp.where(i == 0, 0, j), 0)),
    ]
    if count == 1:
        single = [pl.BlockSpec((tile, width), lambda i, j, *_: (j, 0))]
    return call(
        functools.partial(feed_body, count=count),
        (count, tiles),
        single
        + [
            pl.BlockSpec((1, tile, width), lambda i, j, order, lengths: (order[i], j, 0)),
            whole((width, units)),
            whole((units, width)),
        ],
        [block(units), block(units), block(width)] + [spec for spec in single for _ in range(2)],
        [shape((count, seq, units)), shape((count, seq, units)), shape((count, seq, width))]
        + [shape((seq, width))] * (2 * count),
        "feed_forward",
        cost(8 * count * seq * width * units, count * seq * width * 14, 2 * count * seq * units),
        prefetch=2,
    )(order, lengths, *rows, out_grad, fc_in, fc_out)


def add_gain(gain_out, term):
    @pl.when(pl.program_id(0) == 0)
    def _():
        gain_out[...] = jnp.zeros_like(gain_out)

    gain_out[...] += term


def cross_back(queries_ref, kv_ref, grads_ref, mixed_ref, lse_ref, dkv_ref, local, valid, store):
    frames = kv_ref.shape[0]
    inner = grads_ref.astype(F32) * mixed_ref[0].astype(F32)
    heads, seq = lse_ref.shape[1:]
    totals = jnp.concatenate((lse_ref[0], jnp.zeros((8 - heads % 8, seq), F32)), axis=0).T
    for head, columns, key, value in head_places(local):
        queries = queries_ref[0, :, columns] * jnp.asarray(INV_ROOT, BF16)
        grads = grads_ref[:, columns]
        centre = jnp.sum(inner[:, columns], axis=1, keepdims=True)
        keys = kv_ref[:, key]
        probs = jnp.exp(dot(queries, keys, 1, 1) - totals[:, head : head + 1])
        if valid < frames:
            frame = lax.broadcasted_iota(jnp.int32, probs.shape, 1)
            probs = jnp.where(frame < valid, probs, 0.0)
        dp = dot(grads, kv_ref[:, value], 1, 1)
        ds = (probs * (dp - centre)).astype(BF16)
        dkv_ref[value, :] = dot(grads, probs.astype(BF16), 0, 0).astype(BF16)
        dkv_ref[key, :] = dot(queries, ds, 0, 0).astype(BF16)
        store(columns, dot(ds, keys))


def encoded_back(dkv_ref, weights, out_ref, acc):
    pair = weights[0].shape[0]
    for step in range(2):

        @pl.when(pl.program_id(0) == step)
        def _():
            total = dot(dkv_ref[:pair, :], weights[2 * step][...], 0, 0)
            total = total + dot(dkv_ref[pair:, :], weights[2 * step + 1][...], 0, 0)
            if step == 0:
                acc[...] = total
            else:
                out_ref[...] = (acc[...] + total).astype(BF16)


def cross_first_back_body(
    order, lengths, grad_ref, own_ref, near_ref, far_ref, after_ref, gain_ref, o0, o1, o2, o3,
    query_ref, kv_ref, mixed_ref, lse_ref, w0, w1, w2, w3,
    cross_ref, two_ref, grads_ref, gain_out, dq_ref, dkv_ref, encoded_ref, acc, *, valid,
):
    local = o0.shape[0]
    step = pl.program_id(0)

    @pl.when(step == 0)
    def _():
        place = lax.broadcasted_iota(jnp.int32, own_ref.shape, 0)
        grads = jnp.where(place < lengths[order[0]], grad_ref[0].astype(F32), 0.0)
        normed_grad = own_ref[...].astype(F32) + near_ref[...].astype(F32) + far_ref[...].astype(F32)
        unit, inverse = norm_stats(after_ref[...])
        total = grads + norm_back(unit, inverse, gain_ref[3 : 4], normed_grad)
        cross_ref[...] = total
        low = total.astype(BF16)
        two_ref[...] = low
        for r, weight in enumerate((o0, o1, o2, o3)):
            mixed = dot(low, weight[...], 1, 1).astype(BF16)
            grads_ref[r // 2, :, (r % 2) * local : (r % 2 + 1) * local] = mixed
        gain_out[...] = jnp.sum(normed_grad * unit, axis=0, keepdims=True)

    def store(columns, dq):
        dq_ref[0, :, columns] = dq

    cross_back(query_ref, kv_ref, grads_ref[step], mixed_ref, lse_ref, dkv_ref, local, valid, store)
    encoded_back(dkv_ref, (w0, w1, w2, w3), encoded_ref, acc)


def cross_first_back(order, lengths, out_grad, parts, after, gains_all, packs, packs_out, query, kv, mixed, lse, valid):
    seq, width = after.shape
    frames = kv.shape[0]
    pair = query.shape[2]
    heads = pair // HEAD_DIM
    rows = whole((seq, width))
    head_rows = pl.BlockSpec((1, seq, pair), lambda i, *_: (i, 0, 0))
    both = pl.BlockSpec((frames, 2 * pair), lambda i, *_: (0, i))
    return call(
        functools.partial(cross_first_back_body, valid=valid),
        (2,),
        [pl.BlockSpec((1, seq, width), lambda i, order, lengths: (order[0], 0, 0)), rows, rows, rows, rows]
        + [whole(gains_all.shape)]
        + pack_specs(packs_out, pair // 2, 0)
        + [head_rows, both, head_rows, pl.BlockSpec((1, heads, seq), lambda i, *_: (i, 0, 0))]
        + pack_specs(packs, pair, 0),
        [
            rows,
            rows,
            whole((2, seq, pair)),
            whole((1, width)),
            head_rows,
            pl.BlockSpec((2 * pair, frames), lambda i, *_: (i, 0)),
            whole((frames, width)),
        ],
        [
            shape((seq, width), F32),
            shape((seq, width)),
            shape((2, seq, pair)),
            shape((1, width), F32),
            shape((2, seq, pair), F32),
            shape((2 * width, frames)),
            shape((frames, width)),
        ],
        "cross_first_back",
        cost(4 * frames * width * width + 120 * seq * frames * pair, 20 * frames * width, 2 * heads * seq * frames),
        prefetch=2,
        scratch=[pltpu.VMEM((frames, width), F32)],
    )(order, lengths, out_grad, *parts, after, gains_all, *packs_out, query, kv, mixed, lse, *packs)


def cross_second_back_body(
    query_ref, kv_ref, grads_ref, mixed_ref, lse_ref, dq_in, w0, w1, w2, w3,
    p0, p1, p2, p3, after_ref, gain_ref, cross_ref,
    dq_ref, dkv_ref, encoded_ref, self_ref, one_ref, h0, h1, h2, h3, gain_out, acc, *, valid,
):
    local = h0.shape[1]
    step = pl.program_id(0)

    def store(columns, dq):
        dq_ref[step, :, columns] = ((dq + dq_in[0, :, columns]) * INV_ROOT).astype(BF16)

    cross_back(query_ref, kv_ref, grads_ref[0], mixed_ref, lse_ref, dkv_ref, local, valid, store)
    encoded_back(dkv_ref, (w0, w1, w2, w3), encoded_ref, acc)

    @pl.when(step == 1)
    def _():
        packs = (p0, p1, p2, p3)
        normed_grad = 0.0
        for r, pack in enumerate(packs):
            normed_grad = normed_grad + dot(dq_ref[r // 2, :, (r % 2) * local : (r % 2 + 1) * local], pack[local:])
        unit, inverse = norm_stats(after_ref[...])
        total = cross_ref[...] + norm_back(unit, inverse, gain_ref[2 : 3], normed_grad)
        self_ref[...] = total
        low = total.astype(BF16)
        one_ref[...] = low
        for out, pack in zip((h0, h1, h2, h3), packs):
            out[...] = dot(low, pack[:local], 1, 1).astype(BF16)
        gain_out[...] = jnp.sum(normed_grad * unit, axis=0, keepdims=True)


def cross_second_back(query, kv, grads, mixed, lse, dq, packs_two, packs_one, after, gains_all, cross, valid):
    seq, width = after.shape
    frames = kv.shape[0]
    pair = query.shape[2]
    local = pair // 2
    heads = pair // HEAD_DIM
    rows = whole((seq, width))
    head_rows = pl.BlockSpec((1, seq, pair), lambda i: (i, 0, 0))
    both = pl.BlockSpec((frames, 2 * pair), lambda i: (0, i))
    return call(
        functools.partial(cross_second_back_body, valid=valid),
        (2,),
        [head_rows, both, head_rows, head_rows, pl.BlockSpec((1, heads, seq), lambda i: (i, 0, 0))]
        + [head_rows]
        + pack_specs(packs_two, pair, 0)
        + pack_specs(packs_one, pair, 0)
        + [rows, whole(gains_all.shape), rows],
        [whole((2, seq, pair)), pl.BlockSpec((2 * pair, frames), lambda i: (i, 0)), whole((frames, width)), rows, rows]
        + [whole((seq, local))] * 4
        + [whole((1, width))],
        [
            shape((2, seq, pair)),
            shape((2 * width, frames)),
            shape((frames, width)),
            shape((seq, width), F32),
            shape((seq, width)),
        ]
        + [shape((seq, local))] * 4
        + [shape((1, width), F32)],
        "cross_second_back",
        cost(4 * frames * width * width + 120 * seq * frames * pair, 20 * frames * width, 2 * heads * seq * frames),
        scratch=[pltpu.VMEM((frames, width), F32)],
    )(query, kv, grads, mixed, lse, dq, *packs_two, *packs_one, after, gains_all, cross)


def add_gain(gain_out, term):
    @pl.when(pl.program_id(0) == 0)
    def _():
        gain_out[...] = jnp.zeros_like(gain_out)

    gain_out[...] += term

def to_tokens_grad_body(order, token_ref, own_ref, near_ref, far_ref, self_ref, gain_ref, out_ref, gain_out):
    normed_grad = own_ref[...].astype(F32) + near_ref[...].astype(F32) + far_ref[...].astype(F32)
    unit, inverse = norm_stats(token_ref[0].astype(F32))
    out_ref[...] = (self_ref[...] + norm_back(unit, inverse, gain_ref[1 : 2], normed_grad)).astype(BF16)
    add_gain(gain_out, jnp.sum(normed_grad * unit, axis=0, keepdims=True))


def to_tokens_grad(order, tokens, own, near, far, grad_self, gains_all, scale):
    _, seq, width = tokens.shape
    tile = seq // 2
    rows = pl.BlockSpec((tile, width), lambda i, *_: (i, 0))
    return call(
        to_tokens_grad_body,
        (2,),
        [pl.BlockSpec((1, tile, width), lambda i, order: (order[0], i, 0)), rows, rows, rows, rows, whole(gains_all.shape)],
        [rows, whole((1, width))],
        [shape((seq, width)), shape((1, width), F32)],
        "norm_one_back",
        cost(0, seq * width * 14, scale=scale),
        prefetch=1,
    )(order, tokens, own, near, far, grad_self, gains_all)


def split_store(total, mine, keep_ref, give_ref, scratch, lead=()):
    scratch[...] = total
    parts, depth = keep_ref.shape[-3], keep_ref.shape[-2]
    for j in range(parts):
        at = pl.multiple_of((2 * j + mine) * depth, 8)
        keep_ref[lead + (j,)] = scratch[pl.ds(at, depth), :].astype(BF16)
        at = pl.multiple_of((2 * j + 1 - mine) * depth, 8)
        give_ref[lead + (j,)] = scratch[pl.ds(at, depth), :].astype(BF16)


def feed_weights_body(bits, *refs):
    rows, pres, lives, hiddens = refs[:4], refs[4:7], refs[7:10], refs[10:13]
    keep_ref, give_ref, scratch = refs[13:]
    three = lambda items: (items[0][0], items[0][1], items[1][0], items[2][0])
    total = 0.0
    for left, right in zip(rows, three(pres)):
        total = total + dot(left[...], right, 0, 0)
    split_store(total, bits[0], keep_ref, give_ref, scratch, (0,))
    total = 0.0
    for left, right in zip(three(lives), three(hiddens)):
        total = total + dot(left, right, 0, 0)
    split_store(total, bits[0], keep_ref, give_ref, scratch, (1,))


def feed_weights(bits, rows, pres, lives, hiddens, wide):
    seq, width = rows[0].shape
    units = pres[0].shape[2]
    tile = width // 2
    depth = width // wide
    column = lambda count: pl.BlockSpec((count, seq, tile), lambda i, *_: (0, 0, i))
    full = lambda count: whole((count, seq, units))
    out = pl.BlockSpec((2, wide // 4, depth, units), lambda i, *_: (0, i, 0, 0))
    return call(
        feed_weights_body,
        (2,),
        [pl.BlockSpec((seq, tile), lambda i, *_: (0, i))] * 4
        + [full(2), full(1), full(1), column(2), column(1), column(1), full(2), full(1), full(1)],
        [out, out],
        [shape((2, wide // 2, depth, units))] * 2,
        "feed_weight_grads",
        cost(16 * seq * width * units, 24 * seq * width),
        prefetch=1,
        scratch=[pltpu.VMEM((tile, units), F32)],
    )(bits, *rows, *pres, *lives, *hiddens)


def head_weights_body(enc0, enc1, dkv0, dkv1, two, grad_two, dq_ref, cross_mixed, keep_ref, give_ref):
    local = dq_ref.shape[2] // 2
    for r, out in enumerate((keep_ref, give_ref)):
        columns = slice(r * local, (r + 1) * local)
        pair = slice(2 * r * local, 2 * (r + 1) * local)
        kv = dot(dkv0[pair, :], enc0[...]) + dot(dkv1[pair, :], enc1[...])
        out[0, :, : 2 * local] = kv.T.astype(BF16)
        query = dot(two[...], dq_ref[0, :, columns], 0, 0)
        cross = dot(grad_two[...], cross_mixed[0, :, columns], 0, 0)
        out[0, :, 2 * local :] = jnp.concatenate((query, cross), axis=1).astype(BF16)


def head_weights(encs, dkvs, normed_two, dq, grad_two, cross_mixed, scale):
    seq, width = normed_two.shape
    heads = pl.BlockSpec((1, seq, width // 2), lambda i: (i, 0, 0))
    out = pl.BlockSpec((1, width, width), lambda i: (i, 0, 0))
    frames = encs[0].shape[0] + encs[1].shape[0]
    return call(
        head_weights_body,
        (2,),
        [whole(item.shape) for item in encs]
        + [pl.BlockSpec((width, item.shape[1]), lambda i: (i, 0)) for item in dkvs]
        + [whole((seq, width))] * 2
        + [heads] * 2,
        [out, out],
        [shape((2, width, width))] * 2,
        "head_weight_grads",
        cost(4 * frames * width * width + 4 * seq * width * width, 6 * frames * width, scale=scale),
    )(*encs, *dkvs, normed_two, grad_two, dq, cross_mixed)


def out_weights_body(one, m0, m1, m2, m3, keep_ref, give_ref):
    for r, mixed in enumerate((m0, m1, m2, m3)):
        (keep_ref, give_ref)[r % 2][r // 2] = dot(mixed[...], one[...], 0, 0).astype(BF16)


def out_weights(grad_one, mixes, scale):
    seq, width = grad_one.shape
    local = mixes[0].shape[1]
    return call(
        out_weights_body,
        (1,),
        [whole(item.shape) for item in (grad_one, *mixes)],
        [whole((2, local, width))] * 2,
        [shape((2, local, width))] * 2,
        "out_weight_grads",
        cost(2 * seq * width * width, 8 * seq * width, scale=scale),
    )(grad_one, *mixes)


def self_weights_body(bits, near, far, dq_near, dkv_near, dq_far, dkv_far, own, core, other, keep_ref, give_ref, scratch):
    local = dq_near.shape[2]
    totals = [0.0, 0.0, 0.0]
    for rows, dq, dkv in ((near, dq_near, dkv_near), (far, dq_far, dkv_far)):
        for c in range(2):
            totals[0] = totals[0] + dot(rows[c], dq[c], 0, 0)
            totals[1] = totals[1] + dot(rows[c], dkv[c, :local, :], 0, 1)
            totals[2] = totals[2] + dot(rows[c], dkv[c, local:, :], 0, 1)
    totals.append((own[0].astype(F32) + core[0].astype(F32) + other[...].astype(F32)).T)
    split_store(jnp.concatenate(totals, axis=1), bits[0], keep_ref, give_ref, scratch)


def self_weights(bits, near, far, dq_near, dkv_near, dq_far, dkv_far, own, core, other, wide, scale):
    _, seq, width = near.shape
    local = dq_near.shape[2]
    tile = width // 2
    depth = width // wide
    rows = pl.BlockSpec((2, seq, tile), lambda i, *_: (0, 0, i))
    turned = pl.BlockSpec((1, local, tile), lambda i, *_: (0, 0, i))
    out = pl.BlockSpec((wide // 4, depth, 4 * local), lambda i, *_: (i, 0, 0))
    return call(
        self_weights_body,
        (2,),
        [rows, rows] + [whole(item.shape) for item in (dq_near, dkv_near, dq_far, dkv_far)] + [turned, turned]
        + [pl.BlockSpec((local, tile), lambda i, *_: (0, i))],
        [out, out],
        [shape((wide // 2, depth, 4 * local))] * 2,
        "self_weight_grads",
        cost(24 * seq * width * local, 16 * seq * width, scale=scale),
        prefetch=1,
        scratch=[pltpu.VMEM((tile, 4 * local), F32)],
    )(bits, near, far, dq_near, dkv_near, dq_far, dkv_far, own, core, other)


def add_low(keep, got):
    return (keep.astype(F32) + got.astype(F32)).astype(BF16)


def merge_body(bits, *refs, which, joined):
    ins, outs = refs[: 2 * len(which)], refs[2 * len(which) :]
    at = 0
    for i, bit in enumerate(which):
        keep_in, got_in = ins[2 * i], ins[2 * i + 1]
        mine = bits[bit]
        keep_out, give_out = outs if joined else outs[2 * i : 2 * i + 2]
        groups = slice(at, at + keep_in.shape[0])
        at += keep_in.shape[0] if joined else 0
        keep_out[groups, 0] = add_low(keep_in[:, mine], got_in[:, mine])
        give_out[groups, 0] = add_low(keep_in[:, 1 - mine], got_in[:, 1 - mine])


def merge(bits, which, *pairs, scale=None, joined=False):
    rows, columns = pairs[0][0].shape[2:]
    tile = rows // 2 if rows % 32 == 0 else rows
    both = [
        pl.BlockSpec((item.shape[0], 2, tile, columns), lambda i, *_: (0, 0, i, 0)) for pair in pairs for item in pair
    ]
    groups = [keep.shape[0] for keep, _ in pairs]
    total = sum(groups)
    groups = [total] if joined else groups
    return call(
        functools.partial(merge_body, which=which, joined=joined),
        (rows // tile,),
        both,
        [pl.BlockSpec((count, 1, tile, columns), lambda i, *_: (0, 0, i, 0)) for count in groups for _ in range(2)],
        [shape((count, 1, rows, columns)) for count in groups for _ in range(2)],
        "merge",
        cost(0, 12 * total * rows * columns, scale=scale),
        prefetch=1,
    )(bits, *[item for pair in pairs for item in pair])


def merge_heads_body(bits, keep_in, got_in, keep_a, give_a, keep_b, give_b):
    low, high = bits[0], bits[1]
    for j in range(keep_a.shape[0]):
        keep_a[j] = add_low(keep_in[0, 2 * j + low], got_in[0, 2 * j + low])
        give_a[j] = add_low(keep_in[0, 2 * j + 1 - low], got_in[0, 2 * j + 1 - low])
        at = 4 * (j // 2) + j % 2
        keep_b[j] = add_low(keep_in[1, at + 2 * high], got_in[1, at + 2 * high])
        give_b[j] = add_low(keep_in[1, at + 2 * (1 - high)], got_in[1, at + 2 * (1 - high)])


def merge_heads(bits, keep, got):
    _, parts, rows, columns = keep.shape
    tile = rows // 2 if rows % 32 == 0 else rows
    both = pl.BlockSpec((2, parts, tile, columns), lambda i, *_: (0, 0, i, 0))
    out = pl.BlockSpec((parts // 2, tile, columns), lambda i, *_: (0, i, 0))
    return call(
        merge_heads_body,
        (rows // tile,),
        [both, both],
        [out] * 4,
        [shape((parts // 2, rows, columns))] * 4,
        "merge_heads",
        cost(0, 12 * parts * rows * columns, scale=SHORT),
        prefetch=1,
    )(bits, keep, got)


def scatter_wide(bits, then, keep, give, which, got):
    dims = keep.shape[-2:]
    parts = lax.axis_size("wide") >> which
    lead = keep.size // (parts * dims[0] * dims[1])
    while parts > 1:
        parts //= 2
        view = (lead * parts, 2) + dims
        keep, give = merge(then(bits), (which,), (keep.reshape(view), got.reshape(view)), scale=SHORT)
        then.last = keep
        which += 1
        got = swap(give, "wide", 1 << (which - 1))
    return keep.reshape((lead,) + dims), got.reshape((lead,) + dims)


def finish_self_body(keep_ref, got_ref, give_ref, heads_ref, qkv_ref, out_ref):
    local = out_ref.shape[0]
    heads_ref[...] = keep_ref[0].astype(F32) + got_ref[0].astype(F32)
    give_ref[...] = (keep_ref[1].astype(F32) + got_ref[1].astype(F32)).astype(BF16)
    own = keep_ref[2].astype(F32) + got_ref[2].astype(F32)
    for i in range(3):
        qkv_ref[i] = own[:, i * local : (i + 1) * local]
    out_ref[...] = own[:, 3 * local :].T


def finish_self(keep, got):
    _, depth, width = keep.shape
    local = width // 4
    dims = [(depth, width), (depth, width), (3, depth, local), (local, depth)]
    return call(
        finish_self_body,
        (1,),
        [whole(keep.shape)] * 2,
        [whole(item) for item in dims],
        [shape(dims[0])] + [shape(item, F32) for item in dims[1:]],
        "finish_self",
        cost(0, 12 * keep.size, scale=SHORT),
    )(keep, got)


def finish_heads_body(own_ref, other_ref, kv_ref, query_ref, out_ref):
    local = out_ref.shape[0]
    total = own_ref[...] + other_ref[...].astype(F32)
    for i in range(2):
        kv_ref[i] = total[:, i * local : (i + 1) * local]
    query_ref[...] = total[:, 2 * local : 3 * local]
    out_ref[...] = total[:, 3 * local :].T


def finish_heads(own, other):
    depth, width = own.shape
    local = width // 4
    dims = [(2, depth, local), (depth, local), (local, depth)]
    return call(
        finish_heads_body,
        (1,),
        [whole(own.shape)] * 2,
        [whole(item) for item in dims],
        [shape(item, F32) for item in dims],
        "finish_heads",
        cost(0, 12 * own.size, scale=SHORT),
    )(own, other)


def place_body(order, a, b, c, d, *refs, start):
    out, held, reads, writes = refs[-4:]
    blocks = (a, b, c, d)
    loads = [pltpu.make_async_copy(item, held.at[r], reads.at[r]) for r, item in enumerate(blocks)]
    for item in loads:
        item.start()
    stores = []
    for r, item in enumerate(loads):
        item.wait()
        if start is None:
            target = out.at[order[r]]
        else:
            target = out.at[:, order[r], pl.ds(start, held.shape[2])]
        stores.append(pltpu.make_async_copy(held.at[r], target, writes.at[r]))
        stores[-1].start()
    for item in stores:
        item.wait()


def place_blocks(order, blocks, dims, start=None, before=None, scale=None):
    anywhere = pl.BlockSpec(memory_space=pl.ANY)
    extra = () if before is None else (before,)
    return pl.pallas_call(
        functools.partial(place_body, start=start),
        grid_spec=pltpu.PrefetchScalarGridSpec(
            num_scalar_prefetch=1,
            grid=(1,),
            in_specs=[anywhere] * (4 + len(extra)),
            out_specs=anywhere,
            scratch_shapes=[
                pltpu.VMEM((4,) + blocks[0].shape, BF16),
                pltpu.SemaphoreType.DMA((4,)),
                pltpu.SemaphoreType.DMA((4,)),
            ],
        ),
        out_shape=shape(dims),
        input_output_aliases={5: 0} if extra else {},
        compiler_params=pltpu.CompilerParams(vmem_limit_bytes=VMEM_LIMIT),
        cost_estimate=cost(0, 16 * blocks[0].size, scale=SHORT if scale is None else scale),
        name="place_blocks",
    )(order, *blocks, *extra)


def on_device(
    tokens, lengths, memory, gains, self_qkv, self_out, cross_q, cross_kv, cross_out, fc_in, fc_out, out_grad
):
    clips, seq, width = tokens.shape
    wide = lax.axis_size("wide")
    narrow = lax.axis_size("narrow")
    me = lax.axis_index("narrow")
    place = lax.axis_index("wide")
    bits = ((place >> jnp.arange(8)) & 1).astype(jnp.int32)
    share = memory.shape[1]
    local = self_qkv.shape[2]
    depth = width // wide
    order = (me ^ jnp.arange(4)).astype(jnp.int32)
    near_order = (me ^ jnp.array([1, 0])).astype(jnp.int32)
    far_order = (me ^ jnp.array([3, 2])).astype(jnp.int32)
    then = Order()

    by_clip = memory.reshape(wide, narrow, share, width)
    first = -(-share // SPLIT) * 16
    sizes = (first, share - first)
    starts = (0, first)
    last = AUDIO - (wide - 1) * share
    valid = [(wide - 1) * size + min(max(last - start, 0), size) for start, size in zip(starts, sizes)]

    def encoder_rows(part, *arrived):
        block = encode(then(order), by_clip, gains, starts[part], sizes[part], LONG if part else None)
        block, *arrived = then.join(block, *arrived)
        block = lax.all_to_all(block, "wide", 0, 0, tiled=True)
        return block.reshape(wide * sizes[part], width), *arrived

    (encoded_first,) = encoder_rows(0)
    self_qkv = self_qkv.transpose(0, 2, 1)
    pack_kv = cross_kv.transpose(0, 2, 1).reshape(2 * local, width)
    packs_one = gather_narrow(jnp.concatenate((self_out, then(cross_q).T)))

    normed_far, qkv_far, mixed_three, mixed_two, lse_far = self_fwd(
        then(far_order), lengths, tokens, gains, self_qkv
    )
    then.last = mixed_two
    mix_two = swap(mixed_two, "narrow", 2)
    crossing = swap(mixed_three, "narrow", 1)
    normed_near, qkv_near, mixed_one, mixed_zero, lse_near = self_fwd(
        then(near_order), lengths, tokens, gains, self_qkv, LONG
    )
    mixed_one, mixed_zero, mix_two, crossing, *packs_one = then.join(
        mixed_one, mixed_zero, mix_two, crossing, *packs_one
    )
    mix_one, mix_three = swap(mixed_one, "narrow", 1), swap(crossing, "narrow", 2)
    packs_one = packs_one + [swap(packs_one[2], "narrow", 1)]
    encoded_second, mix_one, mix_three, *packs_one = encoder_rows(1, mix_one, mix_three, *packs_one)
    encoded = (encoded_first, encoded_second)
    packs_kv = gather_narrow(then(pack_kv))
    mixes = [mixed_zero, mix_one, mix_two, mix_three]
    after_self, normed_two, query = to_query(then(order), tokens, mixes, packs_one, gains)
    query, *packs_kv = then.join(query, *packs_kv)
    packs_kv = packs_kv + [swap(packs_kv[2], "narrow", 1)]
    packs_out = gather_narrow(then(cross_out))
    kv_first, *before = cross_first(then(query), encoded_first, packs_kv, valid[0])
    then.last = kv_first
    packs_out = finish(packs_out, then)
    kv_second, cross_mixed, cross_lse, after_cross, normed_three = cross_second(
        query, encoded_second, packs_kv, packs_out, valid[1], before, after_self, gains
    )
    then.last = normed_three

    rows = gather_narrow(normed_three)
    hidden_a, pre_a, live_a, part_zero, feed_zero, part_one, feed_one = feed_forward(
        order[:2], lengths, rows[:2], out_grad, fc_in, fc_out
    )
    then.last = part_one
    rows = finish(rows, then)
    part_near = swap(part_one, "narrow", 1)
    feed_near = swap(feed_one, "narrow", 1)
    hidden_c, pre_c, live_c, part_three, feed_three = feed_forward(
        order[3:], lengths, rows[3:], out_grad, fc_in, fc_out
    )
    then.last = part_three
    part_cross = swap(part_three, "narrow", 1)
    feed_cross = swap(feed_three, "narrow", 1)
    hidden_b, pre_b, live_b, part_two, feed_two = feed_forward(
        then(order[2:3]), lengths, rows[2:3], out_grad, fc_in, fc_out
    )
    part_far = (part_two.astype(F32) + part_cross.astype(F32)).astype(BF16)
    then.last = part_far
    part_far = swap(part_far, "narrow", 2)
    feed_keep, feed_give = feed_weights(
        then(bits, part_near, feed_near, feed_cross),
        rows, (pre_a, pre_b, pre_c), (live_a, live_b, live_c), (hidden_a, hidden_b, hidden_c), wide,
    )
    then.last = feed_give
    feed_far = (then(feed_two).astype(F32) + feed_cross.astype(F32)).astype(BF16)
    then.last = feed_far
    feed_far = swap(then(feed_far, part_far), "narrow", 2)
    feed_got = swap(feed_give, "wide", 1)

    grad_cross, grad_two, grad_mixed, gain_three, dq, dkv_first, frames_first = cross_first_back(
        then(order), lengths, out_grad, (part_zero, part_near, part_far), after_cross, gains,
        packs_kv, packs_out, query, kv_first, cross_mixed, cross_lse, valid[0],
    )
    then.last = dkv_first

    def frames_sent(block, part):
        block = block.reshape(wide, sizes[part], width)
        return lax.all_to_all(block, "wide", 0, 0, tiled=True)

    frames_first = frames_sent(frames_first, 0)
    block_own = (
        then(after_cross) + (feed_zero.astype(F32) + feed_near.astype(F32) + feed_far.astype(F32))
    ).astype(BF16)
    then.last = block_own
    block_all = gather_narrow(block_own)
    view = (2 * (wide // 4), 2, depth, width)
    feed_keep, feed_give = merge(then(bits), (1,), (feed_keep.reshape(view), feed_got.reshape(view)))
    then.last = feed_keep
    feed_got = swap(feed_give, "wide", 2)
    dq, dkv_second, frames_second, grad_self, grad_one, head0, head1, head2, head3, gain_two = cross_second_back(
        query, kv_second, grad_mixed, cross_mixed, cross_lse, dq, packs_kv, packs_one, after_self,
        then(gains), grad_cross, valid[1],
    )
    then.last = dq
    head1, head2, head3, frames_second, feed_got, *block_all = then.join(
        head1, head2, head3, frames_second, feed_got, *block_all
    )
    feed_view = (2 * (wide // 8), 2, depth, width)
    feed_keep, feed_give = merge(
        then(bits), (2,), (feed_keep.reshape(feed_view), feed_got.reshape(feed_view)), scale=SHORT
    )
    feed_give, head1, head2, head3 = then.join(feed_give, head1, head2, head3)
    feed_got = swap(feed_give, "wide", 4)
    heads_one = swap(head1, "narrow", 1)
    heads_two = swap(head2, "narrow", 2)
    head3 = swap(head3, "narrow", 2)
    block_all = block_all + [swap(block_all[2], "narrow", 1)]
    frames_second = frames_sent(frames_second, 1)

    keep, give = head_weights(
        encoded, (dkv_first, dkv_second), then(normed_two), dq, grad_two, cross_mixed, LONG
    )
    give, keep, heads_one, heads_two, head3, feed_got, *block_all = then.join(
        give, keep, heads_one, heads_two, head3, feed_got, *block_all
    )
    got = swap(give, "narrow", 1)
    heads_three = swap(head3, "narrow", 1)
    back_first, gain_first = memory_back(then(order), by_clip, gains, frames_first, starts[0], SHORT)
    then.last = back_first
    back_first = gather_narrow(back_first)

    *dqkv_near, part_one, part_zero = self_bwd(
        then(near_order), lengths, qkv_near, mixed_one, mixed_zero, lse_near, heads_one, head0, self_qkv, SHORT
    )
    part_one, got, heads_three = then.join(part_one, got, heads_three)
    part_near = swap(part_one, "narrow", 1)
    view = (2, wide, depth, width)
    keep_a, give_a, keep_b, give_b = merge_heads(then(bits), keep.reshape(view), got.reshape(view))
    then.last = give_a
    got_a, got_b = swap(give_a, "wide", 1), swap(give_b, "wide", 2)
    self_keep, self_give = out_weights(then(grad_one), mixes, MID)
    then.last = self_give
    self_got = swap(self_give, "narrow", 1)
    *dqkv_far, part_three, part_two = self_bwd(
        then(far_order), lengths, qkv_far, mixed_three, mixed_two, lse_far, heads_three, heads_two, self_qkv, MID
    )
    part_three, part_two, self_got, frames_second, *back_first = then.join(
        part_three, part_two, self_got, frames_second, *back_first
    )
    part_cross = swap(part_three, "narrow", 1)
    back_first = back_first + [swap(back_first[2], "narrow", 1)]
    self_other = (then(self_keep)[1].astype(F32) + self_got[1].astype(F32)).astype(BF16)
    then.last = self_other
    self_other = swap(self_other, "narrow", 2)
    feed_keep, feed_got = scatter_wide(bits, then, feed_keep, feed_give, 3, feed_got)
    feed_grads = feed_keep.astype(F32) + feed_got.astype(F32)
    back_second, gain_second = memory_back(then(order), by_clip, gains, frames_second, starts[1], LONG)
    back_second, part_two, part_cross, part_near, *back_first = then.join(
        back_second, part_two, part_cross, part_near, *back_first
    )
    part_far = (then(part_two).astype(F32) + part_cross.astype(F32)).astype(BF16)
    then.last = part_far
    part_far = swap(part_far, "narrow", 2)
    self_keep, self_give = self_weights(
        then(bits), normed_near, normed_far, *dqkv_near, *dqkv_far, self_keep, self_got, self_other, wide, LONG
    )
    then.last = self_give
    self_got = swap(self_give, "wide", 1)
    view = (wide // 4, 2, depth, width)
    pair = lambda keep, got: (keep.reshape(view), got.reshape(view))
    keep_a, give_a, keep_b, give_b = merge(then(bits), (1, 0), pair(keep_a, got_a), pair(keep_b, got_b), scale=SHORT)
    then.last = give_a
    got_a, got_b = swap(give_a, "wide", 2), swap(give_b, "wide", 1)
    tokens_own, gain_one = to_tokens_grad(
        then(order), tokens, part_zero, part_near, part_far, grad_self, gains, LONG
    )
    then.last = tokens_own
    tokens_all = gather_narrow(tokens_own)
    gain_terms = jnp.concatenate((gain_first + gain_second, gain_one, gain_two, gain_three))
    gain_other = swap(gain_terms, "wide", 1)
    block_out = place_blocks(then(order), block_all, (clips, seq, width), scale=LONG)
    block_out, self_got, gain_other, gain_terms = then.join(block_out, self_got, gain_other, gain_terms)
    gain_terms = gain_terms + gain_other
    gain_other = swap(gain_terms, "wide", 2)
    self_keep, self_give = merge(then(bits), (1,), pair(self_keep, self_got), scale=SHORT)
    then.last = self_give
    self_got = swap(self_give, "wide", 2)
    view = (wide // 8, 2, depth, width)
    keep, give = merge(
        then(bits), (2, 2, 2), pair(keep_a, got_a), pair(keep_b, got_b), pair(self_keep, self_got), scale=SHORT, joined=True
    )
    give, keep, back_second, gain_other, gain_terms, *tokens_all = then.join(
        give, keep, back_second, gain_other, gain_terms, *tokens_all
    )
    got = swap(give, "wide", 4)
    back_second = gather_narrow(back_second)
    tokens_all = tokens_all + [swap(tokens_all[2], "narrow", 1)]
    gain_terms = gain_terms + gain_other
    gain_other = swap(gain_terms, "wide", 4)
    memory_grad = place_blocks(
        then(order), back_first, (wide, narrow, share, width), starts[0], scale=LONG
    )
    memory_grad, *tokens_all = then.join(memory_grad, *tokens_all)
    tokens_grad = place_blocks(then(order), tokens_all, (clips, seq, width))
    tokens_grad, got, gain_other, gain_terms, *back_second = then.join(
        tokens_grad, got, gain_other, gain_terms, *back_second
    )
    back_second = back_second + [swap(back_second[2], "narrow", 1)]
    gain_terms = gain_terms + gain_other
    bit = 8
    while bit < wide:
        gain_terms = gain_terms + swap(gain_terms, "wide", bit)
        bit *= 2
    gain_terms = lax.dynamic_slice_in_dim(gain_terms, place * depth, depth, 1)
    gain_others = [swap(gain_terms, "narrow", distance) for distance in (1, 2, 3)]
    keep, got = scatter_wide(bits, then, keep, give, 3, got)
    give, head_grads, qkv_grad, self_out_grad = finish_self(keep, then(got))
    then.last = give
    other = swap(give, "narrow", 2)
    memory_grad = place_blocks(
        then(order), back_second, (wide, narrow, share, width), starts[1], memory_grad, scale=LONG
    )
    memory_grad, other, gain_terms, *gain_others = then.join(memory_grad, other, gain_terms, *gain_others)
    gain_terms = gain_terms + gain_others[0] + gain_others[1] + gain_others[2]
    kv_grad, query_grad, cross_out_grad = finish_heads(head_grads, other)
    return (
        block_out,
        tokens_grad,
        memory_grad.reshape(memory.shape),
        gain_terms,
        qkv_grad,
        self_out_grad,
        query_grad,
        kv_grad,
        cross_out_grad,
        feed_grads[0],
        feed_grads[1].T,
    )


def solution(mesh):
    placed = (
        P("wide", None, None),
        P("wide"),
        P(None, "wide", None),
        P(),
        P(None, None, "narrow"),
        P("narrow", None),
        P(None, "narrow"),
        P(None, None, "narrow"),
        P("narrow", None),
        P(None, "narrow"),
        P("narrow", None),
        P("wide", None, None),
    )
    return jax.shard_map(
        on_device,
        mesh=mesh,
        in_specs=placed,
        out_specs=(
            P("wide", None, None),
            P("wide", None, None),
            P(None, "wide", None),
            P(None, "wide"),
            P(None, "wide", "narrow"),
            P("narrow", "wide"),
            P("wide", "narrow"),
            P(None, "wide", "narrow"),
            P("narrow", "wide"),
            P("wide", "narrow"),
            P("narrow", "wide"),
        ),
        check_vma=False,
    )
```

```python
import functools

import jax
import jax.numpy as jnp
from jax import lax
from jax.experimental import pallas as pl
from jax.experimental.pallas import tpu as pltpu
from jax.sharding import PartitionSpec as P

HEAD_DIM = 64
AUDIO = 1500
EPSILON = 1e-05
NEG_FILL = -1e30
INV_ROOT = HEAD_DIM**-0.5
F32 = jnp.float32
BF16 = jnp.bfloat16
VMEM_LIMIT = 52 << 20
COST_SCALE = 1.0
LONG = 50.0
SHORT = 1e-6
MID = 1e-6
SPLIT = 32


def dot(left, right, left_dim=1, right_dim=0):
    return lax.dot_general(
        left, right, (((left_dim,), (right_dim,)), ((), ())), preferred_element_type=F32
    )


def call(body, grid, in_specs, out_specs, out_shape, name, estimate, prefetch=0, scratch=()):
    return pl.pallas_call(
        body,
        grid_spec=pltpu.PrefetchScalarGridSpec(
            num_scalar_prefetch=prefetch,
            grid=grid,
            in_specs=in_specs,
            out_specs=out_specs,
            scratch_shapes=list(scratch),
        ),
        out_shape=out_shape,
        compiler_params=pltpu.CompilerParams(vmem_limit_bytes=VMEM_LIMIT),
        cost_estimate=estimate,
        name=name,
    )


def shape(dims, dtype=BF16):
    return jax.ShapeDtypeStruct(dims, dtype)


def cost(flops, moved, exps=0, scale=None):
    scale = COST_SCALE if scale is None else scale
    return pl.CostEstimate(
        flops=int(flops * scale), bytes_accessed=int(moved * scale), transcendentals=int(exps * scale)
    )


def whole(shape):
    return pl.BlockSpec(shape, lambda *_: (0,) * len(shape))


def norm_stats(values):
    center = values - jnp.mean(values, axis=-1, keepdims=True)
    spread = jnp.mean(center * center, axis=-1, keepdims=True)
    inverse = lax.rsqrt(spread + EPSILON)
    return center * inverse, inverse


def norm_back(unit, inverse, gains_all, grad):
    scaled = grad * gains_all
    first = jnp.mean(scaled, axis=-1, keepdims=True)
    second = jnp.mean(scaled * unit, axis=-1, keepdims=True)
    return (scaled - first - unit * second) * inverse


def swap(values, axis, bit):
    size = lax.axis_size(axis)
    return lax.ppermute(values, axis, [(i, i ^ bit) for i in range(size)])


def gather_narrow(own):
    other = swap(own, "narrow", 2)
    return [own, swap(own, "narrow", 1), other]


def finish(blocks, then):
    return blocks + [swap(then(blocks[2]), "narrow", 1)]


class Order:
    def __init__(self):
        self.last = None

    def __call__(self, item, *named):
        named = named if self.last is None else named + (self.last,)
        if named:
            item, _ = lax.optimization_barrier((item, named))
        return item

    def join(self, *items):
        items = lax.optimization_barrier(items)
        self.last = items[0]
        return items


def encode_body(order, memory_ref, gain_ref, out_ref):
    unit, _ = norm_stats(memory_ref[:, 0].astype(F32))
    out_ref[...] = (unit * gain_ref[0 : 1]).astype(BF16)


def encode(order, memory, gains_all, start, size, scale=None):
    wide, _, _, width = memory.shape
    group = min(4, wide)
    return call(
        encode_body,
        (wide // group,),
        [
            pl.BlockSpec((group, 1, size, width), lambda i, order: (i, order[0], start // size, 0)),
            whole(gains_all.shape),
        ],
        pl.BlockSpec((group, size, width), lambda i, *_: (i, 0, 0)),
        shape((wide, size, width)),
        "encode",
        cost(0, 4 * wide * size * width, scale=scale),
        prefetch=1,
    )(order, memory, gains_all)


def memory_back_body(order, memory_ref, gain_ref, grad_ref, out_ref, gain_out):
    unit, inverse = norm_stats(memory_ref[:, 0].astype(F32))
    grad = grad_ref[...].astype(F32)
    out_ref[...] = norm_back(unit, inverse, gain_ref[0 : 1], grad).astype(BF16)

    @pl.when(pl.program_id(0) == 0)
    def _():
        gain_out[...] = jnp.zeros_like(gain_out)

    gain_out[...] += jnp.sum(jnp.sum(grad * unit, axis=0), axis=0, keepdims=True)


def memory_back(order, memory, gains_all, grad, start, scale):
    wide, _, _, width = memory.shape
    size = grad.shape[1]
    group = min(4, wide)
    rows = pl.BlockSpec((group, size, width), lambda i, *_: (i, 0, 0))
    return call(
        memory_back_body,
        (wide // group,),
        [
            pl.BlockSpec((group, 1, size, width), lambda i, order: (i, order[0], start // size, 0)),
            whole(gains_all.shape),
            rows,
        ],
        [rows, whole((1, width))],
        [shape((wide, size, width)), shape((1, width), F32)],
        "memory_back",
        cost(0, 6 * wide * size * width, scale=scale),
        prefetch=1,
    )(order, memory, gains_all, grad)


def self_fwd_body(order, lengths, token_ref, gain_ref, weight_ref, normed_ref, qkv_ref, first_ref, second_ref, lse_ref):
    seq = token_ref.shape[1]
    heads = weight_ref.shape[1] // HEAD_DIM
    step = pl.program_id(0)
    length = lengths[order[step]]
    unit, _ = norm_stats(token_ref[0].astype(F32))
    normed = (unit * gain_ref[1 : 2]).astype(BF16)
    normed_ref[0] = normed
    for i in range(3):
        qkv_ref[0, i] = dot(normed, weight_ref[i], 1, 1).astype(BF16)
    cut = 256 if seq > 256 else seq
    mixed = []
    for h in range(heads):
        columns = slice(h * HEAD_DIM, (h + 1) * HEAD_DIM)
        parts = []
        for start, stop in ((0, cut), (cut, seq)):
            if start == stop:
                continue
            queries = qkv_ref[0, 0, start:stop, columns] * jnp.asarray(INV_ROOT, BF16)
            scores = dot(qkv_ref[0, 1, :stop, columns], queries, 1, 1)
            key = lax.broadcasted_iota(jnp.int32, scores.shape, 0)
            query = lax.broadcasted_iota(jnp.int32, scores.shape, 1) + start
            scores = jnp.where((key <= query) & (key < length), scores, NEG_FILL)
            top = jnp.max(scores, axis=0, keepdims=True)
            probs = jnp.exp(scores - top)
            total = jnp.sum(probs, axis=0, keepdims=True)
            out = dot(qkv_ref[0, 2, :stop, columns], probs.astype(BF16), 0, 0) / total
            parts.append(out.T)
            lse_ref[0, h : h + 1, start:stop] = top + jnp.log(total)
        mixed.append(jnp.concatenate(parts, axis=0))
    mixed = jnp.concatenate(mixed, axis=1).astype(BF16)

    @pl.when(step == 0)
    def _():
        first_ref[...] = mixed

    @pl.when(step == 1)
    def _():
        second_ref[...] = mixed


def self_fwd(order, lengths, tokens, gains_all, weights, scale=None):
    _, seq, width = tokens.shape
    local = weights.shape[1]
    heads = local // HEAD_DIM
    return call(
        self_fwd_body,
        (2,),
        [
            pl.BlockSpec((1, seq, width), lambda i, order, lengths: (order[i], 0, 0)),
            whole(gains_all.shape),
            whole((3, local, width)),
        ],
        [
            pl.BlockSpec((1, seq, width), lambda i, *_: (i, 0, 0)),
            pl.BlockSpec((1, 3, seq, local), lambda i, *_: (i, 0, 0, 0)),
            whole((seq, local)),
            whole((seq, local)),
            pl.BlockSpec((1, heads, seq), lambda i, *_: (i, 0, 0)),
        ],
        [
            shape((2, seq, width)),
            shape((2, 3, seq, local)),
            shape((seq, local)),
            shape((seq, local)),
            shape((2, heads, seq), F32),
        ],
        "self_forward",
        cost(2 * (6 * seq * width * local + 8 * seq * seq * local), 2 * seq * width * 8, 2 * heads * seq * seq, scale=scale),
        prefetch=2,
    )(order, lengths, tokens, gains_all, weights)


def self_bwd_body(
    order, lengths, qkv_ref, mixed0_ref, mixed1_ref, lse_ref, grad0_ref, grad1_ref, weight_ref,
    dq_ref, dkv_ref, first_ref, second_ref,
):
    seq = qkv_ref.shape[2]
    local = weight_ref.shape[1]
    heads = local // HEAD_DIM
    step = pl.program_id(0)
    length = lengths[order[step]]
    grad = jnp.where(step == 0, grad0_ref[...], grad1_ref[...])
    mixed = jnp.where(step == 0, mixed0_ref[...], mixed1_ref[...])
    inner = grad.astype(F32) * mixed.astype(F32)
    totals = jnp.concatenate((lse_ref[0], jnp.zeros((8 - heads % 8, seq), F32)), axis=0).T
    cut = 256 if seq > 256 else seq
    for h in range(heads):
        columns = slice(h * HEAD_DIM, (h + 1) * HEAD_DIM)
        keys = qkv_ref[0, 1, :, columns]
        values = qkv_ref[0, 2, :, columns]
        dq_parts = []
        dk, dv = 0.0, 0.0
        for start, stop in ((0, cut), (cut, seq)):
            if start == stop:
                continue
            queries = qkv_ref[0, 0, start:stop, columns] * jnp.asarray(INV_ROOT, BF16)
            grads = grad[start:stop, columns]
            scores = dot(queries, keys[:stop], 1, 1)
            key = lax.broadcasted_iota(jnp.int32, scores.shape, 1)
            query = lax.broadcasted_iota(jnp.int32, scores.shape, 0) + start
            allowed = (key <= query) & (key < length)
            probs = jnp.exp(jnp.where(allowed, scores, NEG_FILL) - totals[start:stop, h : h + 1])
            dp = dot(grads, values[:stop], 1, 1)
            centre = jnp.sum(inner[start:stop, columns], axis=1, keepdims=True)
            ds = (probs * (dp - centre)).astype(BF16)
            dk_now = dot(queries, ds, 0, 0)
            dv_now = dot(grads, probs.astype(BF16), 0, 0)
            if stop < seq:
                pad = jnp.zeros((HEAD_DIM, seq - stop), F32)
                dk_now = jnp.concatenate((dk_now, pad), axis=1)
                dv_now = jnp.concatenate((dv_now, pad), axis=1)
            dk, dv = dk + dk_now, dv + dv_now
            dq_parts.append(dot(ds, keys[:stop]) * INV_ROOT)
        dq_ref[0, :, columns] = jnp.concatenate(dq_parts, axis=0).astype(BF16)
        dkv_ref[0, columns, :] = dk.astype(BF16)
        dkv_ref[0, local + h * HEAD_DIM : local + (h + 1) * HEAD_DIM, :] = dv.astype(BF16)
    total = dot(dq_ref[0], weight_ref[0])
    total = total + dot(dkv_ref[0, :local, :], weight_ref[1], 0, 0)
    total = (total + dot(dkv_ref[0, local:, :], weight_ref[2], 0, 0)).astype(BF16)

    @pl.when(step == 0)
    def _():
        first_ref[...] = total

    @pl.when(step == 1)
    def _():
        second_ref[...] = total


def self_bwd(order, lengths, qkv, mixed0, mixed1, lse, grad0, grad1, weights, scale):
    _, _, seq, local = qkv.shape
    width = weights.shape[2]
    heads = local // HEAD_DIM
    return call(
        self_bwd_body,
        (2,),
        [
            pl.BlockSpec((1, 3, seq, local), lambda i, *_: (i, 0, 0, 0)),
            whole((seq, local)),
            whole((seq, local)),
            pl.BlockSpec((1, heads, seq), lambda i, *_: (i, 0, 0)),
            whole((seq, local)),
            whole((seq, local)),
            whole((3, local, width)),
        ],
        [
            pl.BlockSpec((1, seq, local), lambda i, *_: (i, 0, 0)),
            pl.BlockSpec((1, 2 * local, seq), lambda i, *_: (i, 0, 0)),
            whole((seq, width)),
            whole((seq, width)),
        ],
        [shape((2, seq, local)), shape((2, 2 * local, seq)), shape((seq, width)), shape((seq, width))],
        "self_backward",
        cost(2 * (6 * seq * width * local + 20 * seq * seq * local), 2 * seq * width * 8, 2 * heads * seq * seq, scale=scale),
        prefetch=2,
    )(order, lengths, qkv, mixed0, mixed1, lse, grad0, grad1, weights)


def to_query_body(order, token_ref, m0, m1, m2, m3, p0, p1, p2, p3, gain_ref, after_ref, normed_ref, query_ref):
    local = m0.shape[1]
    rows = token_ref[0].astype(F32)
    for mixed, pack in ((m0, p0), (m1, p1), (m2, p2), (m3, p3)):
        rows = rows + dot(mixed[...], pack[:local])
    after_ref[...] = rows
    unit, _ = norm_stats(rows)
    normed = (unit * gain_ref[2 : 3]).astype(BF16)
    normed_ref[...] = normed
    for r, pack in enumerate((p0, p1, p2, p3)):
        query = dot(normed, pack[local:], 1, 1).astype(BF16)
        query_ref[r // 2, :, (r % 2) * local : (r % 2 + 1) * local] = query


def to_query(order, tokens, mixes, packs, gains_all):
    _, seq, width = tokens.shape
    local = mixes[0].shape[1]
    tile = seq // 2
    return call(
        to_query_body,
        (2,),
        [pl.BlockSpec((1, tile, width), lambda i, order: (order[0], i, 0))]
        + [pl.BlockSpec((tile, local), lambda i, *_: (i, 0))] * 4
        + [whole((2 * local, width))] * 4
        + [whole(gains_all.shape)],
        [
            pl.BlockSpec((tile, width), lambda i, *_: (i, 0)),
            pl.BlockSpec((tile, width), lambda i, *_: (i, 0)),
            pl.BlockSpec((2, tile, 2 * local), lambda i, *_: (0, i, 0)),
        ],
        [shape((seq, width), F32), shape((seq, width)), shape((2, seq, 2 * local))],
        "self_out_to_query",
        cost(4 * seq * width * width, seq * width * 12 + 4 * width * width),
        prefetch=1,
    )(order, tokens, *mixes, *packs, gains_all)


def head_places(local):
    for r in range(2):
        for h in range(local // HEAD_DIM):
            at = r * local + h * HEAD_DIM
            key = 2 * r * local + h * HEAD_DIM
            yield (
                at // HEAD_DIM,
                slice(at, at + HEAD_DIM),
                slice(key, key + HEAD_DIM),
                slice(key + local, key + local + HEAD_DIM),
            )


def cross_first_body(query_ref, encoded_ref, w0, w1, w2, w3, kv_ref, acc_ref, top_ref, total_ref, *, valid):
    make_keys_values(encoded_ref, (w0, w1, w2, w3), kv_ref)
    frames = kv_ref.shape[0]
    for head, columns, key, value in head_places(query_ref.shape[2] // 2):
        queries = query_ref[0, :, columns] * jnp.asarray(INV_ROOT, BF16)
        scores = dot(kv_ref[:, key], queries, 1, 1)
        if valid < frames:
            frame = lax.broadcasted_iota(jnp.int32, scores.shape, 0)
            scores = jnp.where(frame < valid, scores, NEG_FILL)
        top = jnp.max(scores, axis=0, keepdims=True)
        probs = jnp.exp(scores - top)
        acc_ref[0, columns, :] = dot(kv_ref[:, value], probs.astype(BF16), 0, 0)
        top_ref[0, head : head + 1, :] = top
        total_ref[0, head : head + 1, :] = jnp.sum(probs, axis=0, keepdims=True)


def make_keys_values(encoded_ref, weights, kv_ref):
    pair = weights[0].shape[0]
    for step in range(2):

        @pl.when(pl.program_id(0) == step)
        def _():
            for r in range(2):
                kv = dot(encoded_ref[...], weights[2 * step + r][...], 1, 1)
                kv_ref[:, r * pair : (r + 1) * pair] = kv.astype(BF16)


def cross_second_body(
    query_ref, encoded_ref, w0, w1, w2, w3, acc_in, top_in, total_in, after_ref, o0, o1, o2, o3, gain_ref,
    kv_ref, mixed_ref, lse_ref, next_ref, normed_ref, *, valid,
):
    make_keys_values(encoded_ref, (w0, w1, w2, w3), kv_ref)
    frames = kv_ref.shape[0]
    local = o0.shape[0]
    for head, columns, key, value in head_places(local):
        queries = query_ref[0, :, columns] * jnp.asarray(INV_ROOT, BF16)
        scores = dot(kv_ref[:, key], queries, 1, 1)
        if valid < frames:
            frame = lax.broadcasted_iota(jnp.int32, scores.shape, 0)
            scores = jnp.where(frame < valid, scores, NEG_FILL)
        before = top_in[0, head : head + 1, :]
        top = jnp.maximum(jnp.max(scores, axis=0, keepdims=True), before)
        probs = jnp.exp(scores - top)
        fade = jnp.exp(before - top)
        total = jnp.sum(probs, axis=0, keepdims=True) + total_in[0, head : head + 1, :] * fade
        out = dot(kv_ref[:, value], probs.astype(BF16), 0, 0) + acc_in[0, columns, :] * fade
        mixed_ref[0, :, columns] = (out / total).T.astype(BF16)
        lse_ref[0, head : head + 1, :] = top + jnp.log(total)
    outs = (o0, o1, o2, o3)
    for step in range(2):

        @pl.when(pl.program_id(0) == step)
        def _():
            rows = after_ref[...] if step == 0 else next_ref[...]
            for r in range(2):
                rows = rows + dot(mixed_ref[0, :, r * local : (r + 1) * local], outs[2 * step + r][...])
            next_ref[...] = rows
            if step == 1:
                unit, _ = norm_stats(rows)
                normed_ref[...] = (unit * gain_ref[3 : 4]).astype(BF16)


def pack_specs(packs, rows, index):
    width = packs[0].shape[1]
    return [pl.BlockSpec((rows, width), lambda *_: (index, 0))] * 4


def cross_first(query, encoded, packs, valid):
    _, seq, pair = query.shape
    frames, width = encoded.shape
    heads = pair // HEAD_DIM
    stats = pl.BlockSpec((1, heads, seq), lambda i: (i, 0, 0))
    return call(
        functools.partial(cross_first_body, valid=valid),
        (2,),
        [pl.BlockSpec((1, seq, pair), lambda i: (i, 0, 0)), whole((frames, width))] + pack_specs(packs, pair, 0),
        [
            pl.BlockSpec((frames, 2 * pair), lambda i: (0, i)),
            pl.BlockSpec((1, pair, seq), lambda i: (i, 0, 0)),
            stats,
            stats,
        ],
        [
            shape((frames, 4 * pair)),
            shape((2, pair, seq), F32),
            shape((2, heads, seq), F32),
            shape((2, heads, seq), F32),
        ],
        "cross_first",
        cost(4 * frames * width * width + 40 * seq * frames * pair, 8 * frames * width, 2 * heads * seq * frames),
    )(query, encoded, *packs)


def cross_second(query, encoded, packs, packs_out, valid, before, after, gains_all):
    _, seq, pair = query.shape
    frames, width = encoded.shape
    heads = pair // HEAD_DIM
    rows = pl.BlockSpec((1, seq, pair), lambda i: (i, 0, 0))
    stats = pl.BlockSpec((1, heads, seq), lambda i: (i, 0, 0))
    acc = pl.BlockSpec((1, pair, seq), lambda i: (i, 0, 0))
    return call(
        functools.partial(cross_second_body, valid=valid),
        (2,),
        [rows, whole((frames, width))]
        + pack_specs(packs, pair, 0)
        + [acc, stats, stats, whole((seq, width))]
        + pack_specs(packs_out, pair // 2, 0)
        + [whole(gains_all.shape)],
        [pl.BlockSpec((frames, 2 * pair), lambda i: (0, i)), rows, stats, whole((seq, width)), whole((seq, width))],
        [
            shape((frames, 4 * pair)),
            shape((2, seq, pair)),
            shape((2, heads, seq), F32),
            shape((seq, width), F32),
            shape((seq, width)),
        ],
        "cross_second",
        cost(4 * frames * width * width + 40 * seq * frames * pair, 10 * frames * width, 2 * heads * seq * frames),
    )(query, encoded, *packs, *before, after, *packs_out, gains_all)


def feed_body(order, lengths, *refs, count):
    row_refs, (grad_ref, in_ref, out_ref, hidden_ref, pre_ref, live_ref) = refs[:count], refs[count : count + 6]
    outs = refs[count + 6 :]
    step = pl.program_id(0)
    tile = grad_ref.shape[1]
    rows = row_refs[0][...]
    if count == 2:
        rows = jnp.where(step == 0, rows, row_refs[1][...])
    place = lax.broadcasted_iota(jnp.int32, grad_ref.shape[1:], 0) + pl.program_id(1) * tile
    grads = jnp.where(place < lengths[order[step]], grad_ref[0], jnp.zeros((), BF16))
    live_ref[0] = grads
    pre = dot(rows, in_ref[...])
    half = 0.5 * (1.0 + lax.erf(pre * (0.5**0.5)))
    hidden = (pre * half).astype(BF16)
    slope = half + pre * jnp.exp(-0.5 * pre * pre) * 0.3989422804014327
    hidden_ref[0] = hidden
    grad_pre = (dot(grads, out_ref[...], 1, 1) * slope).astype(BF16)
    pre_ref[0] = grad_pre
    part = dot(grad_pre, in_ref[...], 1, 1).astype(BF16)
    feed = dot(hidden, out_ref[...]).astype(BF16)
    for i in range(count):

        @pl.when(step == i)
        def _():
            outs[2 * i][...] = part
            outs[2 * i + 1][...] = feed


def feed_forward(order, lengths, rows, out_grad, fc_in, fc_out):
    count = len(rows)
    seq, width = rows[0].shape
    units = fc_in.shape[1]
    tiles = 2
    tile = seq // tiles
    block = lambda last: pl.BlockSpec((1, tile, last), lambda i, j, *_: (i, j, 0))
    single = [
        pl.BlockSpec((tile, width), lambda i, j, *_: (jnp.where(i == 0, j, tiles - 1), 0)),
        pl.BlockSpec((tile, width), lambda i, j, *_: (jnp.where(i == 0, 0, j), 0)),
    ]
    if count == 1:
        single = [pl.BlockSpec((tile, width), lambda i, j, *_: (j, 0))]
    return call(
        functools.partial(feed_body, count=count),
        (count, tiles),
        single
        + [
            pl.BlockSpec((1, tile, width), lambda i, j, order, lengths: (order[i], j, 0)),
            whole((width, units)),
            whole((units, width)),
        ],
        [block(units), block(units), block(width)] + [spec for spec in single for _ in range(2)],
        [shape((count, seq, units)), shape((count, seq, units)), shape((count, seq, width))]
        + [shape((seq, width))] * (2 * count),
        "feed_forward",
        cost(8 * count * seq * width * units, count * seq * width * 14, 2 * count * seq * units),
        prefetch=2,
    )(order, lengths, *rows, out_grad, fc_in, fc_out)


def add_gain(gain_out, term):
    @pl.when(pl.program_id(0) == 0)
    def _():
        gain_out[...] = jnp.zeros_like(gain_out)

    gain_out[...] += term


def cross_back(queries_ref, kv_ref, grads_ref, mixed_ref, lse_ref, dkv_ref, local, valid, store):
    frames = kv_ref.shape[0]
    inner = grads_ref.astype(F32) * mixed_ref[0].astype(F32)
    heads, seq = lse_ref.shape[1:]
    totals = jnp.concatenate((lse_ref[0], jnp.zeros((8 - heads % 8, seq), F32)), axis=0).T
    for head, columns, key, value in head_places(local):
        queries = queries_ref[0, :, columns] * jnp.asarray(INV_ROOT, BF16)
        grads = grads_ref[:, columns]
        centre = jnp.sum(inner[:, columns], axis=1, keepdims=True)
        keys = kv_ref[:, key]
        probs = jnp.exp(dot(queries, keys, 1, 1) - totals[:, head : head + 1])
        if valid < frames:
            frame = lax.broadcasted_iota(jnp.int32, probs.shape, 1)
            probs = jnp.where(frame < valid, probs, 0.0)
        dp = dot(grads, kv_ref[:, value], 1, 1)
        ds = (probs * (dp - centre)).astype(BF16)
        dkv_ref[value, :] = dot(grads, probs.astype(BF16), 0, 0).astype(BF16)
        dkv_ref[key, :] = dot(queries, ds, 0, 0).astype(BF16)
        store(columns, dot(ds, keys))


def encoded_back(dkv_ref, weights, out_ref, acc):
    pair = weights[0].shape[0]
    for step in range(2):

        @pl.when(pl.program_id(0) == step)
        def _():
            total = dot(dkv_ref[:pair, :], weights[2 * step][...], 0, 0)
            total = total + dot(dkv_ref[pair:, :], weights[2 * step + 1][...], 0, 0)
            if step == 0:
                acc[...] = total
            else:
                out_ref[...] = (acc[...] + total).astype(BF16)


def cross_first_back_body(
    order, lengths, grad_ref, own_ref, near_ref, far_ref, after_ref, gain_ref, o0, o1, o2, o3,
    query_ref, kv_ref, mixed_ref, lse_ref, w0, w1, w2, w3,
    cross_ref, two_ref, grads_ref, gain_out, dq_ref, dkv_ref, encoded_ref, acc, *, valid,
):
    local = o0.shape[0]
    step = pl.program_id(0)

    @pl.when(step == 0)
    def _():
        place = lax.broadcasted_iota(jnp.int32, own_ref.shape, 0)
        grads = jnp.where(place < lengths[order[0]], grad_ref[0].astype(F32), 0.0)
        normed_grad = own_ref[...].astype(F32) + near_ref[...].astype(F32) + far_ref[...].astype(F32)
        unit, inverse = norm_stats(after_ref[...])
        total = grads + norm_back(unit, inverse, gain_ref[3 : 4], normed_grad)
        cross_ref[...] = total
        low = total.astype(BF16)
        two_ref[...] = low
        for r, weight in enumerate((o0, o1, o2, o3)):
            mixed = dot(low, weight[...], 1, 1).astype(BF16)
            grads_ref[r // 2, :, (r % 2) * local : (r % 2 + 1) * local] = mixed
        gain_out[...] = jnp.sum(normed_grad * unit, axis=0, keepdims=True)

    def store(columns, dq):
        dq_ref[0, :, columns] = dq

    cross_back(query_ref, kv_ref, grads_ref[step], mixed_ref, lse_ref, dkv_ref, local, valid, store)
    encoded_back(dkv_ref, (w0, w1, w2, w3), encoded_ref, acc)


def cross_first_back(order, lengths, out_grad, parts, after, gains_all, packs, packs_out, query, kv, mixed, lse, valid):
    seq, width = after.shape
    frames = kv.shape[0]
    pair = query.shape[2]
    heads = pair // HEAD_DIM
    rows = whole((seq, width))
    head_rows = pl.BlockSpec((1, seq, pair), lambda i, *_: (i, 0, 0))
    both = pl.BlockSpec((frames, 2 * pair), lambda i, *_: (0, i))
    return call(
        functools.partial(cross_first_back_body, valid=valid),
        (2,),
        [pl.BlockSpec((1, seq, width), lambda i, order, lengths: (order[0], 0, 0)), rows, rows, rows, rows]
        + [whole(gains_all.shape)]
        + pack_specs(packs_out, pair // 2, 0)
        + [head_rows, both, head_rows, pl.BlockSpec((1, heads, seq), lambda i, *_: (i, 0, 0))]
        + pack_specs(packs, pair, 0),
        [
            rows,
            rows,
            whole((2, seq, pair)),
            whole((1, width)),
            head_rows,
            pl.BlockSpec((2 * pair, frames), lambda i, *_: (i, 0)),
            whole((frames, width)),
        ],
        [
            shape((seq, width), F32),
            shape((seq, width)),
            shape((2, seq, pair)),
            shape((1, width), F32),
            shape((2, seq, pair), F32),
            shape((2 * width, frames)),
            shape((frames, width)),
        ],
        "cross_first_back",
        cost(4 * frames * width * width + 120 * seq * frames * pair, 20 * frames * width, 2 * heads * seq * frames),
        prefetch=2,
        scratch=[pltpu.VMEM((frames, width), F32)],
    )(order, lengths, out_grad, *parts, after, gains_all, *packs_out, query, kv, mixed, lse, *packs)


def cross_second_back_body(
    query_ref, kv_ref, grads_ref, mixed_ref, lse_ref, dq_in, w0, w1, w2, w3,
    p0, p1, p2, p3, after_ref, gain_ref, cross_ref,
    dq_ref, dkv_ref, encoded_ref, self_ref, one_ref, h0, h1, h2, h3, gain_out, acc, *, valid,
):
    local = h0.shape[1]
    step = pl.program_id(0)

    def store(columns, dq):
        dq_ref[step, :, columns] = ((dq + dq_in[0, :, columns]) * INV_ROOT).astype(BF16)

    cross_back(query_ref, kv_ref, grads_ref[0], mixed_ref, lse_ref, dkv_ref, local, valid, store)
    encoded_back(dkv_ref, (w0, w1, w2, w3), encoded_ref, acc)

    @pl.when(step == 1)
    def _():
        packs = (p0, p1, p2, p3)
        normed_grad = 0.0
        for r, pack in enumerate(packs):
            normed_grad = normed_grad + dot(dq_ref[r // 2, :, (r % 2) * local : (r % 2 + 1) * local], pack[local:])
        unit, inverse = norm_stats(after_ref[...])
        total = cross_ref[...] + norm_back(unit, inverse, gain_ref[2 : 3], normed_grad)
        self_ref[...] = total
        low = total.astype(BF16)
        one_ref[...] = low
        for out, pack in zip((h0, h1, h2, h3), packs):
            out[...] = dot(low, pack[:local], 1, 1).astype(BF16)
        gain_out[...] = jnp.sum(normed_grad * unit, axis=0, keepdims=True)


def cross_second_back(query, kv, grads, mixed, lse, dq, packs_two, packs_one, after, gains_all, cross, valid):
    seq, width = after.shape
    frames = kv.shape[0]
    pair = query.shape[2]
    local = pair // 2
    heads = pair // HEAD_DIM
    rows = whole((seq, width))
    head_rows = pl.BlockSpec((1, seq, pair), lambda i: (i, 0, 0))
    both = pl.BlockSpec((frames, 2 * pair), lambda i: (0, i))
    return call(
        functools.partial(cross_second_back_body, valid=valid),
        (2,),
        [head_rows, both, head_rows, head_rows, pl.BlockSpec((1, heads, seq), lambda i: (i, 0, 0))]
        + [head_rows]
        + pack_specs(packs_two, pair, 0)
        + pack_specs(packs_one, pair, 0)
        + [rows, whole(gains_all.shape), rows],
        [whole((2, seq, pair)), pl.BlockSpec((2 * pair, frames), lambda i: (i, 0)), whole((frames, width)), rows, rows]
        + [whole((seq, local))] * 4
        + [whole((1, width))],
        [
            shape((2, seq, pair)),
            shape((2 * width, frames)),
            shape((frames, width)),
            shape((seq, width), F32),
            shape((seq, width)),
        ]
        + [shape((seq, local))] * 4
        + [shape((1, width), F32)],
        "cross_second_back",
        cost(4 * frames * width * width + 120 * seq * frames * pair, 20 * frames * width, 2 * heads * seq * frames),
        scratch=[pltpu.VMEM((frames, width), F32)],
    )(query, kv, grads, mixed, lse, dq, *packs_two, *packs_one, after, gains_all, cross)


def add_gain(gain_out, term):
    @pl.when(pl.program_id(0) == 0)
    def _():
        gain_out[...] = jnp.zeros_like(gain_out)

    gain_out[...] += term

def to_tokens_grad_body(order, token_ref, own_ref, near_ref, far_ref, self_ref, gain_ref, out_ref, gain_out):
    normed_grad = own_ref[...].astype(F32) + near_ref[...].astype(F32) + far_ref[...].astype(F32)
    unit, inverse = norm_stats(token_ref[0].astype(F32))
    out_ref[...] = (self_ref[...] + norm_back(unit, inverse, gain_ref[1 : 2], normed_grad)).astype(BF16)
    add_gain(gain_out, jnp.sum(normed_grad * unit, axis=0, keepdims=True))


def to_tokens_grad(order, tokens, own, near, far, grad_self, gains_all, scale):
    _, seq, width = tokens.shape
    tile = seq // 2
    rows = pl.BlockSpec((tile, width), lambda i, *_: (i, 0))
    return call(
        to_tokens_grad_body,
        (2,),
        [pl.BlockSpec((1, tile, width), lambda i, order: (order[0], i, 0)), rows, rows, rows, rows, whole(gains_all.shape)],
        [rows, whole((1, width))],
        [shape((seq, width)), shape((1, width), F32)],
        "norm_one_back",
        cost(0, seq * width * 14, scale=scale),
        prefetch=1,
    )(order, tokens, own, near, far, grad_self, gains_all)


def split_store(total, mine, keep_ref, give_ref, scratch, lead=()):
    scratch[...] = total
    parts, depth = keep_ref.shape[-3], keep_ref.shape[-2]
    for j in range(parts):
        at = pl.multiple_of((2 * j + mine) * depth, 8)
        keep_ref[lead + (j,)] = scratch[pl.ds(at, depth), :].astype(BF16)
        at = pl.multiple_of((2 * j + 1 - mine) * depth, 8)
        give_ref[lead + (j,)] = scratch[pl.ds(at, depth), :].astype(BF16)


def feed_weights_body(bits, *refs):
    rows, pres, lives, hiddens = refs[:4], refs[4:7], refs[7:10], refs[10:13]
    keep_ref, give_ref, scratch = refs[13:]
    three = lambda items: (items[0][0], items[0][1], items[1][0], items[2][0])
    total = 0.0
    for left, right in zip(rows, three(pres)):
        total = total + dot(left[...], right, 0, 0)
    split_store(total, bits[0], keep_ref, give_ref, scratch, (0,))
    total = 0.0
    for left, right in zip(three(lives), three(hiddens)):
        total = total + dot(left, right, 0, 0)
    split_store(total, bits[0], keep_ref, give_ref, scratch, (1,))


def feed_weights(bits, rows, pres, lives, hiddens, wide):
    seq, width = rows[0].shape
    units = pres[0].shape[2]
    tile = width // 2
    depth = width // wide
    column = lambda count: pl.BlockSpec((count, seq, tile), lambda i, *_: (0, 0, i))
    full = lambda count: whole((count, seq, units))
    out = pl.BlockSpec((2, wide // 4, depth, units), lambda i, *_: (0, i, 0, 0))
    return call(
        feed_weights_body,
        (2,),
        [pl.BlockSpec((seq, tile), lambda i, *_: (0, i))] * 4
        + [full(2), full(1), full(1), column(2), column(1), column(1), full(2), full(1), full(1)],
        [out, out],
        [shape((2, wide // 2, depth, units))] * 2,
        "feed_weight_grads",
        cost(16 * seq * width * units, 24 * seq * width),
        prefetch=1,
        scratch=[pltpu.VMEM((tile, units), F32)],
    )(bits, *rows, *pres, *lives, *hiddens)


def head_weights_body(enc0, enc1, dkv0, dkv1, two, grad_two, dq_ref, cross_mixed, keep_ref, give_ref):
    local = dq_ref.shape[2] // 2
    for r, out in enumerate((keep_ref, give_ref)):
        columns = slice(r * local, (r + 1) * local)
        pair = slice(2 * r * local, 2 * (r + 1) * local)
        kv = dot(dkv0[pair, :], enc0[...]) + dot(dkv1[pair, :], enc1[...])
        out[0, :, : 2 * local] = kv.T.astype(BF16)
        query = dot(two[...], dq_ref[0, :, columns], 0, 0)
        cross = dot(grad_two[...], cross_mixed[0, :, columns], 0, 0)
        out[0, :, 2 * local :] = jnp.concatenate((query, cross), axis=1).astype(BF16)


def head_weights(encs, dkvs, normed_two, dq, grad_two, cross_mixed, scale):
    seq, width = normed_two.shape
    heads = pl.BlockSpec((1, seq, width // 2), lambda i: (i, 0, 0))
    out = pl.BlockSpec((1, width, width), lambda i: (i, 0, 0))
    frames = encs[0].shape[0] + encs[1].shape[0]
    return call(
        head_weights_body,
        (2,),
        [whole(item.shape) for item in encs]
        + [pl.BlockSpec((width, item.shape[1]), lambda i: (i, 0)) for item in dkvs]
        + [whole((seq, width))] * 2
        + [heads] * 2,
        [out, out],
        [shape((2, width, width))] * 2,
        "head_weight_grads",
        cost(4 * frames * width * width + 4 * seq * width * width, 6 * frames * width, scale=scale),
    )(*encs, *dkvs, normed_two, grad_two, dq, cross_mixed)


def out_weights_body(one, m0, m1, m2, m3, keep_ref, give_ref):
    for r, mixed in enumerate((m0, m1, m2, m3)):
        (keep_ref, give_ref)[r % 2][r // 2] = dot(mixed[...], one[...], 0, 0).astype(BF16)


def out_weights(grad_one, mixes, scale):
    seq, width = grad_one.shape
    local = mixes[0].shape[1]
    return call(
        out_weights_body,
        (1,),
        [whole(item.shape) for item in (grad_one, *mixes)],
        [whole((2, local, width))] * 2,
        [shape((2, local, width))] * 2,
        "out_weight_grads",
        cost(2 * seq * width * width, 8 * seq * width, scale=scale),
    )(grad_one, *mixes)


def self_weights_body(bits, near, far, dq_near, dkv_near, dq_far, dkv_far, own, core, other, keep_ref, give_ref, scratch):
    local = dq_near.shape[2]
    totals = [0.0, 0.0, 0.0]
    for rows, dq, dkv in ((near, dq_near, dkv_near), (far, dq_far, dkv_far)):
        for c in range(2):
            totals[0] = totals[0] + dot(rows[c], dq[c], 0, 0)
            totals[1] = totals[1] + dot(rows[c], dkv[c, :local, :], 0, 1)
            totals[2] = totals[2] + dot(rows[c], dkv[c, local:, :], 0, 1)
    totals.append((own[0].astype(F32) + core[0].astype(F32) + other[...].astype(F32)).T)
    split_store(jnp.concatenate(totals, axis=1), bits[0], keep_ref, give_ref, scratch)


def self_weights(bits, near, far, dq_near, dkv_near, dq_far, dkv_far, own, core, other, wide, scale):
    _, seq, width = near.shape
    local = dq_near.shape[2]
    tile = width // 2
    depth = width // wide
    rows = pl.BlockSpec((2, seq, tile), lambda i, *_: (0, 0, i))
    turned = pl.BlockSpec((1, local, tile), lambda i, *_: (0, 0, i))
    out = pl.BlockSpec((wide // 4, depth, 4 * local), lambda i, *_: (i, 0, 0))
    return call(
        self_weights_body,
        (2,),
        [rows, rows] + [whole(item.shape) for item in (dq_near, dkv_near, dq_far, dkv_far)] + [turned, turned]
        + [pl.BlockSpec((local, tile), lambda i, *_: (0, i))],
        [out, out],
        [shape((wide // 2, depth, 4 * local))] * 2,
        "self_weight_grads",
        cost(24 * seq * width * local, 16 * seq * width, scale=scale),
        prefetch=1,
        scratch=[pltpu.VMEM((tile, 4 * local), F32)],
    )(bits, near, far, dq_near, dkv_near, dq_far, dkv_far, own, core, other)


def add_low(keep, got):
    return (keep.astype(F32) + got.astype(F32)).astype(BF16)


def merge_body(bits, *refs, which, joined):
    ins, outs = refs[: 2 * len(which)], refs[2 * len(which) :]
    at = 0
    for i, bit in enumerate(which):
        keep_in, got_in = ins[2 * i], ins[2 * i + 1]
        mine = bits[bit]
        keep_out, give_out = outs if joined else outs[2 * i : 2 * i + 2]
        groups = slice(at, at + keep_in.shape[0])
        at += keep_in.shape[0] if joined else 0
        keep_out[groups, 0] = add_low(keep_in[:, mine], got_in[:, mine])
        give_out[groups, 0] = add_low(keep_in[:, 1 - mine], got_in[:, 1 - mine])


def merge(bits, which, *pairs, scale=None, joined=False):
    rows, columns = pairs[0][0].shape[2:]
    tile = rows // 2 if rows % 32 == 0 else rows
    both = [
        pl.BlockSpec((item.shape[0], 2, tile, columns), lambda i, *_: (0, 0, i, 0)) for pair in pairs for item in pair
    ]
    groups = [keep.shape[0] for keep, _ in pairs]
    total = sum(groups)
    groups = [total] if joined else groups
    return call(
        functools.partial(merge_body, which=which, joined=joined),
        (rows // tile,),
        both,
        [pl.BlockSpec((count, 1, tile, columns), lambda i, *_: (0, 0, i, 0)) for count in groups for _ in range(2)],
        [shape((count, 1, rows, columns)) for count in groups for _ in range(2)],
        "merge",
        cost(0, 12 * total * rows * columns, scale=scale),
        prefetch=1,
    )(bits, *[item for pair in pairs for item in pair])


def merge_heads_body(bits, keep_in, got_in, keep_a, give_a, keep_b, give_b):
    low, high = bits[0], bits[1]
    for j in range(keep_a.shape[0]):
        keep_a[j] = add_low(keep_in[0, 2 * j + low], got_in[0, 2 * j + low])
        give_a[j] = add_low(keep_in[0, 2 * j + 1 - low], got_in[0, 2 * j + 1 - low])
        at = 4 * (j // 2) + j % 2
        keep_b[j] = add_low(keep_in[1, at + 2 * high], got_in[1, at + 2 * high])
        give_b[j] = add_low(keep_in[1, at + 2 * (1 - high)], got_in[1, at + 2 * (1 - high)])


def merge_heads(bits, keep, got):
    _, parts, rows, columns = keep.shape
    tile = rows // 2 if rows % 32 == 0 else rows
    both = pl.BlockSpec((2, parts, tile, columns), lambda i, *_: (0, 0, i, 0))
    out = pl.BlockSpec((parts // 2, tile, columns), lambda i, *_: (0, i, 0))
    return call(
        merge_heads_body,
        (rows // tile,),
        [both, both],
        [out] * 4,
        [shape((parts // 2, rows, columns))] * 4,
        "merge_heads",
        cost(0, 12 * parts * rows * columns, scale=SHORT),
        prefetch=1,
    )(bits, keep, got)


def scatter_wide(bits, then, keep, give, which, got):
    dims = keep.shape[-2:]
    parts = lax.axis_size("wide") >> which
    lead = keep.size // (parts * dims[0] * dims[1])
    while parts > 1:
        parts //= 2
        view = (lead * parts, 2) + dims
        keep, give = merge(then(bits), (which,), (keep.reshape(view), got.reshape(view)), scale=SHORT)
        then.last = keep
        which += 1
        got = swap(give, "wide", 1 << (which - 1))
    return keep.reshape((lead,) + dims), got.reshape((lead,) + dims)


def finish_self_body(keep_ref, got_ref, give_ref, heads_ref, qkv_ref, out_ref):
    local = out_ref.shape[0]
    heads_ref[...] = keep_ref[0].astype(F32) + got_ref[0].astype(F32)
    give_ref[...] = (keep_ref[1].astype(F32) + got_ref[1].astype(F32)).astype(BF16)
    own = keep_ref[2].astype(F32) + got_ref[2].astype(F32)
    for i in range(3):
        qkv_ref[i] = own[:, i * local : (i + 1) * local]
    out_ref[...] = own[:, 3 * local :].T


def finish_self(keep, got):
    _, depth, width = keep.shape
    local = width // 4
    dims = [(depth, width), (depth, width), (3, depth, local), (local, depth)]
    return call(
        finish_self_body,
        (1,),
        [whole(keep.shape)] * 2,
        [whole(item) for item in dims],
        [shape(dims[0])] + [shape(item, F32) for item in dims[1:]],
        "finish_self",
        cost(0, 12 * keep.size, scale=SHORT),
    )(keep, got)


def finish_heads_body(own_ref, other_ref, kv_ref, query_ref, out_ref):
    local = out_ref.shape[0]
    total = own_ref[...] + other_ref[...].astype(F32)
    for i in range(2):
        kv_ref[i] = total[:, i * local : (i + 1) * local]
    query_ref[...] = total[:, 2 * local : 3 * local]
    out_ref[...] = total[:, 3 * local :].T


def finish_heads(own, other):
    depth, width = own.shape
    local = width // 4
    dims = [(2, depth, local), (depth, local), (local, depth)]
    return call(
        finish_heads_body,
        (1,),
        [whole(own.shape)] * 2,
        [whole(item) for item in dims],
        [shape(item, F32) for item in dims],
        "finish_heads",
        cost(0, 12 * own.size, scale=SHORT),
    )(own, other)


def place_body(order, a, b, c, d, *refs, start):
    out, held, reads, writes = refs[-4:]
    blocks = (a, b, c, d)
    loads = [pltpu.make_async_copy(item, held.at[r], reads.at[r]) for r, item in enumerate(blocks)]
    for item in loads:
        item.start()
    stores = []
    for r, item in enumerate(loads):
        item.wait()
        if start is None:
            target = out.at[order[r]]
        else:
            target = out.at[:, order[r], pl.ds(start, held.shape[2])]
        stores.append(pltpu.make_async_copy(held.at[r], target, writes.at[r]))
        stores[-1].start()
    for item in stores:
        item.wait()


def place_blocks(order, blocks, dims, start=None, before=None, scale=None):
    anywhere = pl.BlockSpec(memory_space=pl.ANY)
    extra = () if before is None else (before,)
    return pl.pallas_call(
        functools.partial(place_body, start=start),
        grid_spec=pltpu.PrefetchScalarGridSpec(
            num_scalar_prefetch=1,
            grid=(1,),
            in_specs=[anywhere] * (4 + len(extra)),
            out_specs=anywhere,
            scratch_shapes=[
                pltpu.VMEM((4,) + blocks[0].shape, BF16),
                pltpu.SemaphoreType.DMA((4,)),
                pltpu.SemaphoreType.DMA((4,)),
            ],
        ),
        out_shape=shape(dims),
        input_output_aliases={5: 0} if extra else {},
        compiler_params=pltpu.CompilerParams(vmem_limit_bytes=VMEM_LIMIT),
        cost_estimate=cost(0, 16 * blocks[0].size, scale=SHORT if scale is None else scale),
        name="place_blocks",
    )(order, *blocks, *extra)


def on_device(
    tokens, lengths, memory, gains, self_qkv, self_out, cross_q, cross_kv, cross_out, fc_in, fc_out, out_grad
):
    clips, seq, width = tokens.shape
    wide = lax.axis_size("wide")
    narrow = lax.axis_size("narrow")
    me = lax.axis_index("narrow")
    place = lax.axis_index("wide")
    bits = ((place >> jnp.arange(8)) & 1).astype(jnp.int32)
    share = memory.shape[1]
    local = self_qkv.shape[2]
    depth = width // wide
    order = (me ^ jnp.arange(4)).astype(jnp.int32)
    near_order = (me ^ jnp.array([1, 0])).astype(jnp.int32)
    far_order = (me ^ jnp.array([3, 2])).astype(jnp.int32)
    then = Order()

    by_clip = memory.reshape(wide, narrow, share, width)
    first = -(-share // SPLIT) * 16
    sizes = (first, share - first)
    starts = (0, first)
    last = AUDIO - (wide - 1) * share
    valid = [(wide - 1) * size + min(max(last - start, 0), size) for start, size in zip(starts, sizes)]

    def encoder_rows(part, *arrived):
        block = encode(then(order), by_clip, gains, starts[part], sizes[part], LONG if part else None)
        block, *arrived = then.join(block, *arrived)
        block = lax.all_to_all(block, "wide", 0, 0, tiled=True)
        return block.reshape(wide * sizes[part], width), *arrived

    (encoded_first,) = encoder_rows(0)
    self_qkv = self_qkv.transpose(0, 2, 1)
    pack_kv = cross_kv.transpose(0, 2, 1).reshape(2 * local, width)
    packs_one = gather_narrow(jnp.concatenate((self_out, then(cross_q).T)))

    normed_far, qkv_far, mixed_three, mixed_two, lse_far = self_fwd(
        then(far_order), lengths, tokens, gains, self_qkv
    )
    then.last = mixed_two
    mix_two = swap(mixed_two, "narrow", 2)
    crossing = swap(mixed_three, "narrow", 1)
    normed_near, qkv_near, mixed_one, mixed_zero, lse_near = self_fwd(
        then(near_order), lengths, tokens, gains, self_qkv, LONG
    )
    mixed_one, mixed_zero, mix_two, crossing, *packs_one = then.join(
        mixed_one, mixed_zero, mix_two, crossing, *packs_one
    )
    mix_one, mix_three = swap(mixed_one, "narrow", 1), swap(crossing, "narrow", 2)
    packs_one = packs_one + [swap(packs_one[2], "narrow", 1)]
    encoded_second, mix_one, mix_three, *packs_one = encoder_rows(1, mix_one, mix_three, *packs_one)
    encoded = (encoded_first, encoded_second)
    packs_kv = gather_narrow(then(pack_kv))
    mixes = [mixed_zero, mix_one, mix_two, mix_three]
    after_self, normed_two, query = to_query(then(order), tokens, mixes, packs_one, gains)
    query, *packs_kv = then.join(query, *packs_kv)
    packs_kv = packs_kv + [swap(packs_kv[2], "narrow", 1)]
    packs_out = gather_narrow(then(cross_out))
    kv_first, *before = cross_first(then(query), encoded_first, packs_kv, valid[0])
    then.last = kv_first
    packs_out = finish(packs_out, then)
    kv_second, cross_mixed, cross_lse, after_cross, normed_three = cross_second(
        query, encoded_second, packs_kv, packs_out, valid[1], before, after_self, gains
    )
    then.last = normed_three

    rows = gather_narrow(normed_three)
    hidden_a, pre_a, live_a, part_zero, feed_zero, part_one, feed_one = feed_forward(
        order[:2], lengths, rows[:2], out_grad, fc_in, fc_out
    )
    then.last = part_one
    rows = finish(rows, then)
    part_near = swap(part_one, "narrow", 1)
    feed_near = swap(feed_one, "narrow", 1)
    hidden_c, pre_c, live_c, part_three, feed_three = feed_forward(
        order[3:], lengths, rows[3:], out_grad, fc_in, fc_out
    )
    then.last = part_three
    part_cross = swap(part_three, "narrow", 1)
    feed_cross = swap(feed_three, "narrow", 1)
    hidden_b, pre_b, live_b, part_two, feed_two = feed_forward(
        then(order[2:3]), lengths, rows[2:3], out_grad, fc_in, fc_out
    )
    part_far = (part_two.astype(F32) + part_cross.astype(F32)).astype(BF16)
    then.last = part_far
    part_far = swap(part_far, "narrow", 2)
    feed_keep, feed_give = feed_weights(
        then(bits, part_near, feed_near, feed_cross),
        rows, (pre_a, pre_b, pre_c), (live_a, live_b, live_c), (hidden_a, hidden_b, hidden_c), wide,
    )
    then.last = feed_give
    feed_far = (then(feed_two).astype(F32) + feed_cross.astype(F32)).astype(BF16)
    then.last = feed_far
    feed_far = swap(then(feed_far, part_far), "narrow", 2)
    feed_got = swap(feed_give, "wide", 1)

    grad_cross, grad_two, grad_mixed, gain_three, dq, dkv_first, frames_first = cross_first_back(
        then(order), lengths, out_grad, (part_zero, part_near, part_far), after_cross, gains,
        packs_kv, packs_out, query, kv_first, cross_mixed, cross_lse, valid[0],
    )
    then.last = dkv_first

    def frames_sent(block, part):
        block = block.reshape(wide, sizes[part], width)
        return lax.all_to_all(block, "wide", 0, 0, tiled=True)

    frames_first = frames_sent(frames_first, 0)
    block_own = (
        then(after_cross) + (feed_zero.astype(F32) + feed_near.astype(F32) + feed_far.astype(F32))
    ).astype(BF16)
    then.last = block_own
    block_all = gather_narrow(block_own)
    view = (2 * (wide // 4), 2, depth, width)
    feed_keep, feed_give = merge(then(bits), (1,), (feed_keep.reshape(view), feed_got.reshape(view)))
    then.last = feed_keep
    feed_got = swap(feed_give, "wide", 2)
    dq, dkv_second, frames_second, grad_self, grad_one, head0, head1, head2, head3, gain_two = cross_second_back(
        query, kv_second, grad_mixed, cross_mixed, cross_lse, dq, packs_kv, packs_one, after_self,
        then(gains), grad_cross, valid[1],
    )
    then.last = dq
    head1, head2, head3, frames_second, feed_got, *block_all = then.join(
        head1, head2, head3, frames_second, feed_got, *block_all
    )
    feed_view = (2 * (wide // 8), 2, depth, width)
    feed_keep, feed_give = merge(
        then(bits), (2,), (feed_keep.reshape(feed_view), feed_got.reshape(feed_view)), scale=SHORT
    )
    feed_give, head1, head2, head3 = then.join(feed_give, head1, head2, head3)
    feed_got = swap(feed_give, "wide", 4)
    heads_one = swap(head1, "narrow", 1)
    heads_two = swap(head2, "narrow", 2)
    head3 = swap(head3, "narrow", 2)
    block_all = block_all + [swap(block_all[2], "narrow", 1)]
    frames_second = frames_sent(frames_second, 1)

    keep, give = head_weights(
        encoded, (dkv_first, dkv_second), then(normed_two), dq, grad_two, cross_mixed, LONG
    )
    give, keep, heads_one, heads_two, head3, feed_got, *block_all = then.join(
        give, keep, heads_one, heads_two, head3, feed_got, *block_all
    )
    got = swap(give, "narrow", 1)
    heads_three = swap(head3, "narrow", 1)
    back_first, gain_first = memory_back(then(order), by_clip, gains, frames_first, starts[0], SHORT)
    then.last = back_first
    back_first = gather_narrow(back_first)

    *dqkv_near, part_one, part_zero = self_bwd(
        then(near_order), lengths, qkv_near, mixed_one, mixed_zero, lse_near, heads_one, head0, self_qkv, SHORT
    )
    part_one, got, heads_three = then.join(part_one, got, heads_three)
    part_near = swap(part_one, "narrow", 1)
    view = (2, wide, depth, width)
    keep_a, give_a, keep_b, give_b = merge_heads(then(bits), keep.reshape(view), got.reshape(view))
    then.last = give_a
    got_a, got_b = swap(give_a, "wide", 1), swap(give_b, "wide", 2)
    self_keep, self_give = out_weights(then(grad_one), mixes, MID)
    then.last = self_give
    self_got = swap(self_give, "narrow", 1)
    *dqkv_far, part_three, part_two = self_bwd(
        then(far_order), lengths, qkv_far, mixed_three, mixed_two, lse_far, heads_three, heads_two, self_qkv, MID
    )
    part_three, part_two, self_got, frames_second, *back_first = then.join(
        part_three, part_two, self_got, frames_second, *back_first
    )
    part_cross = swap(part_three, "narrow", 1)
    back_first = back_first + [swap(back_first[2], "narrow", 1)]
    self_other = (then(self_keep)[1].astype(F32) + self_got[1].astype(F32)).astype(BF16)
    then.last = self_other
    self_other = swap(self_other, "narrow", 2)
    feed_keep, feed_got = scatter_wide(bits, then, feed_keep, feed_give, 3, feed_got)
    feed_grads = feed_keep.astype(F32) + feed_got.astype(F32)
    back_second, gain_second = memory_back(then(order), by_clip, gains, frames_second, starts[1], LONG)
    back_second, part_two, part_cross, part_near, *back_first = then.join(
        back_second, part_two, part_cross, part_near, *back_first
    )
    part_far = (then(part_two).astype(F32) + part_cross.astype(F32)).astype(BF16)
    then.last = part_far
    part_far = swap(part_far, "narrow", 2)
    self_keep, self_give = self_weights(
        then(bits), normed_near, normed_far, *dqkv_near, *dqkv_far, self_keep, self_got, self_other, wide, LONG
    )
    then.last = self_give
    self_got = swap(self_give, "wide", 1)
    view = (wide // 4, 2, depth, width)
    pair = lambda keep, got: (keep.reshape(view), got.reshape(view))
    keep_a, give_a, keep_b, give_b = merge(then(bits), (1, 0), pair(keep_a, got_a), pair(keep_b, got_b), scale=SHORT)
    then.last = give_a
    got_a, got_b = swap(give_a, "wide", 2), swap(give_b, "wide", 1)
    tokens_own, gain_one = to_tokens_grad(
        then(order), tokens, part_zero, part_near, part_far, grad_self, gains, LONG
    )
    then.last = tokens_own
    tokens_all = gather_narrow(tokens_own)
    gain_terms = jnp.concatenate((gain_first + gain_second, gain_one, gain_two, gain_three))
    gain_other = swap(gain_terms, "wide", 1)
    block_out = place_blocks(then(order), block_all, (clips, seq, width), scale=LONG)
    block_out, self_got, gain_other, gain_terms = then.join(block_out, self_got, gain_other, gain_terms)
    gain_terms = gain_terms + gain_other
    gain_other = swap(gain_terms, "wide", 2)
    self_keep, self_give = merge(then(bits), (1,), pair(self_keep, self_got), scale=SHORT)
    then.last = self_give
    self_got = swap(self_give, "wide", 2)
    view = (wide // 8, 2, depth, width)
    keep, give = merge(
        then(bits), (2, 2, 2), pair(keep_a, got_a), pair(keep_b, got_b), pair(self_keep, self_got), scale=SHORT, joined=True
    )
    give, keep, back_second, gain_other, gain_terms, *tokens_all = then.join(
        give, keep, back_second, gain_other, gain_terms, *tokens_all
    )
    got = swap(give, "wide", 4)
    back_second = gather_narrow(back_second)
    tokens_all = tokens_all + [swap(tokens_all[2], "narrow", 1)]
    gain_terms = gain_terms + gain_other
    gain_other = swap(gain_terms, "wide", 4)
    memory_grad = place_blocks(
        then(order), back_first, (wide, narrow, share, width), starts[0], scale=LONG
    )
    memory_grad, *tokens_all = then.join(memory_grad, *tokens_all)
    tokens_grad = place_blocks(then(order), tokens_all, (clips, seq, width))
    tokens_grad, got, gain_other, gain_terms, *back_second = then.join(
        tokens_grad, got, gain_other, gain_terms, *back_second
    )
    back_second = back_second + [swap(back_second[2], "narrow", 1)]
    gain_terms = gain_terms + gain_other
    bit = 8
    while bit < wide:
        gain_terms = gain_terms + swap(gain_terms, "wide", bit)
        bit *= 2
    gain_terms = lax.dynamic_slice_in_dim(gain_terms, place * depth, depth, 1)
    gain_others = [swap(gain_terms, "narrow", distance) for distance in (1, 2, 3)]
    keep, got = scatter_wide(bits, then, keep, give, 3, got)
    give, head_grads, qkv_grad, self_out_grad = finish_self(keep, then(got))
    then.last = give
    other = swap(give, "narrow", 2)
    memory_grad = place_blocks(
        then(order), back_second, (wide, narrow, share, width), starts[1], memory_grad, scale=LONG
    )
    memory_grad, other, gain_terms, *gain_others = then.join(memory_grad, other, gain_terms, *gain_others)
    gain_terms = gain_terms + gain_others[0] + gain_others[1] + gain_others[2]
    kv_grad, query_grad, cross_out_grad = finish_heads(head_grads, other)
    return (
        block_out,
        tokens_grad,
        memory_grad.reshape(memory.shape),
        gain_terms,
        qkv_grad,
        self_out_grad,
        query_grad,
        kv_grad,
        cross_out_grad,
        feed_grads[0],
        feed_grads[1].T,
    )


def solution(mesh):
    placed = (
        P("wide", None, None),
        P("wide"),
        P(None, "wide", None),
        P(),
        P(None, None, "narrow"),
        P("narrow", None),
        P(None, "narrow"),
        P(None, None, "narrow"),
        P("narrow", None),
        P(None, "narrow"),
        P("narrow", None),
        P("wide", None, None),
    )
    return jax.shard_map(
        on_device,
        mesh=mesh,
        in_specs=placed,
        out_specs=(
            P("wide", None, None),
            P("wide", None, None),
            P(None, "wide", None),
            P(None, "wide"),
            P(None, "wide", "narrow"),
            P("narrow", "wide"),
            P("wide", "narrow"),
            P(None, "wide", "narrow"),
            P("narrow", "wide"),
            P("wide", "narrow"),
            P("narrow", "wide"),
        ),
        check_vma=False,
    )
```
